32 devices in a mesh: gx: 4 (over y, x), gy: 4 (over z), gz: 2 (over core).
Axes of the slice: x: 2, y: 2, z: 4, core: 2. Of those that a mesh axis runs over, the one named last changes fastest.
Arguments:
- solution: float32 [3, 32, 32, 512], P(None, 'gx', 'gy', 'gz'), may hold values from -6 to 6
- residual: float32 [3, 32, 32, 512], P(None, 'gx', 'gy', 'gz'), may hold values from -6 to 6
- prev_direction: float32 [3, 32, 32, 512], P(None, 'gx', 'gy', 'gz'), may hold values from -6 to 6
- prev_image: float32 [3, 32, 32, 512], P(None, 'gx', 'gy', 'gz'), may hold values from -6 to 6
- prev_rz: float32 [], replicated, may hold values from 524288 to 2097152
- density_index: int32 [32, 32, 512], P('gx', 'gy', 'gz'), may hold values from 0 to 15
- stiffness_table: float32 [16], replicated, may hold values from 0.2 to 2
- coarse_inverse: float32 [4, 4, 48, 48], P('gx', 'gy'), may hold values from -0.05 to 5, as said below
Outputs:
- new_solution: float32 [3, 32, 32, 512], P(None, 'gx', 'gy', 'gz')
- new_residual: float32 [3, 32, 32, 512], P(None, 'gx', 'gy', 'gz')
- direction: float32 [3, 32, 32, 512], P(None, 'gx', 'gy', 'gz')
- image: float32 [3, 32, 32, 512], P(None, 'gx', 'gy', 'gz')
The draws below stay inside these ranges and needn't reach their ends.
Inputs may be any that keep to these rules, and one draw needn't show every extreme that they name: `coarse_inverse`: each group's matrix is symmetric positive definite.
All inputs are finite; a program needn't handle non-finite values.
Results may differ from the reference program's by a relative error of at most 0.00016.
Values sent between devices are 32-bit elements; how exact they have to be, the bound alone decides.
No kernel may reach another device: no remote copies, remote signals or barrier semaphores. Data moves between devices by JAX's collectives and lax.ppermute only.
A program may use at most 128 MiB of HBM per device.

```python
import math
import jax
import jax.numpy as jnp
from jax import lax

CX = 8
CY = 8
CZ = 256
LEVELS = 16
SWEEPS = 2
NX = 32
NY = 32
NZ = 512
KC = 48
N_GX = 4
N_GY = 4
N_GZ = 2


def draw_coarse_inverse(key, part):
    key_off = jax.random.fold_in(key, 11)
    key_diag = jax.random.fold_in(key, 12)
    spread = 0.5 / KC
    raw = jax.random.uniform(key_off, (N_GX, N_GY, KC, KC), jnp.float32, -0.5 * spread, 0.5 * spread)
    symmetric = raw + jnp.swapaxes(raw, 2, 3)
    identity = jnp.eye(KC, dtype=jnp.float32)
    index = jnp.arange(KC, dtype=jnp.int32)
    group = index // 24
    component = index % 24 // 8
    place_x = (index % 8 // 4).astype(jnp.float32)
    place_y = (index % 4 // 2).astype(jnp.float32)
    place_z = (2 * group + index % 2).astype(jnp.float32)
    delta_x = place_x[:, None] - place_x[None, :]
    delta_y = place_y[:, None] - place_y[None, :]
    delta_z = place_z[:, None] - place_z[None, :]
    distance = jnp.sqrt(delta_x * delta_x + delta_y * delta_y + delta_z * delta_z)
    coupling = jnp.where(component[:, None] == component[None, :], 1.0, 0.3).astype(jnp.float32)
    kernel = 0.12 * coupling * jnp.exp(-distance / 4.0)
    diag_values = jax.random.uniform(key_diag, (N_GX, N_GY, KC), jnp.float32, 1.0, 2.0)
    matrix = symmetric * (1.0 - identity) + diag_values[:, :, :, None] * identity + kernel[None, None, :, :]
    return matrix


def plant(drawn, rng, least, top_value):
    longest = drawn.shape.index(max(drawn.shape))
    spots = []
    for shift in (0, 1):
        where = [jax.random.randint(jax.random.fold_in(rng, axis), (), 0, length) for axis, length in enumerate(drawn.shape)]
        where[longest] = (where[longest] + shift) % drawn.shape[longest]
        spots.append(tuple(where))
    return drawn.at[spots[0]].set(least).at[spots[1]].set(top_value)


def level_of(key, dims, pieces, least, largest):
    factor_of, own = 1.0, jax.random.fold_in(key, 6)
    for position, blocks in pieces:
        steps = jnp.exp(jax.random.uniform(jax.random.fold_in(own, position), (blocks,), jnp.float32, least / len(pieces), largest / len(pieces)))
        factor_of = factor_of * jnp.repeat(steps, dims[position] // blocks).reshape([-1 if axis == position else 1 for axis in range(len(dims))])
    return factor_of


def bell_draw(own_key, shape, deviation, bound, pieces=(), kind=jnp.bfloat16):
    factor_of = level_of(own_key, shape, pieces, -0.22, 0.18) if pieces else 1.0
    entries = jax.random.normal(own_key, shape, jnp.float32) * deviation * factor_of
    return jnp.minimum(jnp.maximum(entries, -bound), bound).astype(kind)


def setup_inputs(seed: int = 0) -> dict:
    key_list = jax.random.split(jax.random.key(seed), 9)
    solution = bell_draw(key_list[0], (3, NX, NY, NZ), 1.0, 6.0, ((1, 4), (2, 4), (3, 2)), jnp.float32)
    residual = bell_draw(key_list[1], (3, NX, NY, NZ), 1.0, 6.0, ((1, 4), (2, 4), (3, 2)), jnp.float32)
    prev_direction = bell_draw(key_list[2], (3, NX, NY, NZ), 1.0, 6.0, ((1, 4), (2, 4), (3, 2)), jnp.float32)
    prev_image = bell_draw(key_list[3], (3, NX, NY, NZ), 1.0, 6.0, ((1, 4), (2, 4), (3, 2)), jnp.float32)
    prev_rz = jnp.clip(jnp.exp(jax.random.uniform(key_list[4], (), jnp.float32, math.log(524288.0), math.log(2097152))), 524288.0, 2097152)
    density_index = plant(jax.random.randint(key_list[5], (NX, NY, NZ), 0, LEVELS), jax.random.fold_in(key_list[5], 1), 0, LEVELS - 1).astype(jnp.int32)
    stiffness_table = jnp.clip(jnp.exp(jax.random.uniform(key_list[6], (LEVELS,), jnp.float32, math.log(0.2), math.log(2.0))), 0.2, 2.0)
    coarse_inverse = draw_coarse_inverse(jax.random.fold_in(key_list[8], 71), 0)
    return dict(solution=solution, residual=residual, prev_direction=prev_direction, prev_image=prev_image, prev_rz=prev_rz, density_index=density_index, stiffness_table=stiffness_table, coarse_inverse=coarse_inverse)


COUPLING = ((1.0, 0.3, 0.3), (0.3, 1.0, 0.3), (0.3, 0.3, 1.0))
DAMPING = 0.6
MASS_SHIFT = 0.1
WEIGHT_BY_KIND = (0.0, 0.1, 0.05, 0.025)

def neighbour_list():
    listing = []
    for step_x in (-1, 0, 1):
        for step_y in (-1, 0, 1):
            for step_z in (-1, 0, 1):
                kind = abs(step_x) + abs(step_y) + abs(step_z)
                if kind > 0:
                    listing.append((step_x, step_y, step_z, 0.5 * WEIGHT_BY_KIND[kind]))
    return listing

def stencil(padded, coeff):
    size_x = padded.shape[1] - 2
    size_y = padded.shape[2] - 2
    size_z = padded.shape[3] - 2
    centre = padded[:, 1:-1, 1:-1, 1:-1]
    coeff_centre = coeff[1:-1, 1:-1, 1:-1]
    total = MASS_SHIFT * coeff_centre * centre
    for step_x, step_y, step_z, weight in neighbour_list():
        other = padded[:, 1 + step_x:1 + step_x + size_x, 1 + step_y:1 + step_y + size_y, 1 + step_z:1 + step_z + size_z]
        other_coeff = coeff[1 + step_x:1 + step_x + size_x, 1 + step_y:1 + step_y + size_y, 1 + step_z:1 + step_z + size_z]
        total = total + weight * (coeff_centre + other_coeff) * (centre - other)
    return jnp.stack([COUPLING[line][0] * total[0] + COUPLING[line][1] * total[1] + COUPLING[line][2] * total[2] for line in range(3)])

def diagonal_of(coeff):
    size_x = coeff.shape[0] - 2
    size_y = coeff.shape[1] - 2
    size_z = coeff.shape[2] - 2
    coeff_centre = coeff[1:-1, 1:-1, 1:-1]
    total = MASS_SHIFT * coeff_centre
    for step_x, step_y, step_z, weight in neighbour_list():
        other_coeff = coeff[1 + step_x:1 + step_x + size_x, 1 + step_y:1 + step_y + size_y, 1 + step_z:1 + step_z + size_z]
        total = total + weight * (coeff_centre + other_coeff)
    return total

def pad_field(field):
    return jnp.pad(field, ((0, 0), (1, 1), (1, 1), (1, 1)))

def boxed_sum(field, box_x, box_y, box_z):
    shaped = field.reshape(3, field.shape[1] // box_x, box_x, field.shape[2] // box_y, box_y, field.shape[3] // box_z, box_z)
    return lax.optimization_barrier(jnp.sum(shaped, axis=(2, 4, 6)))

def coarsen_cells(cells):
    shaped = cells.reshape(cells.shape[0] // 2, 2, cells.shape[1] // 2, 2, cells.shape[2] // 2, 2)
    return lax.optimization_barrier(jnp.sum(shaped, axis=(1, 3, 5))) * 0.125

def spread_up(field, box_x, box_y, box_z):
    comps, size_x, size_y, size_z = field.shape
    wide = jnp.broadcast_to(field[:, :, None, :, None, :, None], (comps, size_x, box_x, size_y, box_y, size_z, box_z))
    return wide.reshape(comps, size_x * box_x, size_y * box_y, size_z * box_z)

def reference(solution, residual, prev_direction, prev_image, prev_rz, density_index, stiffness_table, coarse_inverse):
    young = stiffness_table[density_index]
    coeff_fine = jnp.pad(young, 1)
    diag_fine = diagonal_of(coeff_fine)

    def fine_apply(field):
        return stencil(pad_field(field), coeff_fine)
    smooth = DAMPING * residual / diag_fine
    for sweep_index in range(SWEEPS - 1):
        smooth = smooth + DAMPING * (residual - fine_apply(smooth)) / diag_fine
    rest = residual - fine_apply(smooth)
    coarse_rhs = 0.5 * boxed_sum(rest, 2, 2, 2)
    coeff_mid = jnp.pad(coarsen_cells(young), 1)
    diag_mid = diagonal_of(coeff_mid)
    middle = DAMPING * coarse_rhs / diag_mid
    mid_rest = coarse_rhs - stencil(pad_field(middle), coeff_mid)
    box_x = CX // 4
    box_y = CY // 4
    box_z = CZ // 4
    lowest = boxed_sum(mid_rest, box_x, box_y, box_z) * (1.0 / math.sqrt(box_x * box_y * box_z))
    gathered = lowest.reshape(3, N_GX, 2, N_GY, 2, N_GZ, 2).transpose(1, 3, 5, 0, 2, 4, 6).reshape(N_GX, N_GY, KC)
    solved = jnp.einsum('abij,abj->abi', coarse_inverse, gathered, precision=lax.Precision.HIGHEST)
    correction = solved.reshape(N_GX, N_GY, N_GZ, 3, 2, 2, 2).transpose(3, 0, 4, 1, 5, 2, 6).reshape(3, 2 * N_GX, 2 * N_GY, 2 * N_GZ)
    middle = middle + spread_up(correction, box_x, box_y, box_z)
    middle = middle + DAMPING * (coarse_rhs - stencil(pad_field(middle), coeff_mid)) / diag_mid
    smooth = smooth + spread_up(middle, 2, 2, 2)
    for sweep_index in range(SWEEPS):
        smooth = smooth + DAMPING * (residual - fine_apply(smooth)) / diag_fine
    precond = smooth
    inner_rz = jnp.sum(residual * precond)
    beta = inner_rz / prev_rz
    direction = precond + beta * prev_direction
    image = fine_apply(precond) + beta * prev_image
    alpha = inner_rz / jnp.sum(direction * image)
    new_solution = solution + alpha * direction
    new_residual = residual - alpha * image
    return (new_solution, new_residual, direction, image)
```

```python
import functools
import math

import jax
import jax.numpy as jnp
from jax import lax
from jax.experimental import pallas as pl
from jax.experimental.pallas import tpu as pltpu
from jax.sharding import PartitionSpec as P

X, Y, Z = 8, 8, 256
COMPS = 3
RIM = 4
WIDE = 6
ROWS = Y + 2 * RIM
LANES = Z + 128
MID_LANES = Z // 2 + 128
DAMPING = 0.6
ALL = ("gx", "gy", "gz")
F32 = jnp.float32
VMEM = pl.BlockSpec(memory_space=pltpu.VMEM)
SMEM = pl.BlockSpec(memory_space=pltpu.SMEM)


def shape(*dims):
    return jax.ShapeDtypeStruct(dims, F32)


def call(body, outs, scratch=(), n_in=0, smem=(), mib=16, flops=1000000):
    return pl.pallas_call(
        body,
        out_shape=outs,
        in_specs=[SMEM if i in smem else VMEM for i in range(n_in)],
        out_specs=[VMEM] * len(outs),
        scratch_shapes=list(scratch),
        compiler_params=pltpu.CompilerParams(vmem_limit_bytes=mib * 1024 * 1024),
    )


def pairs(count, odd):
    if odd:
        return [(i, (i + 1) % count if i % 2 else (i - 1) % count) for i in range(count)]
    return [(i, i ^ 1) for i in range(count)]


def swap(axis, even_pack, odd_pack):
    count = lax.axis_size(axis)
    got_even = lax.ppermute(even_pack, axis, pairs(count, False))
    if count == 2:
        return [got_even]
    return [got_even, lax.ppermute(odd_pack, axis, pairs(count, True))]


def is_even(axis):
    return lax.rem(lax.axis_index(axis), 2) == 0


def inner(axis):
    index = lax.axis_index(axis)
    return jnp.logical_and(index > 0, index < lax.axis_size(axis) - 1)


def from_sides(got, axis):
    even = is_even(axis)
    if len(got) == 1:

        def lower(key):
            value = got[0][key]
            return jnp.where(even, 0.0, value)

        def upper(key):
            value = got[0][key]
            return jnp.where(even, value, 0.0)

        return lower, upper
    ok = inner(axis)

    def lower(key):
        return jnp.where(even, jnp.where(ok, got[1][key], 0.0), got[0][key])

    def upper(key):
        return jnp.where(even, got[0][key], jnp.where(ok, got[1][key], 0.0))

    return lower, upper


def tri_yz(a):
    rows, lanes = a.shape
    a = a + pltpu.roll(a, 1, 0)
    a = a + pltpu.roll(a, rows - 1, 0)
    a = a + pltpu.roll(a, 1, 1)
    return a + pltpu.roll(a, lanes - 1, 1)


def tri_x(before, centre, after):
    return before + after + (centre + centre)


def coupled(parts):
    total = 0.3 * (parts[0] + parts[1] + parts[2])
    return [0.7 * part + total for part in parts]


def row_of(shape):
    return lax.broadcasted_iota(jnp.int32, shape, 0)


def lane_of(shape):
    return lax.broadcasted_iota(jnp.int32, shape, 1)


def up(a, shift):
    shift %= a.shape[0]
    return pltpu.roll(a, shift, 0) if shift else a


def pool_matrix(value):
    lane = row_of((LANES, MID_LANES))
    mid = jnp.where(lane < Z + 64, lane // 2, lane // 2 + 64)
    return jnp.where(mid == lane_of((LANES, MID_LANES)), value, 0.0).astype(F32)


def spread_matrix():
    lane = lane_of((MID_LANES, LANES))
    mid = jnp.where(lane < Z + 64, lane // 2, lane // 2 + 64)
    return jnp.where(mid == row_of((MID_LANES, LANES)), 1.0, 0.0).astype(F32)


def put_tiles(ref, at, value):
    for k in range(ref.shape[0]):
        ref[k, at : at + value.shape[0]] = value[:, 128 * k : 128 * k + 128]


def every_other(ref, at, size):
    return jnp.concatenate(
        [ref[k, pl.ds(at, size, stride=2)] for k in range(ref.shape[0])], axis=1
    )


def exact_dot(a, b):
    return jnp.dot(a, b, precision=lax.Precision.HIGHEST, preferred_element_type=F32)


X_PACK = COMPS * RIM + WIDE
R_TILES = COMPS * X
E_PLANES = X + 2 * WIDE
E4_TILES = E_PLANES // 2
E2_TILES = E_PLANES // 4
Y_PACK = R_TILES + E4_TILES + E2_TILES
Z_PACK = COMPS * (X + 2 * RIM) * ROWS + E_PLANES * 24
R_SLAB = COMPS * (X + 2 * RIM) * ROWS


def pack_x_body(table, index, res, young, pack_even, pack_odd):
    levels = index[...]
    value = jnp.zeros(levels.shape, F32)
    for level in range(table.shape[0]):
        value = jnp.where(levels == level, table[level], value)
    young[...] = value
    even = is_even("gx")
    high_first = jnp.where(even, 1, 0)
    for pack, high in ((pack_even, high_first), (pack_odd, 1 - high_first)):
        for c in range(COMPS):
            pack[c * RIM : (c + 1) * RIM] = res[c, pl.ds(high * (X - RIM), RIM)]
        pack[COMPS * RIM :] = young[pl.ds(high * (X - WIDE), WIDE)]


def x_planes(res, young, got_x, lanes=slice(None)):
    lower, upper = from_sides(got_x, "gx")
    whole = slice(None)

    def res_plane(c, i):
        if i < RIM:
            return lower((c * RIM + i, whole, lanes))
        if i < RIM + X:
            return res[c, i - RIM, :, lanes]
        return upper((c * RIM + i - RIM - X, whole, lanes))

    def young_plane(i):
        if i < WIDE:
            return lower((COMPS * RIM + i, whole, lanes))
        if i < WIDE + X:
            return young[i - WIDE, :, lanes]
        return upper((COMPS * RIM + i - WIDE - X, whole, lanes))

    return res_plane, young_plane


def pack_y_body(res, young, got_a, got_b, pack_even, pack_odd):
    res_plane, young_plane = x_planes(res, young, (got_a, got_b))
    row = row_of((Y, Z))
    even = is_even("gy")

    def put(tile, low, high):
        pack_even[tile] = jnp.where(even, high, low)
        pack_odd[tile] = jnp.where(even, low, high)

    def halves(tile, a, b):
        put(
            tile,
            jnp.where(row < 4, a, up(b, 4)),
            jnp.where(row < 4, up(a, 4), b),
        )

    for c in range(COMPS):
        for i in range(X):
            halves(c * X + i, res_plane(c, i), res_plane(c, i + X))
    planes = [young_plane(i) for i in range(E_PLANES)]
    for i in range(E4_TILES):
        halves(R_TILES + i, planes[i], planes[i + E4_TILES])
    for j in range(E2_TILES):
        low = high = None
        for k in range(4):
            plane = planes[4 * j + k]
            a, b = up(plane, 2 * k - 4), up(plane, 2 * k - 2)
            low = a if k == 0 else jnp.where(row < 2 * k, low, a)
            high = b if k == 0 else jnp.where(row < 2 * k, high, b)
        put(R_TILES + E4_TILES + j, low, high)


def xy_planes(res, young, got_x, got_y, lanes, width):
    res_plane, young_plane = x_planes(res, young, got_x, lanes)
    lower, upper = from_sides(got_y, "gy")
    row = row_of((Y, width))
    whole = slice(None)

    def res_tiles(c, i):
        own = up(res_plane(c, i), 4)
        key = (c * X + i % X, whole, lanes)
        low, high = lower(key), upper(key)
        if i < X:
            high = up(high, 4)
        else:
            low = up(low, 4)
        return [jnp.where(row < 4, low, own), jnp.where(row < 4, own, high)]

    def young_tiles(i):
        four = (R_TILES + i % E4_TILES, whole, lanes)
        two = (R_TILES + E4_TILES + i // 4, whole, lanes)
        k = i % 4
        low4, high4 = lower(four), upper(four)
        if i < E4_TILES:
            low4 = up(low4, 4)
        else:
            high4 = up(high4, 4)
        low2, high2 = up(lower(two), 2 - 2 * k), up(upper(two), 4 - 2 * k)
        low = jnp.where(row < 4, jnp.where(row < 2, 0.0, low2), low4)
        high = jnp.where(row < 4, high4, jnp.where(row < 6, high2, 0.0))
        return [low, young_plane(i), high]

    return res_tiles, young_tiles


def pack_z_body(res, young, xa, xb, ya, yb, *packs):
    high_first = jnp.where(is_even("gz"), 1, 0)
    for pack, high in zip(packs, (high_first, 1 - high_first)):
        lanes = pl.ds(pl.multiple_of(high * (Z - 128), 128), 128)
        res_tiles, young_tiles = xy_planes(res, young, (xa, xb), (ya, yb), lanes, 128)
        at = 0
        for c in range(COMPS):
            for i in range(X + 2 * RIM):
                for tile in res_tiles(c, i):
                    pack[at : at + 8] = tile
                    at += 8
        for i in range(E_PLANES):
            for tile in young_tiles(i):
                pack[at : at + 8] = tile
                at += 8


M_PLANES = X // 2 + 4
EM_PLANES = X // 2 + 6
LOW_TILE = COMPS * (X // 2)
MZ_PACK = (LOW_TILE + 1) * 8


def fine_apply(s, es, c1, e, i):
    parts = []
    for c in range(COMPS):
        tv = tri_yz(tri_x(s[c, i - 1], s[c, i], s[c, i + 1]))
        te = tri_yz(tri_x(es[c, i - 1], es[c, i], es[c, i + 1]))
        parts.append(c1[i] * s[c, i] - (e[i] * tv + te))
    return coupled(parts)


def smooth_body(n_z, *refs):
    res, young, xa, xb, ya, yb = refs[:6]
    got_z = refs[6 : 6 + n_z]
    r, s1, e, c1, w, em, c1m, wm, pack = refs[6 + n_z : 15 + n_z]
    wide, s0, es0, es1, rest, pooled, wide_x, wide_p = refs[15 + n_z :]
    lane = lane_of((8, 128))

    res_tiles, young_tiles = xy_planes(res, young, (xa, xb), (ya, yb), slice(None), Z)
    left, right = from_sides(got_z, "gz")

    def side(at):
        key = (slice(at, at + 8), slice(None))
        return jnp.where(lane < 64, right(key), left(key))

    at = 0
    for c in range(COMPS):
        for i in range(X + 2 * RIM):
            for t, tile in enumerate(res_tiles(c, i)):
                r[c, i, 8 * t : 8 * t + 8, :Z] = tile
                r[c, i, 8 * t : 8 * t + 8, Z:] = side(at)
                at += 8
    for i in range(E_PLANES):
        for t, tile in enumerate(young_tiles(i)):
            wide[i, 8 * t : 8 * t + 8, :Z] = tile * 0.0125
            wide[i, 8 * t : 8 * t + 8, Z:] = side(at) * 0.0125
            at += 8

    def prepare(i, _):
        total = tri_yz(tri_x(wide[i + 1], wide[i + 2], wide[i + 3]))[4:20]
        centre = wide[i + 2, 4:20]
        e[i] = centre
        c1[i] = 72.0 * centre + total
        inverse = jnp.where(centre > 0.0, DAMPING / (56.0 * centre + total), 0.0)
        w[i] = inverse
        for c in range(COMPS):
            value = inverse * r[c, i]
            s0[c, i] = value
            es0[c, i] = centre * value
        return _

    lax.fori_loop(0, X + 2 * RIM, prepare, 0)

    def sweep(i, _):
        applied = fine_apply(s0, es0, c1, e, i)
        for c in range(COMPS):
            value = s0[c, i] + w[i] * (r[c, i] - applied[c])
            s1[c, i] = value
            es1[c, i] = e[i] * value
        return _

    lax.fori_loop(1, X + 2 * RIM - 1, sweep, 0)

    def residue(m, _):
        first = fine_apply(s1, es1, c1, e, 2 * m + 2)
        second = fine_apply(s1, es1, c1, e, 2 * m + 3)
        for c in range(COMPS):
            total = (r[c, 2 * m + 2] - first[c]) + (r[c, 2 * m + 3] - second[c])
            rest[pl.ds((c * 6 + m) * ROWS, ROWS)] = total
        return _

    lax.fori_loop(0, 6, residue, 0)

    pool = pool_matrix(0.5)
    put_tiles(pooled, 0, exact_dot(rest[...], pool))
    for m in range(EM_PLANES):
        wide_x[24 * m : 24 * m + 24] = wide[2 * m] + wide[2 * m + 1]
    wide_p[...] = jnp.zeros(wide_p.shape, F32)
    put_tiles(wide_p, 0, exact_dot(wide_x[...], pool))
    for m in range(EM_PLANES):
        a = every_other(wide_p, 24 * m, 16) + every_other(wide_p, 24 * m + 1, 16)
        em[m] = jnp.where(row_of(a.shape) < 12, 0.25 * a, 0.0)
    for m in range(M_PLANES):
        total = tri_yz(tri_x(em[m], em[m + 1], em[m + 2]))[2:10]
        centre = em[m + 1, 2:10]
        c1m[m] = 72.0 * centre + total
        wm[m] = jnp.where(centre > 0.0, DAMPING / (56.0 * centre + total), 0.0)

    rhs, mid, e_mid = {}, {}, {}
    for m in range(6):
        centre = em[m + 2, 2:10]
        for c in range(COMPS):
            at = (c * 6 + m) * ROWS
            a = every_other(pooled, at, 8) + every_other(pooled, at + 1, 8)
            rhs[c, m] = a
            mid[c, m] = wm[m + 1] * a
            e_mid[c, m] = centre * mid[c, m]
    rows = []
    kept = {}
    for m in range(1, 5):
        parts = []
        for c in range(COMPS):
            tv = tri_yz(tri_x(mid[c, m - 1], mid[c, m], mid[c, m + 1]))
            te = tri_yz(tri_x(e_mid[c, m - 1], e_mid[c, m], e_mid[c, m + 1]))
            parts.append(c1m[m + 1] * mid[c, m] - (em[m + 2, 2:10] * tv + te))
        applied = coupled(parts)
        for c in range(COMPS):
            left_over = rhs[c, m] - applied[c]
            kept[c, m - 1] = left_over
            value = mid[c, m] + wm[m + 1] * left_over
            tile = c * 4 + m - 1
            pack[8 * tile : 8 * tile + 8] = value[:, :128]
    for c in range(COMPS):
        for b in range(2):
            rows.append(kept[c, 2 * b] + kept[c, 2 * b + 1])
    stacked = jnp.concatenate(rows, axis=0)
    lane_box = row_of((MID_LANES, 128))
    column = lane_of((MID_LANES, 128))
    boxes = jnp.where(
        jnp.logical_and(lane_box < Z // 2, lane_box // 64 == column % 2), 1.0, 0.0
    ).astype(F32)
    sums = exact_dot(stacked, boxes)
    line = row_of((48, 128))
    entry = lane_of((48, 128))
    inside = line % 8
    match = (line // 8) * 2 + (inside - 2) // 2 == entry // 2
    match = jnp.logical_and(match, jnp.logical_and(inside >= 2, inside < 6))
    scale = 1.0 / math.sqrt((X // 4) * (Y // 4) * (Z // 4))
    low = jnp.sum(jnp.where(match, sums, 0.0), axis=0, keepdims=True) * scale
    pack[8 * LOW_TILE :] = jnp.broadcast_to(low, (8, 128))


def coarse_body(n_z, *refs):
    pack = refs[0]
    got_z = refs[1 : 1 + n_z]
    rhs, matrix = refs[1 + n_z : 3 + n_z]
    planes, column, pack_even, pack_odd, scratch = refs[3 + n_z :]
    place = lax.axis_index("gz")
    count = lax.axis_size("gz")
    left, right = from_sides(got_z, "gz")
    lane = lane_of((8, 128))
    for t in range(LOW_TILE):
        key = (slice(8 * t, 8 * t + 8), slice(None))
        planes[t, :, :128] = pack[key]
        planes[t, :, 128:] = jnp.where(lane < 64, right(key), left(key))

    solved = jnp.sum(matrix[...] * rhs[...], axis=1, keepdims=True)
    size = 24
    scratch[...] = jnp.zeros(scratch.shape, F32)
    scratch[size : size + matrix.shape[0]] = jnp.broadcast_to(solved, (matrix.shape[0], 128))
    base = pl.multiple_of(place * size, 8)
    wide = lane_of((16, MID_LANES))
    before, own_a, own_b, after = [
        jnp.concatenate([scratch[pl.ds(base + at, 16, stride=2)]] * 2, axis=1)
        for at in (1, size, size + 1, 2 * size)
    ]
    value = jnp.where(wide < 64, own_a, own_b)
    value = jnp.where(wide < 128, value, jnp.where(wide < 192, after, before))
    value = jnp.where(row_of((16, MID_LANES)) < 12, value, 0.0)
    column[...] = value

    even = is_even("gx")
    row = row_of((8, MID_LANES))
    for c in range(COMPS):
        tiles = [
            jnp.where(row < 4, up(planes[c * 4 + p], -2), up(planes[c * 4 + p + 1], 2))
            for p in (0, 2)
        ]
        pack_even[8 * c : 8 * c + 8] = jnp.where(even, tiles[1], tiles[0])
        pack_odd[8 * c : 8 * c + 8] = jnp.where(even, tiles[0], tiles[1])
    pack_even[24:] = value
    pack_odd[24:] = value


MX_PACK = 24 + 16
MY_PACK = 48 + 40


def mid_y_body(planes, column, got_a, got_b, wide_planes, columns, pack_even, pack_odd):
    lower, upper = from_sides((got_a, got_b), "gx")
    whole = slice(None)
    row = row_of((8, MID_LANES))
    even = is_even("gy")
    for c in range(COMPS):
        key = (slice(8 * c, 8 * c + 8), whole)
        low, high = lower(key), upper(key)
        tiles = [up(low, 2), up(low, -2)]
        tiles += [planes[c * 4 + p] for p in range(4)]
        tiles += [up(high, 2), up(high, -2)]
        for t in range(8):
            wide_planes[c * 8 + t] = tiles[t]
        for h in range(2):
            below = above = None
            for k in range(4):
                tile = tiles[4 * h + k]
                a, b = up(tile, 2 * k - 2), up(tile, 2 * k - 4)
                below = a if k == 0 else jnp.where(row < 2 * k, below, a)
                above = b if k == 0 else jnp.where(row < 2 * k, above, b)
            at = (c * 2 + h) * 8
            pack_even[at : at + 8] = jnp.where(even, above, below)
            pack_odd[at : at + 8] = jnp.where(even, below, above)
    columns[:12] = lower((slice(24, 36), whole))
    columns[12:24] = column[:12]
    columns[24:36] = upper((slice(24, 36), whole))
    columns[36:] = jnp.zeros((4, MID_LANES), F32)
    pack_even[48:] = columns[...]
    pack_odd[48:] = columns[...]


def finish_body(
    wide_planes, columns, got_a, got_b, r, s1, e, c1, w, em, c1m, wm, prev_d, prev_i,
    precond, operated, sums, cor, mid, big, s2, es2, s3, es3, p, ep,
):
    lower, upper = from_sides((got_a, got_b), "gy")
    whole = slice(None)
    row = row_of((8, MID_LANES))
    line = row_of((16, MID_LANES))

    below = lower((slice(48, 88), whole))
    above = upper((slice(48, 88), whole))
    middle = columns[...]
    for c in range(COMPS):
        for b in range(6):
            at = (b // 2) * 12 + c * 4 + (b % 2) * 2
            bands = [source[at + by : at + by + 1] for source in (below, middle, above) for by in range(2)]
            field = jnp.zeros((16, MID_LANES), F32)
            for t, band in enumerate(bands):
                inside = jnp.logical_and(line >= 2 * t, line < 2 * t + 2)
                field = jnp.where(inside, jnp.broadcast_to(band, (16, MID_LANES)), field)
            cor[c, b] = field

    def box(m):
        return (m + 1) // 2

    for m in range(M_PLANES):
        parts = []
        for c in range(COMPS):
            near = [cor[c, box(m + k)] for k in range(3)]
            tv = tri_yz(tri_x(*near))
            te = tri_yz(tri_x(*[em[m + k] * near[k] for k in range(3)]))
            part = em[m + 1] * tv + te
            parts.append(c1m[m] * near[1][2:10] - part[2:10])
        applied = coupled(parts)
        for c in range(COMPS):
            tile = wide_planes[c * 8 + m]
            at = ((c * 2 + m // 4) * 8, (c * 2 + m // 4) * 8 + 8)
            key = (slice(*at), whole)
            k = m % 4
            tile = jnp.where(row < 2, up(lower(key), -2 * k), tile)
            tile = jnp.where(row < 6, tile, up(upper(key), 6 - 2 * k))
            value = tile + cor[c, box(m + 1), 2:10] - wm[m] * applied[c]
            at = (c * 8 + m) * 8
            mid[at : at + 8] = value
    spread = exact_dot(mid[...], spread_matrix())
    for t in range(COMPS * 8):
        piece = spread[8 * t : 8 * t + 8]
        for k in range(LANES // 128):
            tile = piece[:, 128 * k : 128 * k + 128]
            big[k, pl.ds(16 * t, 8, stride=2)] = tile
            big[k, pl.ds(16 * t + 1, 8, stride=2)] = tile

    def add_up(i, _):
        for c in range(COMPS):
            at = pl.multiple_of((c * 8 + i // 2) * 16, 16)
            more = [big[k, pl.ds(at, 16)] for k in range(LANES // 128)]
            value = s1[c, i] + jnp.concatenate(more, axis=1)
            s2[c, i] = value
            es2[c, i] = e[i] * value
        return _

    lax.fori_loop(1, X + 2 * RIM - 1, add_up, 0)

    def sweep(source, e_source, target, e_target):
        def body(i, _):
            applied = fine_apply(source, e_source, c1, e, i)
            for c in range(COMPS):
                value = source[c, i] + w[i] * (r[c, i] - applied[c])
                target[c, i] = value
                e_target[c, i] = e[i] * value
            return _

        return body

    lax.fori_loop(2, X + 2 * RIM - 2, sweep(s2, es2, s3, es3), 0)
    lax.fori_loop(3, X + 2 * RIM - 3, sweep(s3, es3, p, ep), 0)

    def image(i, carry):
        applied = fine_apply(p, ep, c1, e, i)
        x = i - RIM
        rz, pp, mix, old = carry
        for c in range(COMPS):
            own_p = p[c, i, 4:12, :Z]
            own_a = applied[c][4:12, :Z]
            precond[c, x] = own_p
            operated[c, x] = own_a
            d, q = prev_d[c, x], prev_i[c, x]
            rz += r[c, i, 4:12, :Z] * own_p
            pp += own_p * own_a
            mix += own_p * q + d * own_a
            old += d * q
        return rz, pp, mix, old

    zero = jnp.zeros((Y, Z), F32)
    found = lax.fori_loop(RIM, RIM + X, image, (zero, zero, zero, zero))
    lane = lane_of((1, 128))
    total = jnp.zeros((1, 128), F32)
    for k, value in enumerate(found):
        total = jnp.where(lane == k, jnp.sum(value), total)
    sums[...] = jnp.broadcast_to(total, sums.shape)


def last_body(prev_rz, sums, precond, operated, prev_d, prev_i, sol, res, new_s, new_r, new_d, new_i):
    total = jnp.sum(sums[...], axis=0, keepdims=True)
    lane = lane_of((1, 128))

    def entry(k):
        return jnp.sum(jnp.where(lane == k, total, 0.0), axis=1, keepdims=True)

    rz = entry(0)
    beta = rz / prev_rz[0]
    alpha = rz / (entry(1) + beta * (entry(2) + beta * entry(3)))
    beta = jnp.broadcast_to(beta, (Y, Z))
    alpha = jnp.broadcast_to(alpha, (Y, Z))
    for c in range(COMPS):
        for x in range(X):
            d = precond[c, x] + beta * prev_d[c, x]
            q = operated[c, x] + beta * prev_i[c, x]
            new_d[c, x] = d
            new_i[c, x] = q
            new_s[c, x] = sol[c, x] + alpha * d
            new_r[c, x] = res[c, x] - alpha * q


def on_device(
    solution,
    residual,
    prev_direction,
    prev_image,
    prev_rz,
    density_index,
    stiffness_table,
    coarse_inverse,
):
    if residual.shape != (COMPS, X, Y, Z):
        raise ValueError(residual.shape)
    block = shape(COMPS, X, Y, Z)
    n_z = 1 if lax.axis_size("gz") == 2 else 2
    n_all = lax.axis_size(ALL)

    young, px, qx = call(
        pack_x_body,
        [shape(X, Y, Z), shape(X_PACK, Y, Z), shape(X_PACK, Y, Z)],
        n_in=3,
        smem=(0,),
    )(stiffness_table, density_index, residual)
    got_x = swap("gx", px, qx)
    py, qy = call(pack_y_body, [shape(Y_PACK, Y, Z)] * 2, n_in=4)(residual, young, *got_x)
    got_y = swap("gy", py, qy)
    packs = call(pack_z_body, [shape(Z_PACK, 128)] * n_z, n_in=6)(residual, young, *got_x, *got_y)
    got_z = swap("gz", packs[0], packs[-1])

    planes = X + 2 * RIM
    field = (COMPS, planes, ROWS, LANES)
    r, s1, e, c1, w, em, c1m, wm, pack = call(
        functools.partial(smooth_body, n_z),
        [
            shape(*field),
            shape(*field),
            shape(planes, ROWS, LANES),
            shape(planes, ROWS, LANES),
            shape(planes, ROWS, LANES),
            shape(EM_PLANES, 16, MID_LANES),
            shape(M_PLANES, 8, MID_LANES),
            shape(M_PLANES, 8, MID_LANES),
            shape(MZ_PACK, 128),
        ],
        scratch=[
            pltpu.VMEM((E_PLANES, 24, LANES), F32),
            pltpu.VMEM(field, F32),
            pltpu.VMEM(field, F32),
            pltpu.VMEM(field, F32),
            pltpu.VMEM((18 * ROWS, LANES), F32),
            pltpu.VMEM((MID_LANES // 128, 18 * ROWS, 128), F32),
            pltpu.VMEM((24 * EM_PLANES, LANES), F32),
            pltpu.VMEM((MID_LANES // 128, 24 * EM_PLANES + 16, 128), F32),
        ],
        n_in=6 + n_z,
        mib=30,
    )(residual, young, *got_x, *got_y, *got_z)

    got_z = swap("gz", pack, pack)
    low = pack[8 * LOW_TILE, :24]
    if n_z == 1:
        other = got_z[0][8 * LOW_TILE, :24]
        first = lax.axis_index("gz") == 0
        rhs = jnp.where(first, jnp.concatenate([low, other]), jnp.concatenate([other, low]))
    else:
        rhs = lax.all_gather(low, "gz", axis=0, tiled=True)
    size = rhs.shape[0]
    mid_planes, column, px, qx = call(
        functools.partial(coarse_body, n_z),
        [
            shape(LOW_TILE, 8, MID_LANES),
            shape(16, MID_LANES),
            shape(MX_PACK, MID_LANES),
            shape(MX_PACK, MID_LANES),
        ],
        scratch=[pltpu.VMEM((size + 64, 128), F32)],
        n_in=3 + n_z,
    )(pack, *got_z, rhs.reshape(1, size), coarse_inverse.reshape(size, size))
    got_x = swap("gx", px, qx)
    mid_planes, columns, py, qy = call(
        mid_y_body,
        [
            shape(COMPS * 8, 8, MID_LANES),
            shape(40, MID_LANES),
            shape(MY_PACK, MID_LANES),
            shape(MY_PACK, MID_LANES),
        ],
        n_in=4,
    )(mid_planes, column, *got_x)
    got_y = swap("gy", py, qy)
    precond, operated, sums = call(
        finish_body,
        [block, block, shape(n_all, 128)],
        scratch=[
            pltpu.VMEM((COMPS, 6, 16, MID_LANES), F32),
            pltpu.VMEM((COMPS * 64, MID_LANES), F32),
            pltpu.VMEM((LANES // 128, COMPS * 128, 128), F32),
        ]
        + [pltpu.VMEM(field, F32)] * 6,
        n_in=14,
        mib=30,
    )(mid_planes, columns, *got_y, r, s1, e, c1, w, em, c1m, wm, prev_direction, prev_image)
    sums = lax.all_to_all(sums, ALL, 0, 0, tiled=True)
    return tuple(
        call(last_body, [block] * 4, n_in=8, smem=(0,))(
            prev_rz.reshape(1), sums, precond, operated, prev_direction, prev_image, solution, residual
        )
    )


def solution(mesh):
    field = P(None, "gx", "gy", "gz")
    return jax.shard_map(
        on_device,
        mesh=mesh,
        in_specs=(
            field,
            field,
            field,
            field,
            P(),
            P("gx", "gy", "gz"),
            P(),
            P("gx", "gy", None, None),
        ),
        out_specs=(field, field, field, field),
        check_vma=False,
    )
```

```python
import functools
import math

import jax
import jax.numpy as jnp
from jax import lax
from jax.experimental import pallas as pl
from jax.experimental.pallas import tpu as pltpu
from jax.sharding import PartitionSpec as P

X, Y, Z = 8, 8, 256
COMPS = 3
RIM = 4
WIDE = 6
ROWS = Y + 2 * RIM
LANES = Z + 128
MID_LANES = Z // 2 + 128
DAMPING = 0.6
ALL = ("gx", "gy", "gz")
F32 = jnp.float32
VMEM = pl.BlockSpec(memory_space=pltpu.VMEM)
SMEM = pl.BlockSpec(memory_space=pltpu.SMEM)
HBM = pl.BlockSpec(memory_space=pltpu.HBM)


def shape(*dims):
    return jax.ShapeDtypeStruct(dims, F32)


def call(body, outs, scratch=(), n_in=0, smem=(), hbm=(), hbm_out=(), mib=16):
    return pl.pallas_call(
        body,
        out_shape=outs,
        in_specs=[SMEM if i in smem else HBM if i in hbm else VMEM for i in range(n_in)],
        out_specs=[HBM if i in hbm_out else VMEM for i in range(len(outs))],
        scratch_shapes=list(scratch),
        compiler_params=pltpu.CompilerParams(vmem_limit_bytes=mib * 1024 * 1024),
    )


def pairs(count, odd, closed):
    if not odd:
        return [(i, i ^ 1) for i in range(count)]
    made = [(i, (i + 1) % count if i % 2 else (i - 1) % count) for i in range(count)]
    return made if closed else made[1:-1]


def swap(axis, even_pack, odd_pack, closed=True):
    count = lax.axis_size(axis)
    got_even = lax.ppermute(even_pack, axis, pairs(count, False, closed))
    if count == 2:
        return [got_even]
    return [got_even, lax.ppermute(odd_pack, axis, pairs(count, True, closed))]


def is_even(axis):
    return lax.rem(lax.axis_index(axis), 2) == 0


def inner(axis):
    index = lax.axis_index(axis)
    return jnp.logical_and(index > 0, index < lax.axis_size(axis) - 1)


def from_sides(got, axis):
    even = is_even(axis)
    if len(got) == 1:

        def lower(key):
            value = got[0][key]
            return jnp.where(even, 0.0, value)

        def upper(key):
            value = got[0][key]
            return jnp.where(even, value, 0.0)

        return lower, upper
    ok = inner(axis)

    def lower(key):
        return jnp.where(even, jnp.where(ok, got[1][key], 0.0), got[0][key])

    def upper(key):
        return jnp.where(even, got[0][key], jnp.where(ok, got[1][key], 0.0))

    return lower, upper


def tri_y(a):
    a = a + pltpu.roll(a, 1, 0)
    return a + pltpu.roll(a, a.shape[0] - 1, 0)


def tri_yz(a):
    a = tri_y(a)
    a = a + pltpu.roll(a, 1, 1)
    return a + pltpu.roll(a, a.shape[1] - 1, 1)


def tri_x(before, centre, after):
    return before + after + (centre + centre)


def coupled(parts):
    total = 0.3 * (parts[0] + parts[1] + parts[2])
    return [0.7 * part + total for part in parts]


def row_of(shape):
    return lax.broadcasted_iota(jnp.int32, shape, 0)


def lane_of(shape):
    return lax.broadcasted_iota(jnp.int32, shape, 1)


def up(a, shift):
    shift %= a.shape[0]
    return pltpu.roll(a, shift, 0) if shift else a


def pool_matrix(value):
    lane = row_of((LANES, MID_LANES))
    mid = jnp.where(lane < Z + 64, lane // 2, lane // 2 + 64)
    return jnp.where(mid == lane_of((LANES, MID_LANES)), value, 0.0).astype(F32)


def spread_matrix():
    lane = lane_of((MID_LANES, LANES))
    mid = jnp.where(lane < Z + 64, lane // 2, lane // 2 + 64)
    return jnp.where(mid == row_of((MID_LANES, LANES)), 1.0, 0.0).astype(F32)


def put_tiles(ref, at, value):
    for k in range(ref.shape[0]):
        ref[k, at : at + value.shape[0]] = value[:, 128 * k : 128 * k + 128]


def every_other(ref, at, size):
    return jnp.concatenate(
        [ref[k, pl.ds(at, size, stride=2)] for k in range(ref.shape[0])], axis=1
    )


def exact_dot(a, b):
    return jnp.dot(a, b, precision=lax.Precision.HIGHEST, preferred_element_type=F32)


X_PACK = COMPS * RIM + WIDE
R_TILES = COMPS * X
E_PLANES = X + 2 * WIDE
E4_TILES = E_PLANES // 2
E2_TILES = E_PLANES // 4
Y_PACK = R_TILES + E4_TILES + E2_TILES
Z_TILES = COMPS * (X + 2 * RIM) * (ROWS // 8) + E_PLANES * 3
Z_PACK = -(-Z_TILES // 16) * 8


def pack_x_body(table, index_in, res_in, res, young, pack_even, pack_odd, index, sems):
    get_index = pltpu.make_async_copy(index_in, index, sems.at[0])
    get_res = pltpu.make_async_copy(res_in, res, sems.at[1])
    get_index.start()
    get_res.start()
    get_index.wait()
    levels = index[...]
    value = jnp.zeros(levels.shape, F32)
    for level in range(table.shape[0]):
        value = jnp.where(levels == level, table[level], value)
    young[...] = value
    get_res.wait()
    even = is_even("gx")
    high_first = jnp.where(even, 1, 0)
    for pack, high in ((pack_even, high_first), (pack_odd, 1 - high_first)):
        for c in range(COMPS):
            pack[c * RIM : (c + 1) * RIM] = res[c, pl.ds(high * (X - RIM), RIM)]
        pack[COMPS * RIM :] = young[pl.ds(high * (X - WIDE), WIDE)]


def x_planes(res, young, got_x, lanes=slice(None)):
    lower, upper = from_sides(got_x, "gx")
    whole = slice(None)

    def res_plane(c, i):
        if i < RIM:
            return lower((c * RIM + i, whole, lanes))
        if i < RIM + X:
            return res[c, i - RIM, :, lanes]
        return upper((c * RIM + i - RIM - X, whole, lanes))

    def young_plane(i):
        if i < WIDE:
            return lower((COMPS * RIM + i, whole, lanes))
        if i < WIDE + X:
            return young[i - WIDE, :, lanes]
        return upper((COMPS * RIM + i - WIDE - X, whole, lanes))

    return res_plane, young_plane


def pack_y_body(res, young, got_a, got_b, pack_even, pack_odd):
    res_plane, young_plane = x_planes(res, young, (got_a, got_b))
    row = row_of((Y, Z))
    even = is_even("gy")

    def put(tile, low, high):
        pack_even[tile] = jnp.where(even, high, low)
        pack_odd[tile] = jnp.where(even, low, high)

    def halves(tile, a, b):
        put(
            tile,
            jnp.where(row < 4, a, up(b, 4)),
            jnp.where(row < 4, up(a, 4), b),
        )

    for c in range(COMPS):
        for i in range(X):
            halves(c * X + i, res_plane(c, i), res_plane(c, i + X))
    planes = [young_plane(i) for i in range(E_PLANES)]
    for i in range(E4_TILES):
        halves(R_TILES + i, planes[i], planes[i + E4_TILES])
    for j in range(E2_TILES):
        low = high = None
        for k in range(4):
            plane = planes[4 * j + k]
            a, b = up(plane, 2 * k - 4), up(plane, 2 * k - 2)
            low = a if k == 0 else jnp.where(row < 2 * k, low, a)
            high = b if k == 0 else jnp.where(row < 2 * k, high, b)
        put(R_TILES + E4_TILES + j, low, high)


def xy_planes(res, young, got_x, got_y, lanes, width):
    res_plane, young_plane = x_planes(res, young, got_x, lanes)
    lower, upper = from_sides(got_y, "gy")
    row = row_of((Y, width))
    whole = slice(None)

    def res_tiles(c, i):
        own = up(res_plane(c, i), 4)
        key = (c * X + i % X, whole, lanes)
        low, high = lower(key), upper(key)
        if i < X:
            high = up(high, 4)
        else:
            low = up(low, 4)
        return [jnp.where(row < 4, low, own), jnp.where(row < 4, own, high)]

    def young_tiles(i):
        four = (R_TILES + i % E4_TILES, whole, lanes)
        two = (R_TILES + E4_TILES + i // 4, whole, lanes)
        k = i % 4
        low4, high4 = lower(four), upper(four)
        if i < E4_TILES:
            low4 = up(low4, 4)
        else:
            high4 = up(high4, 4)
        low2, high2 = up(lower(two), 2 - 2 * k), up(upper(two), 4 - 2 * k)
        low = jnp.where(row < 4, jnp.where(row < 2, 0.0, low2), low4)
        high = jnp.where(row < 4, high4, jnp.where(row < 6, high2, 0.0))
        return [low, young_plane(i), high]

    return res_tiles, young_tiles


def pack_z_body(res, young, xa, xb, ya, yb, *packs):
    high_first = jnp.where(is_even("gz"), 1, 0)
    lane = lane_of((8, 128))
    for pack, high in zip(packs, (high_first, 1 - high_first)):
        lanes = pl.ds(pl.multiple_of(high * (Z - 128), 128), 128)
        res_tiles, young_tiles = xy_planes(res, young, (xa, xb), (ya, yb), lanes, 128)
        tiles = [t for c in range(COMPS) for i in range(X + 2 * RIM) for t in res_tiles(c, i)]
        tiles += [t for i in range(E_PLANES) for t in young_tiles(i)]
        for first in range(0, len(tiles), 16):
            packed = None
            for j, tile in enumerate(tiles[first : first + 16]):
                moved = pltpu.roll(tile, lax.rem(8 * j + 8 * high, 128), 1)
                packed = moved if j == 0 else jnp.where(lane < 8 * j, packed, moved)
            pack[first // 2 : first // 2 + 8] = packed


def z_rims(got_z):
    lane = lane_of((8, 128))
    even = is_even("gz")

    def piece(got, t, right):
        start = jnp.where(right, 0, 120)
        tile = got[8 * (t // 16) : 8 * (t // 16) + 8, :]
        moved = pltpu.roll(tile, lax.rem(start + 128 - 8 * (t % 16), 128), 1)
        inside = jnp.logical_and(lane >= start, lane < start + 8)
        return jnp.where(inside, moved, 0.0)

    def rim(t):
        first = piece(got_z[0], t, even)
        if len(got_z) == 1:
            return first
        second = piece(got_z[1], t, jnp.logical_not(even))
        return first + jnp.where(inner("gz"), second, 0.0)

    return rim


M_PLANES = X // 2 + 4
EM_PLANES = X // 2 + 6
LOW_TILE = COMPS * (X // 2)
MZ_PACK = (LOW_TILE + 1) * 8


def fine_apply(s, es, c1, e, i):
    parts = []
    for c in range(COMPS):
        v = tri_y(tri_x(s[c, i - 1], s[c, i], s[c, i + 1]))
        ev = tri_y(tri_x(es[c, i - 1], es[c, i], es[c, i + 1]))
        total = pltpu.roll(e[1, i] * v + ev, 1, 1) + pltpu.roll(e[2, i] * v + ev, LANES - 1, 1)
        both = e[0, i] * v + ev
        parts.append(c1[i] * s[c, i] - (total + (both + both)))
    return coupled(parts)


def smooth_body(n_z, *refs):
    res, young, xa, xb, ya, yb = refs[:6]
    got_z = refs[6 : 6 + n_z]
    r, s1, e, c1, w, em, c1m, wm, pack = refs[6 + n_z : 15 + n_z]
    wide, s0, es0, es1, rest, pooled, wide_x, wide_p = refs[15 + n_z :]

    res_tiles, young_tiles = xy_planes(res, young, (xa, xb), (ya, yb), slice(None), Z)
    rim = z_rims(got_z)
    at = 0
    for c in range(COMPS):
        for i in range(X + 2 * RIM):
            for t, tile in enumerate(res_tiles(c, i)):
                r[c, i, 8 * t : 8 * t + 8, :Z] = tile
                r[c, i, 8 * t : 8 * t + 8, Z:] = rim(at)
                at += 1
    for i in range(E_PLANES):
        for t, tile in enumerate(young_tiles(i)):
            wide[i, 8 * t : 8 * t + 8, :Z] = tile * 0.0125
            wide[i, 8 * t : 8 * t + 8, Z:] = rim(at) * 0.0125
            at += 1

    def prepare(i, _):
        total = tri_yz(tri_x(wide[i + 1], wide[i + 2], wide[i + 3]))[4:20]
        centre = wide[i + 2, 4:20]
        e[0, i] = centre
        e[1, i] = pltpu.roll(centre, LANES - 1, 1)
        e[2, i] = pltpu.roll(centre, 1, 1)
        c1[i] = 72.0 * centre + total
        inverse = jnp.where(centre > 0.0, DAMPING / (56.0 * centre + total), 0.0)
        w[i] = inverse
        for c in range(COMPS):
            value = inverse * r[c, i]
            s0[c, i] = value
            es0[c, i] = centre * value
        return _

    lax.fori_loop(0, X + 2 * RIM, prepare, 0)

    def sweep(i, _):
        applied = fine_apply(s0, es0, c1, e, i)
        for c in range(COMPS):
            value = s0[c, i] + w[i] * (r[c, i] - applied[c])
            s1[c, i] = value
            es1[c, i] = e[0, i] * value
        return _

    lax.fori_loop(1, X + 2 * RIM - 1, sweep, 0, unroll=2)

    def residue(m, _):
        first = fine_apply(s1, es1, c1, e, 2 * m + 2)
        second = fine_apply(s1, es1, c1, e, 2 * m + 3)
        for c in range(COMPS):
            total = (r[c, 2 * m + 2] - first[c]) + (r[c, 2 * m + 3] - second[c])
            rest[pl.ds((c * 6 + m) * ROWS, ROWS)] = total
        return _

    lax.fori_loop(0, 6, residue, 0)

    pool = pool_matrix(0.5)
    put_tiles(pooled, 0, exact_dot(rest[...], pool))
    for m in range(EM_PLANES):
        wide_x[24 * m : 24 * m + 24] = wide[2 * m] + wide[2 * m + 1]
    wide_p[...] = jnp.zeros(wide_p.shape, F32)
    put_tiles(wide_p, 0, exact_dot(wide_x[...], pool))
    for m in range(EM_PLANES):
        a = every_other(wide_p, 24 * m, 16) + every_other(wide_p, 24 * m + 1, 16)
        em[m] = jnp.where(row_of(a.shape) < 12, 0.25 * a, 0.0)
    for m in range(M_PLANES):
        total = tri_yz(tri_x(em[m], em[m + 1], em[m + 2]))[2:10]
        centre = em[m + 1, 2:10]
        c1m[m] = 72.0 * centre + total
        wm[m] = jnp.where(centre > 0.0, DAMPING / (56.0 * centre + total), 0.0)

    rhs, mid, e_mid = {}, {}, {}
    for m in range(6):
        centre = em[m + 2, 2:10]
        for c in range(COMPS):
            at = (c * 6 + m) * ROWS
            a = every_other(pooled, at, 8) + every_other(pooled, at + 1, 8)
            rhs[c, m] = a
            mid[c, m] = wm[m + 1] * a
            e_mid[c, m] = centre * mid[c, m]
    rows = []
    kept = {}
    for m in range(1, 5):
        parts = []
        for c in range(COMPS):
            tv = tri_yz(tri_x(mid[c, m - 1], mid[c, m], mid[c, m + 1]))
            te = tri_yz(tri_x(e_mid[c, m - 1], e_mid[c, m], e_mid[c, m + 1]))
            parts.append(c1m[m + 1] * mid[c, m] - (em[m + 2, 2:10] * tv + te))
        applied = coupled(parts)
        for c in range(COMPS):
            left_over = rhs[c, m] - applied[c]
            kept[c, m - 1] = left_over
            value = mid[c, m] + wm[m + 1] * left_over
            tile = c * 4 + m - 1
            pack[8 * tile : 8 * tile + 8] = value[:, :128]
    for c in range(COMPS):
        for b in range(2):
            rows.append(kept[c, 2 * b] + kept[c, 2 * b + 1])
    stacked = jnp.concatenate(rows, axis=0)
    lane_box = row_of((MID_LANES, 128))
    column = lane_of((MID_LANES, 128))
    boxes = jnp.where(
        jnp.logical_and(lane_box < Z // 2, lane_box // 64 == column % 2), 1.0, 0.0
    ).astype(F32)
    sums = exact_dot(stacked, boxes)
    line = row_of((48, 128))
    entry = lane_of((48, 128))
    inside = line % 8
    match = (line // 8) * 2 + (inside - 2) // 2 == entry // 2
    match = jnp.logical_and(match, jnp.logical_and(inside >= 2, inside < 6))
    scale = 1.0 / math.sqrt((X // 4) * (Y // 4) * (Z // 4))
    low = jnp.sum(jnp.where(match, sums, 0.0), axis=0, keepdims=True) * scale
    pack[8 * LOW_TILE :] = jnp.broadcast_to(low, (8, 128))


def coarse_body(n_z, *refs):
    pack = refs[0]
    got_z = refs[1 : 1 + n_z]
    matrix = refs[1 + n_z]
    gathered = refs[2 + n_z : -5]
    planes, column, pack_even, pack_odd, scratch = refs[-5:]
    place = lax.axis_index("gz")
    count = lax.axis_size("gz")
    left, right = from_sides(got_z, "gz")
    lane = lane_of((8, 128))
    for t in range(LOW_TILE):
        key = (slice(8 * t, 8 * t + 8), slice(None))
        planes[t, :, :128] = pack[key]
        planes[t, :, 128:] = jnp.where(lane < 64, right(key), left(key))

    size = 24
    if gathered:
        rhs = gathered[0][...]
    else:
        mine = pack[8 * LOW_TILE : 8 * LOW_TILE + 8]
        other = got_z[0][8 * LOW_TILE : 8 * LOW_TILE + 8]
        first = jnp.where(place == 0, mine, other)
        second = jnp.where(place == 0, other, mine)
        rhs = jnp.where(lane < size, first, pltpu.roll(second, size, 1))[:1, : 2 * size]
    solved = jnp.sum(matrix[0, 0] * rhs, axis=1, keepdims=True)
    scratch[...] = jnp.zeros(scratch.shape, F32)
    scratch[size : size + solved.shape[0]] = jnp.broadcast_to(solved, (solved.shape[0], 128))
    base = pl.multiple_of(place * size, 8)
    wide = lane_of((16, MID_LANES))
    before, own_a, own_b, after = [
        jnp.concatenate([scratch[pl.ds(base + at, 16, stride=2)]] * 2, axis=1)
        for at in (1, size, size + 1, 2 * size)
    ]
    value = jnp.where(wide < 64, own_a, own_b)
    value = jnp.where(wide < 128, value, jnp.where(wide < 192, after, before))
    value = jnp.where(row_of((16, MID_LANES)) < 12, value, 0.0)
    column[...] = value

    even = is_even("gx")
    row = row_of((8, MID_LANES))
    for c in range(COMPS):
        tiles = [
            jnp.where(row < 4, up(planes[c * 4 + p], -2), up(planes[c * 4 + p + 1], 2))
            for p in (0, 2)
        ]
        pack_even[8 * c : 8 * c + 8] = jnp.where(even, tiles[1], tiles[0])
        pack_odd[8 * c : 8 * c + 8] = jnp.where(even, tiles[0], tiles[1])
    pack_even[24:] = value
    pack_odd[24:] = value


MX_PACK = 24 + 16
MY_PACK = 48 + 40


def mid_y_body(planes, column, got_a, got_b, wide_planes, columns, pack_even, pack_odd):
    lower, upper = from_sides((got_a, got_b), "gx")
    whole = slice(None)
    row = row_of((8, MID_LANES))
    even = is_even("gy")
    for c in range(COMPS):
        key = (slice(8 * c, 8 * c + 8), whole)
        low, high = lower(key), upper(key)
        tiles = [up(low, 2), up(low, -2)]
        tiles += [planes[c * 4 + p] for p in range(4)]
        tiles += [up(high, 2), up(high, -2)]
        for t in range(8):
            wide_planes[c * 8 + t] = tiles[t]
        for h in range(2):
            below = above = None
            for k in range(4):
                tile = tiles[4 * h + k]
                a, b = up(tile, 2 * k - 2), up(tile, 2 * k - 4)
                below = a if k == 0 else jnp.where(row < 2 * k, below, a)
                above = b if k == 0 else jnp.where(row < 2 * k, above, b)
            at = (c * 2 + h) * 8
            pack_even[at : at + 8] = jnp.where(even, above, below)
            pack_odd[at : at + 8] = jnp.where(even, below, above)
    columns[:12] = lower((slice(24, 36), whole))
    columns[12:24] = column[:12]
    columns[24:36] = upper((slice(24, 36), whole))
    columns[36:] = jnp.zeros((4, MID_LANES), F32)
    pack_even[48:] = columns[...]
    pack_odd[48:] = columns[...]


def finish_body(
    wide_planes, columns, got_a, got_b, r, s1, e, c1, w, em, c1m, wm, prev_d, prev_i,
    precond_out, operated_out, sums, cor, mid, big, s2, es2, s3, es3, p, ep, precond, operated, sems,
):
    lower, upper = from_sides((got_a, got_b), "gy")
    whole = slice(None)
    row = row_of((8, MID_LANES))
    line = row_of((16, MID_LANES))

    below = lower((slice(48, 88), whole))
    above = upper((slice(48, 88), whole))
    middle = columns[...]
    for c in range(COMPS):
        for b in range(6):
            at = (b // 2) * 12 + c * 4 + (b % 2) * 2
            bands = [source[at + by : at + by + 1] for source in (below, middle, above) for by in range(2)]
            field = jnp.zeros((16, MID_LANES), F32)
            for t, band in enumerate(bands):
                inside = jnp.logical_and(line >= 2 * t, line < 2 * t + 2)
                field = jnp.where(inside, jnp.broadcast_to(band, (16, MID_LANES)), field)
            cor[c, b] = field

    def box(m):
        return (m + 1) // 2

    for m in range(M_PLANES):
        parts = []
        for c in range(COMPS):
            near = [cor[c, box(m + k)] for k in range(3)]
            tv = tri_yz(tri_x(*near))
            te = tri_yz(tri_x(*[em[m + k] * near[k] for k in range(3)]))
            part = em[m + 1] * tv + te
            parts.append(c1m[m] * near[1][2:10] - part[2:10])
        applied = coupled(parts)
        for c in range(COMPS):
            tile = wide_planes[c * 8 + m]
            at = ((c * 2 + m // 4) * 8, (c * 2 + m // 4) * 8 + 8)
            key = (slice(*at), whole)
            k = m % 4
            tile = jnp.where(row < 2, up(lower(key), -2 * k), tile)
            tile = jnp.where(row < 6, tile, up(upper(key), 6 - 2 * k))
            value = tile + cor[c, box(m + 1), 2:10] - wm[m] * applied[c]
            at = (c * 8 + m) * 8
            mid[at : at + 8] = value
    spread = exact_dot(mid[...], spread_matrix())
    for t in range(COMPS * 8):
        piece = spread[8 * t : 8 * t + 8]
        for k in range(LANES // 128):
            tile = piece[:, 128 * k : 128 * k + 128]
            big[k, pl.ds(16 * t, 8, stride=2)] = tile
            big[k, pl.ds(16 * t + 1, 8, stride=2)] = tile

    def add_up(i, _):
        for c in range(COMPS):
            at = pl.multiple_of((c * 8 + i // 2) * 16, 16)
            more = [big[k, pl.ds(at, 16)] for k in range(LANES // 128)]
            value = s1[c, i] + jnp.concatenate(more, axis=1)
            s2[c, i] = value
            es2[c, i] = e[0, i] * value
        return _

    lax.fori_loop(1, X + 2 * RIM - 1, add_up, 0)

    def sweep(source, e_source, target, e_target):
        def body(i, _):
            applied = fine_apply(source, e_source, c1, e, i)
            for c in range(COMPS):
                value = source[c, i] + w[i] * (r[c, i] - applied[c])
                target[c, i] = value
                e_target[c, i] = e[0, i] * value
            return _

        return body

    lax.fori_loop(2, X + 2 * RIM - 2, sweep(s2, es2, s3, es3), 0, unroll=2)
    lax.fori_loop(3, X + 2 * RIM - 3, sweep(s3, es3, p, ep), 0, unroll=2)
    leaving = (
        (precond, precond_out, sems.at[0]),
        (operated, operated_out, sems.at[1]),
    )

    def image(i, carry):
        applied = fine_apply(p, ep, c1, e, i)
        x = i - RIM
        rz, pp, mix, old = carry
        for c in range(COMPS):
            own_p = p[c, i, 4:12, :Z]
            own_a = applied[c][4:12, :Z]
            precond[x, c] = own_p
            operated[x, c] = own_a
            d, q = prev_d[c, x], prev_i[c, x]
            rz += r[c, i, 4:12, :Z] * own_p
            pp += own_p * own_a
            mix += own_p * q + d * own_a
            old += d * q
        for source, target, sem in leaving:
            pltpu.make_async_copy(source.at[x], target.at[x], sem).start()
        return rz, pp, mix, old

    zero = jnp.zeros((Y, Z), F32)
    found = lax.fori_loop(RIM, RIM + X, image, (zero, zero, zero, zero))
    lane = lane_of((1, 128))
    total = jnp.zeros((1, 128), F32)
    for k, value in enumerate(found):
        total = jnp.where(lane == k, jnp.sum(value), total)
    sums[...] = jnp.broadcast_to(total, sums.shape)
    for source, target, sem in leaving:
        pltpu.make_async_copy(source, target, sem).wait()


def last_body(
    prev_rz, sums, precond_in, operated_in, prev_d_in, prev_i_in, sol_in, res_in,
    new_s_out, new_r_out, new_d_out, new_i_out, precond, operated, fields, news, sems,
):
    arriving = [
        pltpu.make_async_copy(precond_in, precond, sems.at[0]),
        pltpu.make_async_copy(operated_in, operated, sems.at[1]),
    ]
    for k, source in enumerate((prev_d_in, prev_i_in, sol_in, res_in)):
        arriving.append(pltpu.make_async_copy(source, fields.at[k], sems.at[2 + k]))
    for copy in arriving:
        copy.start()
    total = jnp.sum(sums[...], axis=0, keepdims=True)
    lane = lane_of((1, 128))

    def entry(k):
        return jnp.sum(jnp.where(lane == k, total, 0.0), axis=1, keepdims=True)

    rz = entry(0)
    beta = rz / prev_rz[0]
    alpha = rz / (entry(1) + beta * (entry(2) + beta * entry(3)))
    beta = jnp.broadcast_to(beta, (Y, Z))
    alpha = jnp.broadcast_to(alpha, (Y, Z))
    for copy in arriving:
        copy.wait()
    leaving = []
    for c in range(COMPS):
        for x in range(X):
            d = precond[x, c] + beta * fields[0, c, x]
            q = operated[x, c] + beta * fields[1, c, x]
            news[2, c, x] = d
            news[3, c, x] = q
            news[0, c, x] = fields[2, c, x] + alpha * d
            news[1, c, x] = fields[3, c, x] - alpha * q
        for k, target in enumerate((new_s_out, new_r_out, new_d_out, new_i_out)):
            copy = pltpu.make_async_copy(news.at[k, c], target.at[c], sems.at[6 + 3 * k + c])
            copy.start()
            leaving.append(copy)
    for copy in leaving:
        copy.wait()


def on_device(
    solution,
    residual,
    prev_direction,
    prev_image,
    prev_rz,
    density_index,
    stiffness_table,
    coarse_inverse,
):
    if residual.shape != (COMPS, X, Y, Z):
        raise ValueError(residual.shape)
    block = shape(COMPS, X, Y, Z)
    n_z = 1 if lax.axis_size("gz") == 2 else 2
    n_all = lax.axis_size(ALL)

    res, young, px, qx = call(
        pack_x_body,
        [block, shape(X, Y, Z), shape(X_PACK, Y, Z), shape(X_PACK, Y, Z)],
        scratch=[pltpu.VMEM((X, Y, Z), jnp.int32), pltpu.SemaphoreType.DMA((2,))],
        n_in=3,
        smem=(0,),
        hbm=(1, 2),
    )(stiffness_table, density_index, residual)
    got_x = swap("gx", px, qx)
    py, qy = call(pack_y_body, [shape(Y_PACK, Y, Z)] * 2, n_in=4)(res, young, *got_x)
    got_y = swap("gy", py, qy, closed=False)
    packs = call(pack_z_body, [shape(Z_PACK, 128)] * n_z, n_in=6)(res, young, *got_x, *got_y)
    got_z = swap("gz", packs[0], packs[-1])

    planes = X + 2 * RIM
    field = (COMPS, planes, ROWS, LANES)
    r, s1, e, c1, w, em, c1m, wm, pack = call(
        functools.partial(smooth_body, n_z),
        [
            shape(*field),
            shape(*field),
            shape(3, planes, ROWS, LANES),
            shape(planes, ROWS, LANES),
            shape(planes, ROWS, LANES),
            shape(EM_PLANES, 16, MID_LANES),
            shape(M_PLANES, 8, MID_LANES),
            shape(M_PLANES, 8, MID_LANES),
            shape(MZ_PACK, 128),
        ],
        scratch=[
            pltpu.VMEM((E_PLANES, 24, LANES), F32),
            pltpu.VMEM(field, F32),
            pltpu.VMEM(field, F32),
            pltpu.VMEM(field, F32),
            pltpu.VMEM((18 * ROWS, LANES), F32),
            pltpu.VMEM((MID_LANES // 128, 18 * ROWS, 128), F32),
            pltpu.VMEM((24 * EM_PLANES, LANES), F32),
            pltpu.VMEM((MID_LANES // 128, 24 * EM_PLANES + 16, 128), F32),
        ],
        n_in=6 + n_z,
        mib=30,
    )(res, young, *got_x, *got_y, *got_z)

    got_z = swap("gz", pack, pack)
    gathered = []
    if n_z > 1:
        gathered = [lax.all_gather(pack[8 * LOW_TILE, :24], "gz", axis=0, tiled=True)[None]]
    size = coarse_inverse.shape[-1]
    mid_planes, column, px, qx = call(
        functools.partial(coarse_body, n_z),
        [
            shape(LOW_TILE, 8, MID_LANES),
            shape(16, MID_LANES),
            shape(MX_PACK, MID_LANES),
            shape(MX_PACK, MID_LANES),
        ],
        scratch=[pltpu.VMEM((size + 64, 128), F32)],
        n_in=2 + n_z + len(gathered),
    )(pack, *got_z, coarse_inverse, *gathered)
    got_x = swap("gx", px, qx)
    mid_planes, columns, py, qy = call(
        mid_y_body,
        [
            shape(COMPS * 8, 8, MID_LANES),
            shape(40, MID_LANES),
            shape(MY_PACK, MID_LANES),
            shape(MY_PACK, MID_LANES),
        ],
        n_in=4,
    )(mid_planes, column, *got_x)
    got_y = swap("gy", py, qy)
    precond, operated, sums = call(
        finish_body,
        [shape(X, COMPS, Y, Z), shape(X, COMPS, Y, Z), shape(n_all, 128)],
        scratch=[
            pltpu.VMEM((COMPS, 6, 16, MID_LANES), F32),
            pltpu.VMEM((COMPS * 64, MID_LANES), F32),
            pltpu.VMEM((LANES // 128, COMPS * 128, 128), F32),
        ]
        + [pltpu.VMEM(field, F32)] * 6
        + [pltpu.VMEM((X, COMPS, Y, Z), F32)] * 2
        + [pltpu.SemaphoreType.DMA((2,))],
        n_in=14,
        hbm_out=(0, 1),
        mib=30,
    )(mid_planes, columns, *got_y, r, s1, e, c1, w, em, c1m, wm, prev_direction, prev_image)
    sums = lax.all_to_all(sums, ALL, 0, 0, tiled=True)
    return tuple(
        call(
            last_body,
            [block] * 4,
            scratch=[pltpu.VMEM((X, COMPS, Y, Z), F32)] * 2
            + [pltpu.VMEM((4, COMPS, X, Y, Z), F32)] * 2
            + [pltpu.SemaphoreType.DMA((18,))],
            n_in=8,
            smem=(0,),
            hbm=(2, 3, 4, 5, 6, 7),
            hbm_out=(0, 1, 2, 3),
        )(
            prev_rz.reshape(1), sums, precond, operated, prev_direction, prev_image, solution, residual
        )
    )


def solution(mesh):
    field = P(None, "gx", "gy", "gz")
    return jax.shard_map(
        on_device,
        mesh=mesh,
        in_specs=(
            field,
            field,
            field,
            field,
            P(),
            P("gx", "gy", "gz"),
            P(),
            P("gx", "gy", None, None),
        ),
        out_specs=(field, field, field, field),
        check_vma=False,
    )
```

```python
import functools
import math

import jax
import jax.numpy as jnp
from jax import lax
from jax.experimental import pallas as pl
from jax.experimental.pallas import tpu as pltpu
from jax.sharding import PartitionSpec as P

X, Y, Z = 8, 8, 256
COMPS = 3
RIM = 4
WIDE = 6
ROWS = Y + 2 * RIM
LANES = Z + 128
MID_LANES = Z // 2 + 128
DAMPING = 0.6
ALL = ("gx", "gy", "gz")
F32 = jnp.float32
VMEM = pl.BlockSpec(memory_space=pltpu.VMEM)
SMEM = pl.BlockSpec(memory_space=pltpu.SMEM)
HBM = pl.BlockSpec(memory_space=pltpu.HBM)


def shape(*dims):
    return jax.ShapeDtypeStruct(dims, F32)


def call(body, outs, scratch=(), n_in=0, smem=(), hbm=(), hbm_out=(), vmem=16 << 20):
    return pl.pallas_call(
        body,
        out_shape=outs,
        in_specs=[SMEM if i in smem else HBM if i in hbm else VMEM for i in range(n_in)],
        out_specs=[HBM if i in hbm_out else VMEM for i in range(len(outs))],
        scratch_shapes=list(scratch),
        compiler_params=pltpu.CompilerParams(vmem_limit_bytes=vmem),
    )


def pairs(count, odd, closed):
    if not odd:
        return [(i, i ^ 1) for i in range(count)]
    made = [(i, (i + 1) % count if i % 2 else (i - 1) % count) for i in range(count)]
    return made if closed else made[1:-1]


def swap(axis, even_pack, odd_pack, closed=True):
    count = lax.axis_size(axis)
    got_even = lax.ppermute(even_pack, axis, pairs(count, False, closed))
    if count == 2:
        return [got_even]
    return [got_even, lax.ppermute(odd_pack, axis, pairs(count, True, closed))]


def is_even(axis):
    return lax.rem(lax.axis_index(axis), 2) == 0


def inner(axis):
    index = lax.axis_index(axis)
    return jnp.logical_and(index > 0, index < lax.axis_size(axis) - 1)


def from_sides(got, axis):
    even = is_even(axis)
    if len(got) == 1:

        def lower(key):
            value = got[0][key]
            return jnp.where(even, 0.0, value)

        def upper(key):
            value = got[0][key]
            return jnp.where(even, value, 0.0)

        return lower, upper
    ok = inner(axis)

    def lower(key):
        return jnp.where(even, jnp.where(ok, got[1][key], 0.0), got[0][key])

    def upper(key):
        return jnp.where(even, got[0][key], jnp.where(ok, got[1][key], 0.0))

    return lower, upper


def tri_y(a):
    a = a + pltpu.roll(a, 1, 0)
    return a + pltpu.roll(a, a.shape[0] - 1, 0)


def tri_y_with(a, below, above, last):
    rows = a.shape[0]
    row = row_of(a.shape)
    former = jnp.where(row == last + 1, below, pltpu.roll(a, 1, 0))
    after = jnp.where(row == last, above, pltpu.roll(a, rows - 1, 0))
    return former + after + (a + a)


def mixed_z(e, e_next, e_last, v, ev):
    both = e * v + ev
    moved = pltpu.roll(e_next * v + ev, 1, 1) + pltpu.roll(e_last * v + ev, v.shape[1] - 1, 1)
    return moved + (both + both)


def tri_x(before, centre, after):
    return before + after + (centre + centre)


def coupled(parts):
    total = 0.3 * (parts[0] + parts[1] + parts[2])
    return [0.7 * part + total for part in parts]


def row_of(shape):
    return lax.broadcasted_iota(jnp.int32, shape, 0)


def lane_of(shape):
    return lax.broadcasted_iota(jnp.int32, shape, 1)


def up(a, shift):
    shift %= a.shape[0]
    return pltpu.roll(a, shift, 0) if shift else a


def pool_matrix(value):
    lane = row_of((LANES, MID_LANES))
    mid = jnp.where(lane < Z + 64, lane // 2, lane // 2 + 64)
    return jnp.where(mid == lane_of((LANES, MID_LANES)), value, 0.0).astype(F32)


def spread_matrix():
    lane = lane_of((MID_LANES, LANES))
    mid = jnp.where(lane < Z + 64, lane // 2, lane // 2 + 64)
    return jnp.where(mid == row_of((MID_LANES, LANES)), 1.0, 0.0).astype(F32)


def every_other(ref, at, size):
    return jnp.concatenate(
        [ref[k, pl.ds(at, size, stride=2)] for k in range(ref.shape[0])], axis=1
    )


def dot_exact_weights(a, b):
    b = b.astype(jnp.bfloat16)
    total = None
    for k in range(3):
        part = a.astype(jnp.bfloat16)
        found = jnp.dot(part, b, preferred_element_type=F32)
        total = found if total is None else total + found
        if k < 2:
            a = a - part.astype(F32)
    return total


X_PACK = COMPS * RIM + WIDE
R_TILES = COMPS * X
E_PLANES = X + 2 * WIDE
E4_TILES = E_PLANES // 2
E2_TILES = E_PLANES // 4
Y_PACK = R_TILES + E4_TILES + E2_TILES
Z_TILES = COMPS * (X + 2 * RIM) * (ROWS // 8) + E_PLANES * 3
Z_PACK = -(-Z_TILES // 16) * 8


def pack_x_body(table, index, res_in, res, young, pack_even, pack_odd):
    res[...] = res_in[...]
    levels = index[...]
    value = jnp.zeros(levels.shape, F32)
    for level in range(table.shape[0]):
        value = jnp.where(levels == level, table[level], value)
    young[...] = value
    high_first = jnp.where(is_even("gx"), 1, 0)
    for pack, high in ((pack_even, high_first), (pack_odd, 1 - high_first)):
        for c in range(COMPS):
            pack[c * RIM : (c + 1) * RIM] = res[c, pl.ds(high * (X - RIM), RIM)]
        pack[COMPS * RIM :] = young[pl.ds(high * (X - WIDE), WIDE)]


def x_planes(res, young, got_x, lanes=slice(None)):
    lower, upper = from_sides(got_x, "gx")
    whole = slice(None)

    def res_plane(c, i):
        if i < RIM:
            return lower((c * RIM + i, whole, lanes))
        if i < RIM + X:
            return res[c, i - RIM, :, lanes]
        return upper((c * RIM + i - RIM - X, whole, lanes))

    def young_plane(i):
        if i < WIDE:
            return lower((COMPS * RIM + i, whole, lanes))
        if i < WIDE + X:
            return young[i - WIDE, :, lanes]
        return upper((COMPS * RIM + i - WIDE - X, whole, lanes))

    return res_plane, young_plane


def pack_y_body(res, young, got_a, got_b, pack_even, pack_odd):
    res_plane, young_plane = x_planes(res, young, (got_a, got_b))
    row = row_of((Y, Z))
    even = is_even("gy")

    def put(tile, low, high):
        pack_even[tile] = jnp.where(even, high, low)
        pack_odd[tile] = jnp.where(even, low, high)

    def halves(tile, a, b):
        put(
            tile,
            jnp.where(row < 4, a, up(b, 4)),
            jnp.where(row < 4, up(a, 4), b),
        )

    for c in range(COMPS):
        for i in range(X):
            halves(c * X + i, res_plane(c, i), res_plane(c, i + X))
    planes = [young_plane(i) for i in range(E_PLANES)]
    for i in range(E4_TILES):
        halves(R_TILES + i, planes[i], planes[i + E4_TILES])
    for j in range(E2_TILES):
        low = high = None
        for k in range(4):
            plane = planes[4 * j + k]
            a, b = up(plane, 2 * k - 4), up(plane, 2 * k - 2)
            low = a if k == 0 else jnp.where(row < 2 * k, low, a)
            high = b if k == 0 else jnp.where(row < 2 * k, high, b)
        put(R_TILES + E4_TILES + j, low, high)


def xy_planes(res, young, got_x, got_y, lanes, width):
    res_plane, young_plane = x_planes(res, young, got_x, lanes)
    lower, upper = from_sides(got_y, "gy")
    row = row_of((Y, width))
    whole = slice(None)

    def rim_tile(tile, second):
        key = (tile, whole, lanes)
        low, high = lower(key), upper(key)
        if second:
            high = up(high, 4)
        else:
            low = up(low, 4)
        return jnp.where(row < 4, high, low)

    def res_tiles(c, i):
        return [res_plane(c, i), rim_tile(c * X + i % X, i >= X)]

    def young_tiles(i):
        two = (R_TILES + E4_TILES + i // 4, whole, lanes)
        k = i % 4
        low2, high2 = up(lower(two), -2 * k), up(upper(two), 2 - 2 * k)
        side = jnp.where(row < 2, low2, jnp.where(row < 4, high2, 0.0))
        return [young_plane(i), rim_tile(R_TILES + i % E4_TILES, i >= E4_TILES), side]

    return res_tiles, young_tiles


def pack_z_body(res, young, xa, xb, ya, yb, *packs):
    high_first = jnp.where(is_even("gz"), 1, 0)
    lane = lane_of((8, 128))
    for pack, high in zip(packs, (high_first, 1 - high_first)):
        lanes = pl.ds(pl.multiple_of(high * (Z - 128), 128), 128)
        res_tiles, young_tiles = xy_planes(res, young, (xa, xb), (ya, yb), lanes, 128)
        tiles = [t for c in range(COMPS) for i in range(X + 2 * RIM) for t in res_tiles(c, i)]
        tiles += [t for i in range(E_PLANES) for t in young_tiles(i)]
        for first in range(0, len(tiles), 16):
            packed = None
            for j, tile in enumerate(tiles[first : first + 16]):
                moved = pltpu.roll(tile, lax.rem(8 * j + 8 * high, 128), 1)
                packed = moved if j == 0 else jnp.where(lane < 8 * j, packed, moved)
            pack[first // 2 : first // 2 + 8] = packed


def z_rims(got_z):
    lane = lane_of((8, 128))
    even = is_even("gz")

    def piece(got, t, right):
        start = jnp.where(right, 0, 120)
        tile = got[8 * (t // 16) : 8 * (t // 16) + 8, :]
        moved = pltpu.roll(tile, lax.rem(start + 128 - 8 * (t % 16), 128), 1)
        inside = jnp.logical_and(lane >= start, lane < start + 8)
        return jnp.where(inside, moved, 0.0)

    def rim(t):
        first = piece(got_z[0], t, even)
        if len(got_z) == 1:
            return first
        second = piece(got_z[1], t, jnp.logical_not(even))
        return first + jnp.where(inner("gz"), second, 0.0)

    return rim


M_PLANES = X // 2 + 4
EM_PLANES = X // 2 + 6
LOW_TILE = COMPS * (X // 2)
MZ_PACK = (LOW_TILE + 1) * 8


def fine_apply(s, es, c1, e, i):
    parts = []
    for c in range(COMPS):
        v = tri_y(tri_x(s[c, i - 1], s[c, i], s[c, i + 1]))
        ev = tri_y(tri_x(es[c, i - 1], es[c, i], es[c, i + 1]))
        parts.append(c1[i] * s[c, i] - mixed_z(e[0, i], e[1, i], e[2, i], v, ev))
    return coupled(parts)


def sweep(source, e_source, target, e_target, r, c1, e, w, first, last):
    def body(k, carry):
        for i in (first + 2 * k, first + 2 * k + 1):
            applied = fine_apply(source, e_source, c1, e, i)
            for c in range(COMPS):
                value = source[c, i] + w[i] * (r[c, i] - applied[c])
                target[c, i] = value
                e_target[c, i] = e[0, i] * value
        return carry

    lax.fori_loop(0, (last - first) // 2, body, 0)


def smooth_body(n_z, *refs):
    res, young, xa, xb, ya, yb = refs[:6]
    got_z = refs[6 : 6 + n_z]
    r, s1, e, c1, w, em, em_side, c1m, wm, pack = refs[6 + n_z : 16 + n_z]
    wide, wide_z, s0, es0, es1, rest, wide_x = refs[16 + n_z :]

    res_tiles, young_tiles = xy_planes(res, young, (xa, xb), (ya, yb), slice(None), Z)
    rim = z_rims(got_z)
    at = 0
    for c in range(COMPS):
        for i in range(PLANES):
            for t, tile in enumerate(res_tiles(c, i)):
                r[c, i, 8 * t : 8 * t + 8, :Z] = tile
                r[c, i, 8 * t : 8 * t + 8, Z:] = rim(at)
                at += 1
    for i in range(E_PLANES):
        for t, tile in enumerate(young_tiles(i)):
            wide[i, 8 * t : 8 * t + 8, :Z] = tile * 0.0125
            wide[i, 8 * t : 8 * t + 8, Z:] = rim(at) * 0.0125
            at += 1

    def shift(k, carry):
        for i in (2 * k, 2 * k + 1):
            centre = wide[i]
            after, before = pltpu.roll(centre, LANES - 1, 1), pltpu.roll(centre, 1, 1)
            wide_z[i] = after + before + (centre + centre)
            e[0, i] = centre[:ROWS]
            e[1, i] = after[:ROWS]
            e[2, i] = before[:ROWS]
        total = wide[2 * k] + wide[2 * k + 1]
        for t in range(LANES // 128):
            wide_x[t, pl.ds(24 * k, 24)] = total[:, 128 * t : 128 * t + 128]
        return carry

    lax.fori_loop(0, E_PLANES // 2, shift, 0, unroll=5)

    def prepare(k, carry):
        for i in (2 * k, 2 * k + 1):
            total = tri_x(wide_z[i + 1], wide_z[i + 2], wide_z[i + 3])
            side = total[ROWS:]
            below = jnp.concatenate([side, up(side, 3)], axis=0)
            above = jnp.concatenate([side, up(side, 1)], axis=0)
            total = tri_y_with(total[:ROWS], below, above, 11)
            centre = e[0, i + 2]
            c1[i] = 72.0 * centre + total
            inverse = jnp.where(centre > 0.0, DAMPING / (56.0 * centre + total), 0.0)
            w[i] = inverse
            for c in range(COMPS):
                value = inverse * r[c, i]
                s0[c, i] = value
                es0[c, i] = centre * value
        return carry

    lax.fori_loop(0, PLANES // 2, prepare, 0)
    e = e.at[:, 2 : 2 + PLANES]
    sweep(s0, es0, s1, es1, r, c1, e, w, 1, PLANES - 1)

    def residue(m, carry):
        first = fine_apply(s1, es1, c1, e, 2 * m + 2)
        second = fine_apply(s1, es1, c1, e, 2 * m + 3)
        for c in range(COMPS):
            total = (r[c, 2 * m + 2] - first[c]) + (r[c, 2 * m + 3] - second[c])
            for t in range(LANES // 128):
                rest[t, pl.ds((c * 6 + m) * ROWS, ROWS)] = total[:, 128 * t : 128 * t + 128]
        return carry

    lax.fori_loop(0, 6, residue, 0)

    wide_x[:, 24 * EM_PLANES :] = jnp.zeros((LANES // 128, 8, 128), F32)
    pieces = []
    for t in range(COMPS * 6):
        pieces.append(every_other(rest, 16 * t, 8) + every_other(rest, 16 * t + 1, 8))
    for m in range(EM_PLANES):
        for at in (24 * m, 24 * m + 16):
            pieces.append(every_other(wide_x, at, 8) + every_other(wide_x, at + 1, 8))
    pooled = dot_exact_weights(jnp.concatenate(pieces, axis=0), pool_matrix(0.5))
    pooled = [pooled[8 * t : 8 * t + 8] for t in range(len(pieces))]
    for m in range(EM_PLANES):
        centre = 0.25 * pooled[COMPS * 6 + 2 * m]
        em[0, m] = centre
        em[1, m] = pltpu.roll(centre, MID_LANES - 1, 1)
        em[2, m] = pltpu.roll(centre, 1, 1)
        em_side[m] = 0.25 * pooled[COMPS * 6 + 2 * m + 1]
    for m in range(M_PLANES):
        total = tri_x(*[em[0, m + k] for k in range(3)])
        side = tri_x(*[em_side[m + k] for k in range(3)])
        total = tri_y_with(total, up(side, 6), up(side, 4), 5)
        total = total + total + pltpu.roll(total, 1, 1) + pltpu.roll(total, MID_LANES - 1, 1)
        centre = em[0, m + 1]
        c1m[m] = 72.0 * centre + total
        wm[m] = jnp.where(centre > 0.0, DAMPING / (56.0 * centre + total), 0.0)

    rhs, mid, e_mid = {}, {}, {}
    for m in range(6):
        for c in range(COMPS):
            rhs[c, m] = pooled[c * 6 + m]
            mid[c, m] = wm[m + 1] * rhs[c, m]
            e_mid[c, m] = em[0, m + 2] * mid[c, m]
    rows = []
    kept = {}
    for m in range(1, 5):
        parts = []
        for c in range(COMPS):
            v = tri_y(tri_x(mid[c, m - 1], mid[c, m], mid[c, m + 1]))
            ev = tri_y(tri_x(e_mid[c, m - 1], e_mid[c, m], e_mid[c, m + 1]))
            mixed = mixed_z(em[0, m + 2], em[1, m + 2], em[2, m + 2], v, ev)
            parts.append(c1m[m + 1] * mid[c, m] - mixed)
        applied = coupled(parts)
        for c in range(COMPS):
            left_over = rhs[c, m] - applied[c]
            kept[c, m - 1] = left_over
            value = mid[c, m] + wm[m + 1] * left_over
            tile = c * 4 + m - 1
            pack[8 * tile : 8 * tile + 8] = value[:, :128]
    for c in range(COMPS):
        for b in range(2):
            rows.append(kept[c, 2 * b] + kept[c, 2 * b + 1])
    stacked = jnp.concatenate(rows, axis=0)
    lane_box = row_of((MID_LANES, 128))
    column = lane_of((MID_LANES, 128))
    boxes = jnp.where(
        jnp.logical_and(lane_box < Z // 2, lane_box // 64 == column % 2), 1.0, 0.0
    ).astype(F32)
    sums = dot_exact_weights(stacked, boxes)
    line = row_of((48, 128))
    entry = lane_of((48, 128))
    inside = line % 8
    match = jnp.logical_and((line // 8) * 2 + inside // 2 == entry // 2, inside < 4)
    scale = 1.0 / math.sqrt((X // 4) * (Y // 4) * (Z // 4))
    low = jnp.sum(jnp.where(match, sums, 0.0), axis=0, keepdims=True) * scale
    pack[8 * LOW_TILE :] = jnp.broadcast_to(low, (8, 128))


def pack_mid(pack, tiles):
    lane = lane_of((8, 128))
    rims = None
    for n, tile in enumerate(tiles):
        pack[8 * n : 8 * n + 8] = tile[:, :128]
        moved = pltpu.roll(tile[:, 128:], 4 + 8 * n, 1)
        rims = moved if n == 0 else jnp.where(lane < 8 * n, rims, moved)
    pack[8 * len(tiles) :] = rims


def unpack_mid(side, count):
    lane = lane_of((8, 128))
    near = jnp.logical_or(lane < 4, lane >= 124)
    rims = side((slice(8 * count, 8 * count + 8), slice(None)))
    tiles = []
    for n in range(count):
        main = side((slice(8 * n, 8 * n + 8), slice(None)))
        rim = jnp.where(near, pltpu.roll(rims, 124 - 8 * n, 1), 0.0)
        tiles.append(jnp.concatenate([main, rim], axis=1))
    return tiles


def coarse_body(n_z, *refs):
    pack = refs[0]
    got_z = refs[1 : 1 + n_z]
    matrix = refs[1 + n_z]
    gathered = refs[2 + n_z : -5]
    planes, column, pack_even, pack_odd, scratch = refs[-5:]
    place = lax.axis_index("gz")
    left, right = from_sides(got_z, "gz")
    lane = lane_of((8, 128))
    for t in range(LOW_TILE):
        key = (slice(8 * t, 8 * t + 8), slice(None))
        planes[t, :, :128] = pack[key]
        planes[t, :, 128:] = jnp.where(lane < 64, right(key), left(key))

    size = 24
    if gathered:
        rhs = gathered[0][...]
    else:
        mine = pack[8 * LOW_TILE : 8 * LOW_TILE + 8]
        other = got_z[0][8 * LOW_TILE : 8 * LOW_TILE + 8]
        first = jnp.where(place == 0, mine, other)
        second = jnp.where(place == 0, other, mine)
        rhs = jnp.where(lane < size, first, pltpu.roll(second, size, 1))[:1, : 2 * size]
    solved = jnp.sum(matrix[0, 0] * rhs, axis=1, keepdims=True)
    scratch[...] = jnp.zeros(scratch.shape, F32)
    scratch[size : size + solved.shape[0]] = jnp.broadcast_to(solved, (solved.shape[0], 128))
    base = pl.multiple_of(place * size, 8)
    wide = lane_of((16, MID_LANES))
    before, own_a, own_b, after = [
        jnp.concatenate([scratch[pl.ds(base + at, 16, stride=2)]] * 2, axis=1)
        for at in (1, size, size + 1, 2 * size)
    ]
    value = jnp.where(wide < 64, own_a, own_b)
    value = jnp.where(wide < 128, value, jnp.where(wide < 192, after, before))
    value = jnp.where(row_of((16, MID_LANES)) < 12, value, 0.0)
    column[...] = value

    even = is_even("gx")
    row = row_of((8, MID_LANES))
    low, high = [
        [jnp.where(row < 4, planes[c * 4 + p], up(planes[c * 4 + p + 1], 4)) for c in range(COMPS)]
        for p in (0, 2)
    ]
    rest = [value[:8], value[8:]]
    pack_mid(pack_even, [jnp.where(even, b, a) for a, b in zip(low, high)] + rest)
    pack_mid(pack_odd, [jnp.where(even, a, b) for a, b in zip(low, high)] + rest)


MX_TILES = COMPS + 2
MY_TILES = 2 * COMPS + 5
MX_PACK = (MX_TILES + 1) * 8
MY_PACK = (MY_TILES + 1) * 8


def mid_y_body(planes, column, got_a, got_b, wide_planes, columns, pack_even, pack_odd):
    lower, upper = from_sides((got_a, got_b), "gx")
    low_tiles, high_tiles = unpack_mid(lower, MX_TILES), unpack_mid(upper, MX_TILES)
    row = row_of((8, MID_LANES))
    even = is_even("gy")
    below_packs, above_packs = [], []
    for c in range(COMPS):
        tiles = [low_tiles[c], up(low_tiles[c], 4)]
        tiles += [planes[c * 4 + p] for p in range(4)]
        tiles += [high_tiles[c], up(high_tiles[c], 4)]
        for t in range(8):
            wide_planes[c * 8 + t] = tiles[t]
        for h in range(2):
            below = above = None
            for k in range(4):
                tile = tiles[4 * h + k]
                a, b = up(tile, 2 * k), up(tile, 2 * k - 2)
                below = a if k == 0 else jnp.where(row < 2 * k, below, a)
                above = b if k == 0 else jnp.where(row < 2 * k, above, b)
            below_packs.append(below)
            above_packs.append(above)
    columns[:8] = low_tiles[COMPS]
    columns[8:12] = low_tiles[COMPS + 1][:4]
    columns[12:24] = column[:12]
    columns[24:32] = high_tiles[COMPS]
    columns[32:36] = high_tiles[COMPS + 1][:4]
    columns[36:] = jnp.zeros((4, MID_LANES), F32)
    rest = [columns[8 * t : 8 * t + 8] for t in range(5)]
    pairs_of = list(zip(below_packs, above_packs))
    pack_mid(pack_even, [jnp.where(even, a, b) for b, a in pairs_of] + rest)
    pack_mid(pack_odd, [jnp.where(even, b, a) for b, a in pairs_of] + rest)


def finish_body(
    wide_planes, columns, got_a, got_b, r, s1, e_all, c1, w, em, em_side, c1m, wm, prev_d, prev_i,
    precond_out, operated_out, sums, cor, cor_side, mid, big, s2, es2, s3, es3, p, ep, precond,
    operated, sems,
):
    e = e_all.at[:, 2 : 2 + PLANES]
    lower, upper = from_sides((got_a, got_b), "gy")
    row = row_of((8, MID_LANES))

    low_tiles, high_tiles = unpack_mid(lower, MY_TILES), unpack_mid(upper, MY_TILES)
    below = jnp.concatenate(low_tiles[2 * COMPS :], axis=0)
    above = jnp.concatenate(high_tiles[2 * COMPS :], axis=0)
    middle = columns[...]
    for c in range(COMPS):
        for b in range(6):
            at = (b // 2) * 12 + c * 4 + (b % 2) * 2

            def band(source, by):
                return jnp.broadcast_to(source[at + by : at + by + 1], (8, MID_LANES))

            field = jnp.where(row < 6, band(above, 0), band(below, 1))
            field = jnp.where(row < 4, band(middle, 1), field)
            cor[c, b] = jnp.where(row < 2, band(middle, 0), field)
            cor_side[c, b] = jnp.where(row == 0, band(below, 0), band(above, 1))

    def box(m):
        return (m + 1) // 2

    for m in range(M_PLANES):
        parts = []
        for c in range(COMPS):
            near = [cor[c, box(m + k)] for k in range(3)]
            near_side = [cor_side[c, box(m + k)] for k in range(3)]
            e_near = [em[0, m + k] * near[k] for k in range(3)]
            e_side = [em_side[m + k] * near_side[k] for k in range(3)]
            side = tri_x(*near_side)
            v = tri_y_with(tri_x(*near), up(side, 6), up(side, 4), 5)
            side = tri_x(*e_side)
            ev = tri_y_with(tri_x(*e_near), up(side, 6), up(side, 4), 5)
            mixed = mixed_z(em[0, m + 1], em[1, m + 1], em[2, m + 1], v, ev)
            parts.append(c1m[m] * near[1] - mixed)
        applied = coupled(parts)
        for c in range(COMPS):
            tile = wide_planes[c * 8 + m]
            n, k = c * 2 + m // 4, m % 4
            outer = jnp.where(row < 6, up(high_tiles[n], 4 - 2 * k), up(low_tiles[n], 6 - 2 * k))
            tile = jnp.where(row < 4, tile, outer)
            at = (c * 8 + m) * 8
            mid[at : at + 8] = tile + cor[c, box(m + 1)] - wm[m] * applied[c]
    spread = dot_exact_weights(mid[...], spread_matrix())
    for t in range(COMPS * 8):
        piece = spread[8 * t : 8 * t + 8]
        for k in range(LANES // 128):
            tile = piece[:, 128 * k : 128 * k + 128]
            big[k, pl.ds(16 * t, 8, stride=2)] = tile
            big[k, pl.ds(16 * t + 1, 8, stride=2)] = tile

    def add_up(i, carry):
        for c in range(COMPS):
            at = pl.multiple_of((c * 8 + i // 2) * 16, 16)
            more = [big[k, pl.ds(at, 16)] for k in range(LANES // 128)]
            value = s1[c, i] + jnp.concatenate(more, axis=1)
            s2[c, i] = value
            es2[c, i] = e[0, i] * value
        return carry

    lax.fori_loop(1, PLANES - 1, add_up, 0)
    sweep(s2, es2, s3, es3, r, c1, e, w, 2, PLANES - 2)
    sweep(s3, es3, p, ep, r, c1, e, w, 3, PLANES - 3)

    leaving = (
        (precond, precond_out, sems.at[0]),
        (operated, operated_out, sems.at[1]),
    )

    def own(a):
        return a[:Y]

    def image_of(x):
        i = x + RIM
        near = [e[k, i, :Y] for k in range(3)]
        centre = c1[i, :Y]
        owned, parts = [], []
        for c in range(COMPS):
            owned.append(p[c, i, :Y])
            v = own(tri_y(tri_x(p[c, i - 1], p[c, i], p[c, i + 1])))
            ev = own(tri_y(tri_x(ep[c, i - 1], ep[c, i], ep[c, i + 1])))
            parts.append(centre * owned[c] - mixed_z(*near, v, ev))
        return owned, coupled(parts)

    def image(k, carry):
        rz, pp, mix, old = carry
        steps = [2 * k, 2 * k + 1]
        found = [image_of(x) for x in steps]
        for x, (owned, applied) in zip(steps, found):
            for c in range(COMPS):
                own_p, own_a = owned[c][:, :Z], applied[c][:, :Z]
                own_r = r[c, x + RIM, :Y, :Z]
                d, q = prev_d[c, x], prev_i[c, x]
                rz += own_r * own_p
                pp += own_p * own_a
                mix += own_p * q + d * own_a
                old += d * q
                precond[x, c] = own_p
                operated[x, c] = own_a
        part = pl.ds(2 * k, 2)
        for source, target, sem in leaving:
            pltpu.make_async_copy(source.at[part], target.at[part], sem).start()
        return rz, pp, mix, old

    zero = jnp.zeros((Y, Z), F32)
    found = lax.fori_loop(0, X // 2, image, (zero, zero, zero, zero))
    row = row_of((8, 128))
    total = jnp.zeros((8, 128), F32)
    for k, value in enumerate(found):
        line = jnp.sum(value[:, :128] + value[:, 128:], axis=0, keepdims=True)
        total = jnp.where(row == k, jnp.broadcast_to(line, (8, 128)), total)
    total = total + pltpu.roll(total, 64, 1)
    total = total + pltpu.roll(total, 32, 1)
    total = jnp.where(row == lane_of((8, 128)) // 32, total, 0.0)
    sums[...] = jnp.broadcast_to(jnp.sum(total, axis=0, keepdims=True), sums.shape)
    for source, target, sem in leaving:
        pltpu.make_async_copy(source, target, sem).wait()


STEP = 2


def last_body(
    prev_rz, sums, precond_in, operated_in, prev_d, prev_i, sol, res,
    new_s_out, new_r_out, new_d_out, new_i_out, precond, operated, news, in_sems, out_sems,
):
    arriving = []
    for x in range(0, X, STEP):
        part = pl.ds(x, STEP)
        pair = [
            pltpu.make_async_copy(source.at[part], target.at[part], in_sems.at[k, x // STEP])
            for k, (source, target) in enumerate(((precond_in, precond), (operated_in, operated)))
        ]
        for copy in pair:
            copy.start()
        arriving.append(pair)
    total = jnp.sum(sums[...], axis=0, keepdims=True)
    lane = lane_of((1, 128))

    def entry(k):
        return jnp.sum(jnp.where(lane // 32 == k, total, 0.0), axis=1, keepdims=True)

    rz = entry(0)
    beta = rz / prev_rz[0]
    alpha = rz / (entry(1) + beta * (entry(2) + beta * entry(3)))
    beta = jnp.broadcast_to(beta, (Y, Z))
    alpha = jnp.broadcast_to(alpha, (Y, Z))
    leaving = []
    for step, pair in enumerate(arriving):
        for copy in pair:
            copy.wait()
        for x in range(step * STEP, step * STEP + STEP):
            for c in range(COMPS):
                d = precond[x, c] + beta * prev_d[c, x]
                q = operated[x, c] + beta * prev_i[c, x]
                news[2, c, x] = d
                news[3, c, x] = q
                news[0, c, x] = sol[c, x] + alpha * d
                news[1, c, x] = res[c, x] - alpha * q
        part = pl.ds(step * STEP, STEP)
        for k, target in enumerate((new_s_out, new_r_out, new_d_out, new_i_out)):
            copy = pltpu.make_async_copy(
                news.at[k, :, part], target.at[:, part], out_sems.at[k, step]
            )
            copy.start()
            leaving.append(copy)
    for copy in leaving:
        copy.wait()


PLANES = X + 2 * RIM
FIELD = (COMPS, PLANES, ROWS, LANES)
COLS_SHAPE = (40, MID_LANES)


def smooth_outs():
    return [
        shape(*FIELD),
        shape(*FIELD),
        shape(3, E_PLANES, ROWS, LANES),
        shape(PLANES, ROWS, LANES),
        shape(PLANES, ROWS, LANES),
        shape(3, EM_PLANES, 8, MID_LANES),
        shape(EM_PLANES, 8, MID_LANES),
        shape(M_PLANES, 8, MID_LANES),
        shape(M_PLANES, 8, MID_LANES),
        shape(MZ_PACK, 128),
    ]


def smooth_call(n_z):
    return call(
        functools.partial(smooth_body, n_z),
        smooth_outs(),
        scratch=[
            pltpu.VMEM((E_PLANES, 24, LANES), F32),
            pltpu.VMEM((E_PLANES, 24, LANES), F32),
            pltpu.VMEM(FIELD, F32),
            pltpu.VMEM(FIELD, F32),
            pltpu.VMEM(FIELD, F32),
            pltpu.VMEM((LANES // 128, 18 * ROWS, 128), F32),
            pltpu.VMEM((LANES // 128, 24 * EM_PLANES + 8, 128), F32),
        ],
        n_in=6 + n_z,
        vmem=30 << 20,
    )


def finish_call(n_all):
    return call(
        finish_body,
        [shape(X, COMPS, Y, Z), shape(X, COMPS, Y, Z), shape(n_all, 128)],
        scratch=[
            pltpu.VMEM((COMPS, 6, 8, MID_LANES), F32),
            pltpu.VMEM((COMPS, 6, 8, MID_LANES), F32),
            pltpu.VMEM((COMPS * 64, MID_LANES), F32),
            pltpu.VMEM((LANES // 128, COMPS * 128, 128), F32),
        ]
        + [pltpu.VMEM(FIELD, F32)] * 6
        + [pltpu.VMEM((X, COMPS, Y, Z), F32)] * 2
        + [pltpu.SemaphoreType.DMA((2,))],
        n_in=15,
        hbm_out=(0, 1),
        vmem=30 << 20,
    )


def on_device(
    solution,
    residual,
    prev_direction,
    prev_image,
    prev_rz,
    density_index,
    stiffness_table,
    coarse_inverse,
):
    if residual.shape != (COMPS, X, Y, Z):
        raise ValueError(residual.shape)
    block = shape(COMPS, X, Y, Z)
    n_z = 1 if lax.axis_size("gz") == 2 else 2
    n_all = lax.axis_size(ALL)

    res, young, px, qx = call(
        pack_x_body,
        [block, shape(X, Y, Z), shape(X_PACK, Y, Z), shape(X_PACK, Y, Z)],
        n_in=3,
        smem=(0,),
    )(stiffness_table, density_index, residual)
    got_x = swap("gx", px, qx)
    py, qy = call(pack_y_body, [shape(Y_PACK, Y, Z)] * 2, n_in=4)(res, young, *got_x)
    got_y = swap("gy", py, qy, closed=False)
    packs = call(pack_z_body, [shape(Z_PACK, 128)] * n_z, n_in=6)(res, young, *got_x, *got_y)
    got_z = swap("gz", packs[0], packs[-1])

    r, s1, e, c1, w, em, em_side, c1m, wm, pack = smooth_call(n_z)(res, young, *got_x, *got_y, *got_z)

    got_z = swap("gz", pack, pack)
    gathered = []
    if n_z > 1:
        gathered = [lax.all_gather(pack[8 * LOW_TILE, :24], "gz", axis=0, tiled=True)[None]]
    size = coarse_inverse.shape[-1]
    mid_planes, column, px, qx = call(
        functools.partial(coarse_body, n_z),
        [
            shape(LOW_TILE, 8, MID_LANES),
            shape(16, MID_LANES),
            shape(MX_PACK, 128),
            shape(MX_PACK, 128),
        ],
        scratch=[pltpu.VMEM((size + 64, 128), F32)],
        n_in=2 + n_z + len(gathered),
    )(pack, *got_z, coarse_inverse, *gathered)
    got_x = swap("gx", px, qx)
    mid_planes, columns, py, qy = call(
        mid_y_body,
        [
            shape(COMPS * 8, 8, MID_LANES),
            shape(40, MID_LANES),
            shape(MY_PACK, 128),
            shape(MY_PACK, 128),
        ],
        n_in=4,
    )(mid_planes, column, *got_x)
    got_y = swap("gy", py, qy)
    precond, operated, sums = finish_call(n_all)(
        mid_planes, columns, *got_y, r, s1, e, c1, w, em, em_side, c1m, wm, prev_direction, prev_image
    )
    sums = lax.all_to_all(sums, ALL, 0, 0, tiled=True)
    return tuple(
        call(
            last_body,
            [block] * 4,
            scratch=[pltpu.VMEM((X, COMPS, Y, Z), F32)] * 2
            + [pltpu.VMEM((4, COMPS, X, Y, Z), F32)]
            + [pltpu.SemaphoreType.DMA((2, X // STEP)), pltpu.SemaphoreType.DMA((4, X // STEP))],
            n_in=8,
            smem=(0,),
            hbm=(2, 3),
            hbm_out=(0, 1, 2, 3),
        )(
            prev_rz.reshape(1), sums, precond, operated, prev_direction, prev_image, solution, residual
        )
    )


def solution(mesh):
    field = P(None, "gx", "gy", "gz")
    return jax.shard_map(
        on_device,
        mesh=mesh,
        in_specs=(
            field,
            field,
            field,
            field,
            P(),
            P("gx", "gy", "gz"),
            P(),
            P("gx", "gy", None, None),
        ),
        out_specs=(field, field, field, field),
        check_vma=False,
    )
```

```python
import functools
import math

import jax
import jax.numpy as jnp
from jax import lax
from jax.experimental import pallas as pl
from jax.experimental.pallas import tpu as pltpu
from jax.sharding import PartitionSpec as P

X, Y, Z = 8, 8, 256
COMPS = 3
RIM = 4
WIDE = 6
ROWS = Y + 2 * RIM
LANES = Z + 128
MID_LANES = Z // 2 + 128
DAMPING = 0.6
ALL = ("gx", "gy", "gz")
F32 = jnp.float32
VMEM = pl.BlockSpec(memory_space=pltpu.VMEM)
SMEM = pl.BlockSpec(memory_space=pltpu.SMEM)
HBM = pl.BlockSpec(memory_space=pltpu.HBM)


def shape(*dims):
    return jax.ShapeDtypeStruct(dims, F32)


def call(body, outs, scratch=(), n_in=0, smem=(), hbm=(), hbm_out=(), vmem=16 << 20):
    return pl.pallas_call(
        body,
        out_shape=outs,
        in_specs=[SMEM if i in smem else HBM if i in hbm else VMEM for i in range(n_in)],
        out_specs=[HBM if i in hbm_out else VMEM for i in range(len(outs))],
        scratch_shapes=list(scratch),
        compiler_params=pltpu.CompilerParams(vmem_limit_bytes=vmem),
    )


def in_hbm(a):
    return pltpu.with_memory_space_constraint(a, pltpu.HBM)


def in_vmem(a):
    return pltpu.with_memory_space_constraint(a, pltpu.VMEM)


def pairs(count, odd, closed):
    if not odd:
        return [(i, i ^ 1) for i in range(count)]
    made = [(i, (i + 1) % count if i % 2 else (i - 1) % count) for i in range(count)]
    return made if closed else made[1:-1]


def swap(axis, even_pack, odd_pack, closed=True):
    count = lax.axis_size(axis)
    got_even = lax.ppermute(even_pack, axis, pairs(count, False, closed))
    if count == 2:
        return [got_even]
    return [got_even, lax.ppermute(odd_pack, axis, pairs(count, True, closed))]


def is_even(axis):
    return lax.rem(lax.axis_index(axis), 2) == 0


def inner(axis):
    index = lax.axis_index(axis)
    return jnp.logical_and(index > 0, index < lax.axis_size(axis) - 1)


def from_sides(got, axis):
    even = is_even(axis)
    if len(got) == 1:

        def lower(key):
            value = got[0][key]
            return jnp.where(even, 0.0, value)

        def upper(key):
            value = got[0][key]
            return jnp.where(even, value, 0.0)

        return lower, upper
    ok = inner(axis)

    def lower(key):
        return jnp.where(even, jnp.where(ok, got[1][key], 0.0), got[0][key])

    def upper(key):
        return jnp.where(even, got[0][key], jnp.where(ok, got[1][key], 0.0))

    return lower, upper


def tri_y(a):
    a = a + pltpu.roll(a, 1, 0)
    return a + pltpu.roll(a, a.shape[0] - 1, 0)


def tri_y_with(a, below, above, last):
    rows = a.shape[0]
    row = row_of(a.shape)
    former = jnp.where(row == last + 1, below, pltpu.roll(a, 1, 0))
    after = jnp.where(row == last, above, pltpu.roll(a, rows - 1, 0))
    return former + after + (a + a)


def mixed_z(e, e_next, e_last, v, ev):
    both = e * v + ev
    moved = pltpu.roll(e_next * v + ev, 1, 1) + pltpu.roll(e_last * v + ev, v.shape[1] - 1, 1)
    return moved + (both + both)


def tri_x(before, centre, after):
    return before + after + (centre + centre)


def tree_sum(terms):
    while len(terms) > 1:
        terms = [sum(terms[k : k + 2]) for k in range(0, len(terms), 2)]
    return terms[0]


def coupled(parts):
    total = 0.3 * (parts[0] + parts[1] + parts[2])
    return [0.7 * part + total for part in parts]


def row_of(shape):
    return lax.broadcasted_iota(jnp.int32, shape, 0)


def lane_of(shape):
    return lax.broadcasted_iota(jnp.int32, shape, 1)


def up(a, shift):
    shift %= a.shape[0]
    return pltpu.roll(a, shift, 0) if shift else a


def pool_matrix(value):
    lane = row_of((LANES, MID_LANES))
    mid = jnp.where(lane < Z + 64, lane // 2, lane // 2 + 64)
    return jnp.where(mid == lane_of((LANES, MID_LANES)), value, 0.0).astype(F32)


def spread_matrix():
    lane = lane_of((MID_LANES, LANES))
    mid = jnp.where(lane < Z + 64, lane // 2, lane // 2 + 64)
    return jnp.where(mid == row_of((MID_LANES, LANES)), 1.0, 0.0).astype(F32)


def every_other(ref, at, size):
    return jnp.concatenate(
        [ref[k, pl.ds(at, size, stride=2)] for k in range(ref.shape[0])], axis=1
    )


def dot_exact_weights(a, b):
    b = b.astype(jnp.bfloat16)
    total = None
    for k in range(3):
        part = a.astype(jnp.bfloat16)
        found = jnp.dot(part, b, preferred_element_type=F32)
        total = found if total is None else total + found
        if k < 2:
            a = a - part.astype(F32)
    return total


X_PACK = COMPS * RIM + WIDE
R_TILES = COMPS * X
E_PLANES = X + 2 * WIDE
E4_TILES = E_PLANES // 2
E2_TILES = E_PLANES // 4
Y_PACK = R_TILES + E4_TILES + E2_TILES
Z_TILES = COMPS * (X + 2 * RIM) * (ROWS // 8) + E_PLANES * 3
Z_PACK = -(-Z_TILES // 16) * 8


def pack_x_body(table_in, index_in, res_in, res, young, pack_even, pack_odd, table, index, sems):
    copies = [
        pltpu.make_async_copy(source, target, sems.at[k])
        for k, (source, target) in enumerate(((table_in, table), (index_in, index), (res_in, res)))
    ]
    for copy in copies:
        copy.start()
    copies[0].wait()
    copies[1].wait()
    levels = index[...]
    value = jnp.zeros(levels.shape, F32)
    for level in range(table.shape[0]):
        value = jnp.where(levels == level, table[level], value)
    young[...] = value
    copies[2].wait()
    high_first = jnp.where(is_even("gx"), 1, 0)
    for pack, high in ((pack_even, high_first), (pack_odd, 1 - high_first)):
        for c in range(COMPS):
            pack[c * RIM : (c + 1) * RIM] = res[c, pl.ds(high * (X - RIM), RIM)]
        pack[COMPS * RIM :] = young[pl.ds(high * (X - WIDE), WIDE)]


def x_planes(res, young, got_x, lanes=slice(None)):
    lower, upper = from_sides(got_x, "gx")
    whole = slice(None)

    def res_plane(c, i):
        if i < RIM:
            return lower((c * RIM + i, whole, lanes))
        if i < RIM + X:
            return res[c, i - RIM, :, lanes]
        return upper((c * RIM + i - RIM - X, whole, lanes))

    def young_plane(i):
        if i < WIDE:
            return lower((COMPS * RIM + i, whole, lanes))
        if i < WIDE + X:
            return young[i - WIDE, :, lanes]
        return upper((COMPS * RIM + i - WIDE - X, whole, lanes))

    return res_plane, young_plane


def pack_y_body(res, young, got_a, got_b, pack_even, pack_odd):
    res_plane, young_plane = x_planes(res, young, (got_a, got_b))
    row = row_of((Y, Z))
    even = is_even("gy")

    def put(tile, low, high):
        pack_even[tile] = jnp.where(even, high, low)
        pack_odd[tile] = jnp.where(even, low, high)

    def halves(tile, a, b):
        put(
            tile,
            jnp.where(row < 4, a, up(b, 4)),
            jnp.where(row < 4, up(a, 4), b),
        )

    for c in range(COMPS):
        for i in range(X):
            halves(c * X + i, res_plane(c, i), res_plane(c, i + X))
    planes = [young_plane(i) for i in range(E_PLANES)]
    for i in range(E4_TILES):
        halves(R_TILES + i, planes[i], planes[i + E4_TILES])
    for j in range(E2_TILES):
        low = high = None
        for k in range(4):
            plane = planes[4 * j + k]
            a, b = up(plane, 2 * k - 4), up(plane, 2 * k - 2)
            low = a if k == 0 else jnp.where(row < 2 * k, low, a)
            high = b if k == 0 else jnp.where(row < 2 * k, high, b)
        put(R_TILES + E4_TILES + j, low, high)


def xy_planes(res, young, got_x, got_y, lanes, width):
    res_plane, young_plane = x_planes(res, young, got_x, lanes)
    lower, upper = from_sides(got_y, "gy")
    row = row_of((Y, width))
    whole = slice(None)

    def rim_tile(tile, second):
        key = (tile, whole, lanes)
        low, high = lower(key), upper(key)
        if second:
            high = up(high, 4)
        else:
            low = up(low, 4)
        return jnp.where(row < 4, high, low)

    def res_tiles(c, i):
        return [res_plane(c, i), rim_tile(c * X + i % X, i >= X)]

    def young_tiles(i):
        two = (R_TILES + E4_TILES + i // 4, whole, lanes)
        k = i % 4
        low2, high2 = up(lower(two), -2 * k), up(upper(two), 2 - 2 * k)
        side = jnp.where(row < 2, low2, jnp.where(row < 4, high2, 0.0))
        return [young_plane(i), rim_tile(R_TILES + i % E4_TILES, i >= E4_TILES), side]

    return res_tiles, young_tiles


def pack_z_body(res, young, xa, xb, ya, yb, *packs):
    high_first = jnp.where(is_even("gz"), 1, 0)
    lane = lane_of((8, 128))
    for pack, high in zip(packs, (high_first, 1 - high_first)):
        lanes = pl.ds(pl.multiple_of(high * (Z - 128), 128), 128)
        res_tiles, young_tiles = xy_planes(res, young, (xa, xb), (ya, yb), lanes, 128)
        tiles = [t for c in range(COMPS) for i in range(X + 2 * RIM) for t in res_tiles(c, i)]
        tiles += [t for i in range(E_PLANES) for t in young_tiles(i)]
        for first in range(0, len(tiles), 16):
            packed = None
            for j, tile in enumerate(tiles[first : first + 16]):
                moved = pltpu.roll(tile, lax.rem(8 * j + 8 * high, 128), 1)
                packed = moved if j == 0 else jnp.where(lane < 8 * j, packed, moved)
            pack[first // 2 : first // 2 + 8] = packed


def z_rims(got_z):
    lane = lane_of((8, 128))
    even = is_even("gz")

    def piece(got, t, right):
        start = jnp.where(right, 0, 120)
        tile = got[8 * (t // 16) : 8 * (t // 16) + 8, :]
        moved = pltpu.roll(tile, lax.rem(start + 128 - 8 * (t % 16), 128), 1)
        inside = jnp.logical_and(lane >= start, lane < start + 8)
        return jnp.where(inside, moved, 0.0)

    def rim(t):
        first = piece(got_z[0], t, even)
        if len(got_z) == 1:
            return first
        second = piece(got_z[1], t, jnp.logical_not(even))
        return first + jnp.where(inner("gz"), second, 0.0)

    return rim


M_PLANES = X // 2 + 4
EM_PLANES = X // 2 + 6
LOW_TILE = COMPS * (X // 2)
MZ_PACK = (LOW_TILE + 1) * 8


def fine_apply(s, es, c1, e, i):
    parts = []
    for c in range(COMPS):
        v = tri_y(tri_x(s[c, i - 1], s[c, i], s[c, i + 1]))
        ev = tri_y(tri_x(es[c, i - 1], es[c, i], es[c, i + 1]))
        parts.append(c1[i] * s[c, i] - mixed_z(e[0, i], e[1, i], e[2, i], v, ev))
    return coupled(parts)


def sweep(source, e_source, target, e_target, r, c1, e, w, first, last):
    def body(k, carry):
        for i in (first + 2 * k, first + 2 * k + 1):
            applied = fine_apply(source, e_source, c1, e, i)
            for c in range(COMPS):
                value = source[c, i] + w[i] * (r[c, i] - applied[c])
                target[c, i] = value
                e_target[c, i] = e[0, i] * value
        return carry

    lax.fori_loop(0, (last - first) // 2, body, 0)


def smooth_body(n_z, *refs):
    res, young, xa, xb, ya, yb = refs[:6]
    got_z = refs[6 : 6 + n_z]
    r, s1, e, c1, w, em, em_side, c1m, wm, pack = refs[6 + n_z : 16 + n_z]
    wide, wide_z, s0, es0, es1, rest, wide_x = refs[16 + n_z :]

    res_tiles, young_tiles = xy_planes(res, young, (xa, xb), (ya, yb), slice(None), Z)
    rim = z_rims(got_z)
    at = 0
    for c in range(COMPS):
        for i in range(PLANES):
            for t, tile in enumerate(res_tiles(c, i)):
                r[c, i, 8 * t : 8 * t + 8, :Z] = tile
                r[c, i, 8 * t : 8 * t + 8, Z:] = rim(at)
                at += 1
    for i in range(E_PLANES):
        for t, tile in enumerate(young_tiles(i)):
            wide[i, 8 * t : 8 * t + 8, :Z] = tile * 0.0125
            wide[i, 8 * t : 8 * t + 8, Z:] = rim(at) * 0.0125
            at += 1

    def shift(k, carry):
        for i in (2 * k, 2 * k + 1):
            centre = wide[i]
            after, before = pltpu.roll(centre, LANES - 1, 1), pltpu.roll(centre, 1, 1)
            wide_z[i] = after + before + (centre + centre)
            e[0, i] = centre[:ROWS]
            e[1, i] = after[:ROWS]
            e[2, i] = before[:ROWS]
        total = wide[2 * k] + wide[2 * k + 1]
        for t in range(LANES // 128):
            wide_x[t, pl.ds(24 * k, 24)] = total[:, 128 * t : 128 * t + 128]
        return carry

    lax.fori_loop(0, E_PLANES // 2, shift, 0, unroll=5)

    def prepare(k, carry):
        for i in (2 * k, 2 * k + 1):
            total = tri_x(wide_z[i + 1], wide_z[i + 2], wide_z[i + 3])
            side = total[ROWS:]
            below = jnp.concatenate([side, up(side, 3)], axis=0)
            above = jnp.concatenate([side, up(side, 1)], axis=0)
            total = tri_y_with(total[:ROWS], below, above, 11)
            centre = e[0, i + 2]
            c1[i] = 72.0 * centre + total
            inverse = jnp.where(centre > 0.0, DAMPING / (56.0 * centre + total), 0.0)
            w[i] = inverse
            for c in range(COMPS):
                value = inverse * r[c, i]
                s0[c, i] = value
                es0[c, i] = centre * value
        return carry

    lax.fori_loop(0, PLANES // 2, prepare, 0)
    e = e.at[:, 2 : 2 + PLANES]
    sweep(s0, es0, s1, es1, r, c1, e, w, 1, PLANES - 1)

    def residue(m, carry):
        first = fine_apply(s1, es1, c1, e, 2 * m + 2)
        second = fine_apply(s1, es1, c1, e, 2 * m + 3)
        for c in range(COMPS):
            total = (r[c, 2 * m + 2] - first[c]) + (r[c, 2 * m + 3] - second[c])
            for t in range(LANES // 128):
                rest[t, pl.ds((c * 6 + m) * ROWS, ROWS)] = total[:, 128 * t : 128 * t + 128]
        return carry

    lax.fori_loop(0, 6, residue, 0)

    wide_x[:, 24 * EM_PLANES :] = jnp.zeros((LANES // 128, 8, 128), F32)
    pieces = []
    for t in range(COMPS * 6):
        pieces.append(every_other(rest, 16 * t, 8) + every_other(rest, 16 * t + 1, 8))
    for m in range(EM_PLANES):
        for at in (24 * m, 24 * m + 16):
            pieces.append(every_other(wide_x, at, 8) + every_other(wide_x, at + 1, 8))
    pooled = dot_exact_weights(jnp.concatenate(pieces, axis=0), pool_matrix(0.5))
    pooled = [pooled[8 * t : 8 * t + 8] for t in range(len(pieces))]
    for m in range(EM_PLANES):
        centre = 0.25 * pooled[COMPS * 6 + 2 * m]
        em[0, m] = centre
        em[1, m] = pltpu.roll(centre, MID_LANES - 1, 1)
        em[2, m] = pltpu.roll(centre, 1, 1)
        em_side[m] = 0.25 * pooled[COMPS * 6 + 2 * m + 1]
    for m in range(M_PLANES):
        total = tri_x(*[em[0, m + k] for k in range(3)])
        side = tri_x(*[em_side[m + k] for k in range(3)])
        total = tri_y_with(total, up(side, 6), up(side, 4), 5)
        total = total + total + pltpu.roll(total, 1, 1) + pltpu.roll(total, MID_LANES - 1, 1)
        centre = em[0, m + 1]
        c1m[m] = 72.0 * centre + total
        wm[m] = jnp.where(centre > 0.0, DAMPING / (56.0 * centre + total), 0.0)

    rhs, mid, e_mid = {}, {}, {}
    for m in range(6):
        for c in range(COMPS):
            rhs[c, m] = pooled[c * 6 + m]
            mid[c, m] = wm[m + 1] * rhs[c, m]
            e_mid[c, m] = em[0, m + 2] * mid[c, m]
    rows = []
    kept = {}
    for m in range(1, 5):
        parts = []
        for c in range(COMPS):
            v = tri_y(tri_x(mid[c, m - 1], mid[c, m], mid[c, m + 1]))
            ev = tri_y(tri_x(e_mid[c, m - 1], e_mid[c, m], e_mid[c, m + 1]))
            mixed = mixed_z(em[0, m + 2], em[1, m + 2], em[2, m + 2], v, ev)
            parts.append(c1m[m + 1] * mid[c, m] - mixed)
        applied = coupled(parts)
        for c in range(COMPS):
            left_over = rhs[c, m] - applied[c]
            kept[c, m - 1] = left_over
            value = mid[c, m] + wm[m + 1] * left_over
            tile = c * 4 + m - 1
            pack[8 * tile : 8 * tile + 8] = value[:, :128]
    for c in range(COMPS):
        for b in range(2):
            rows.append(kept[c, 2 * b] + kept[c, 2 * b + 1])
    stacked = jnp.concatenate(rows, axis=0)
    lane_box = row_of((MID_LANES, 128))
    column = lane_of((MID_LANES, 128))
    boxes = jnp.where(
        jnp.logical_and(lane_box < Z // 2, lane_box // 64 == column % 2), 1.0, 0.0
    ).astype(F32)
    sums = dot_exact_weights(stacked, boxes)
    line = row_of((48, 128))
    entry = lane_of((48, 128))
    inside = line % 8
    match = jnp.logical_and((line // 8) * 2 + inside // 2 == entry // 2, inside < 4)
    scale = 1.0 / math.sqrt((X // 4) * (Y // 4) * (Z // 4))
    low = jnp.sum(jnp.where(match, sums, 0.0), axis=0, keepdims=True) * scale
    pack[8 * LOW_TILE :] = jnp.broadcast_to(low, (8, 128))


def pack_mid(pack, tiles):
    lane = lane_of((8, 128))
    rims = None
    for n, tile in enumerate(tiles):
        pack[8 * n : 8 * n + 8] = tile[:, :128]
        moved = pltpu.roll(tile[:, 128:], 4 + 8 * n, 1)
        rims = moved if n == 0 else jnp.where(lane < 8 * n, rims, moved)
    pack[8 * len(tiles) :] = rims


def unpack_mid(side, count):
    lane = lane_of((8, 128))
    near = jnp.logical_or(lane < 4, lane >= 124)
    rims = side((slice(8 * count, 8 * count + 8), slice(None)))
    tiles = []
    for n in range(count):
        main = side((slice(8 * n, 8 * n + 8), slice(None)))
        rim = jnp.where(near, pltpu.roll(rims, 124 - 8 * n, 1), 0.0)
        tiles.append(jnp.concatenate([main, rim], axis=1))
    return tiles


def coarse_body(n_z, *refs):
    pack = refs[0]
    got_z = refs[1 : 1 + n_z]
    matrix = refs[1 + n_z]
    gathered = refs[2 + n_z : -5]
    planes, column, pack_even, pack_odd, scratch = refs[-5:]
    place = lax.axis_index("gz")
    left, right = from_sides(got_z, "gz")
    lane = lane_of((8, 128))
    for t in range(LOW_TILE):
        key = (slice(8 * t, 8 * t + 8), slice(None))
        planes[t, :, :128] = pack[key]
        planes[t, :, 128:] = jnp.where(lane < 64, right(key), left(key))

    size = 24
    if gathered:
        rhs = gathered[0][...]
    else:
        mine = pack[8 * LOW_TILE : 8 * LOW_TILE + 8]
        other = got_z[0][8 * LOW_TILE : 8 * LOW_TILE + 8]
        first = jnp.where(place == 0, mine, other)
        second = jnp.where(place == 0, other, mine)
        rhs = jnp.where(lane < size, first, pltpu.roll(second, size, 1))[:1, : 2 * size]
    solved = jnp.sum(matrix[0, 0] * rhs, axis=1, keepdims=True)
    scratch[...] = jnp.zeros(scratch.shape, F32)
    scratch[size : size + solved.shape[0]] = jnp.broadcast_to(solved, (solved.shape[0], 128))
    base = pl.multiple_of(place * size, 8)
    wide = lane_of((16, MID_LANES))
    before, own_a, own_b, after = [
        jnp.concatenate([scratch[pl.ds(base + at, 16, stride=2)]] * 2, axis=1)
        for at in (1, size, size + 1, 2 * size)
    ]
    value = jnp.where(wide < 64, own_a, own_b)
    value = jnp.where(wide < 128, value, jnp.where(wide < 192, after, before))
    value = jnp.where(row_of((16, MID_LANES)) < 12, value, 0.0)
    column[...] = value

    even = is_even("gx")
    row = row_of((8, MID_LANES))
    low, high = [
        [jnp.where(row < 4, planes[c * 4 + p], up(planes[c * 4 + p + 1], 4)) for c in range(COMPS)]
        for p in (0, 2)
    ]
    rest = [value[:8], value[8:]]
    pack_mid(pack_even, [jnp.where(even, b, a) for a, b in zip(low, high)] + rest)
    pack_mid(pack_odd, [jnp.where(even, a, b) for a, b in zip(low, high)] + rest)


MX_TILES = COMPS + 2
MY_TILES = 2 * COMPS + 5
MX_PACK = (MX_TILES + 1) * 8
MY_PACK = (MY_TILES + 1) * 8


def mid_y_body(planes, column, got_a, got_b, wide_planes, columns, pack_even, pack_odd):
    lower, upper = from_sides((got_a, got_b), "gx")
    low_tiles, high_tiles = unpack_mid(lower, MX_TILES), unpack_mid(upper, MX_TILES)
    row = row_of((8, MID_LANES))
    even = is_even("gy")
    below_packs, above_packs = [], []
    for c in range(COMPS):
        tiles = [low_tiles[c], up(low_tiles[c], 4)]
        tiles += [planes[c * 4 + p] for p in range(4)]
        tiles += [high_tiles[c], up(high_tiles[c], 4)]
        for t in range(8):
            wide_planes[c * 8 + t] = tiles[t]
        for h in range(2):
            below = above = None
            for k in range(4):
                tile = tiles[4 * h + k]
                a, b = up(tile, 2 * k), up(tile, 2 * k - 2)
                below = a if k == 0 else jnp.where(row < 2 * k, below, a)
                above = b if k == 0 else jnp.where(row < 2 * k, above, b)
            below_packs.append(below)
            above_packs.append(above)
    columns[:8] = low_tiles[COMPS]
    columns[8:12] = low_tiles[COMPS + 1][:4]
    columns[12:24] = column[:12]
    columns[24:32] = high_tiles[COMPS]
    columns[32:36] = high_tiles[COMPS + 1][:4]
    columns[36:] = jnp.zeros((4, MID_LANES), F32)
    rest = [columns[8 * t : 8 * t + 8] for t in range(5)]
    pairs_of = list(zip(below_packs, above_packs))
    pack_mid(pack_even, [jnp.where(even, a, b) for b, a in pairs_of] + rest)
    pack_mid(pack_odd, [jnp.where(even, b, a) for b, a in pairs_of] + rest)


def finish_body(
    wide_planes, columns, got_a, got_b, r, s1, e_all, c1, w, em, em_side, c1m, wm, prev_d, prev_i,
    precond, operated, sums, cor, cor_side, mid, big, s2, es2, s3, es3, p, ep,
):
    e = e_all.at[:, 2 : 2 + PLANES]
    lower, upper = from_sides((got_a, got_b), "gy")
    row = row_of((8, MID_LANES))

    low_tiles, high_tiles = unpack_mid(lower, MY_TILES), unpack_mid(upper, MY_TILES)
    below = jnp.concatenate(low_tiles[2 * COMPS :], axis=0)
    above = jnp.concatenate(high_tiles[2 * COMPS :], axis=0)
    middle = columns[...]
    for c in range(COMPS):
        for b in range(6):
            at = (b // 2) * 12 + c * 4 + (b % 2) * 2

            def band(source, by):
                return jnp.broadcast_to(source[at + by : at + by + 1], (8, MID_LANES))

            field = jnp.where(row < 6, band(above, 0), band(below, 1))
            field = jnp.where(row < 4, band(middle, 1), field)
            cor[c, b] = jnp.where(row < 2, band(middle, 0), field)
            cor_side[c, b] = jnp.where(row == 0, band(below, 0), band(above, 1))

    def box(m):
        return (m + 1) // 2

    for m in range(M_PLANES):
        parts = []
        for c in range(COMPS):
            near = [cor[c, box(m + k)] for k in range(3)]
            near_side = [cor_side[c, box(m + k)] for k in range(3)]
            e_near = [em[0, m + k] * near[k] for k in range(3)]
            e_side = [em_side[m + k] * near_side[k] for k in range(3)]
            side = tri_x(*near_side)
            v = tri_y_with(tri_x(*near), up(side, 6), up(side, 4), 5)
            side = tri_x(*e_side)
            ev = tri_y_with(tri_x(*e_near), up(side, 6), up(side, 4), 5)
            mixed = mixed_z(em[0, m + 1], em[1, m + 1], em[2, m + 1], v, ev)
            parts.append(c1m[m] * near[1] - mixed)
        applied = coupled(parts)
        for c in range(COMPS):
            tile = wide_planes[c * 8 + m]
            n, k = c * 2 + m // 4, m % 4
            outer = jnp.where(row < 6, up(high_tiles[n], 4 - 2 * k), up(low_tiles[n], 6 - 2 * k))
            tile = jnp.where(row < 4, tile, outer)
            at = (c * 8 + m) * 8
            mid[at : at + 8] = tile + cor[c, box(m + 1)] - wm[m] * applied[c]
    spread = dot_exact_weights(mid[...], spread_matrix())
    for t in range(COMPS * 8):
        piece = spread[8 * t : 8 * t + 8]
        for k in range(LANES // 128):
            tile = piece[:, 128 * k : 128 * k + 128]
            big[k, pl.ds(16 * t, 8, stride=2)] = tile
            big[k, pl.ds(16 * t + 1, 8, stride=2)] = tile

    def add_up(i, carry):
        for c in range(COMPS):
            at = pl.multiple_of((c * 8 + i // 2) * 16, 16)
            more = [big[k, pl.ds(at, 16)] for k in range(LANES // 128)]
            value = s1[c, i] + jnp.concatenate(more, axis=1)
            s2[c, i] = value
            es2[c, i] = e[0, i] * value
        return carry

    lax.fori_loop(1, PLANES - 1, add_up, 0)
    sweep(s2, es2, s3, es3, r, c1, e, w, 2, PLANES - 2)
    sweep(s3, es3, p, ep, r, c1, e, w, 3, PLANES - 3)


    def own(a):
        return a[:Y]

    def image_of(x):
        i = x + RIM
        near = [e[k, i, :Y] for k in range(3)]
        centre = c1[i, :Y]
        owned, parts = [], []
        for c in range(COMPS):
            owned.append(p[c, i, :Y])
            v = own(tri_y(tri_x(p[c, i - 1], p[c, i], p[c, i + 1])))
            ev = own(tri_y(tri_x(ep[c, i - 1], ep[c, i], ep[c, i + 1])))
            parts.append(centre * owned[c] - mixed_z(*near, v, ev))
        return owned, coupled(parts)

    def image(k, carry):
        steps = [2 * k, 2 * k + 1]
        found = [image_of(x) for x in steps]
        for x, (owned, applied) in zip(steps, found):
            for c in range(COMPS):
                precond[x, c] = owned[c][:, :Z]
                operated[x, c] = applied[c][:, :Z]
        return carry

    lax.fori_loop(0, X // 2, image, 0)
    found = [[], [], [], []]
    for x in range(X):
        for c in range(COMPS):
            own_p, own_a = precond[x, c], operated[x, c]
            d, q = prev_d[c, x], prev_i[c, x]
            terms = (r[c, x + RIM, :Y, :Z] * own_p, own_p * own_a, own_p * q + d * own_a, d * q)
            for kept, term in zip(found, terms):
                kept.append(term)
    found = [tree_sum(kept) for kept in found]
    row = row_of((8, 128))
    total = jnp.zeros((8, 128), F32)
    for k, value in enumerate(found):
        line = jnp.sum(value[:, :128] + value[:, 128:], axis=0, keepdims=True)
        total = jnp.where(row == k, jnp.broadcast_to(line, (8, 128)), total)
    total = total + pltpu.roll(total, 64, 1)
    total = total + pltpu.roll(total, 32, 1)
    total = jnp.where(row == lane_of((8, 128)) // 32, total, 0.0)
    sums[...] = jnp.broadcast_to(jnp.sum(total, axis=0, keepdims=True), sums.shape)


STEP = 2


def last_body(
    prev_rz, sums, precond, operated, prev_d, prev_i, sol, res,
    new_s_out, new_r_out, new_d_out, new_i_out, news, out_sems,
):
    total = jnp.sum(sums[...], axis=0, keepdims=True)
    lane = lane_of((1, 128))

    def entry(k):
        return jnp.sum(jnp.where(lane // 32 == k, total, 0.0), axis=1, keepdims=True)

    rz = entry(0)
    beta = rz / prev_rz[0]
    alpha = rz / (entry(1) + beta * (entry(2) + beta * entry(3)))
    beta = jnp.broadcast_to(beta, (Y, Z))
    alpha = jnp.broadcast_to(alpha, (Y, Z))
    leaving = []
    for step in range(X // STEP):
        for x in range(step * STEP, step * STEP + STEP):
            for c in range(COMPS):
                d = precond[x, c] + beta * prev_d[c, x]
                q = operated[x, c] + beta * prev_i[c, x]
                news[2, c, x] = d
                news[3, c, x] = q
                news[0, c, x] = sol[c, x] + alpha * d
                news[1, c, x] = res[c, x] - alpha * q
        part = pl.ds(step * STEP, STEP)
        for k, target in enumerate((new_s_out, new_r_out, new_d_out, new_i_out)):
            copy = pltpu.make_async_copy(
                news.at[k, :, part], target.at[:, part], out_sems.at[k, step]
            )
            copy.start()
            leaving.append(copy)
    for copy in leaving:
        copy.wait()


PLANES = X + 2 * RIM
FIELD = (COMPS, PLANES, ROWS, LANES)
COLS_SHAPE = (40, MID_LANES)


def smooth_outs():
    return [
        shape(*FIELD),
        shape(*FIELD),
        shape(3, E_PLANES, ROWS, LANES),
        shape(PLANES, ROWS, LANES),
        shape(PLANES, ROWS, LANES),
        shape(3, EM_PLANES, 8, MID_LANES),
        shape(EM_PLANES, 8, MID_LANES),
        shape(M_PLANES, 8, MID_LANES),
        shape(M_PLANES, 8, MID_LANES),
        shape(MZ_PACK, 128),
    ]


def smooth_call(n_z):
    return call(
        functools.partial(smooth_body, n_z),
        smooth_outs(),
        scratch=[
            pltpu.VMEM((E_PLANES, 24, LANES), F32),
            pltpu.VMEM((E_PLANES, 24, LANES), F32),
            pltpu.VMEM(FIELD, F32),
            pltpu.VMEM(FIELD, F32),
            pltpu.VMEM(FIELD, F32),
            pltpu.VMEM((LANES // 128, 18 * ROWS, 128), F32),
            pltpu.VMEM((LANES // 128, 24 * EM_PLANES + 8, 128), F32),
        ],
        n_in=6 + n_z,
        vmem=30 << 20,
    )


def finish_call(n_all):
    return call(
        finish_body,
        [pltpu.VMEM((X, COMPS, Y, Z), F32)] * 2 + [shape(n_all, 128)],
        scratch=[
            pltpu.VMEM((COMPS, 6, 8, MID_LANES), F32),
            pltpu.VMEM((COMPS, 6, 8, MID_LANES), F32),
            pltpu.VMEM((COMPS * 64, MID_LANES), F32),
            pltpu.VMEM((LANES // 128, COMPS * 128, 128), F32),
        ]
        + [pltpu.VMEM(FIELD, F32)] * 6,
        n_in=15,
        vmem=30 << 20,
    )


def on_device(
    solution,
    residual,
    prev_direction,
    prev_image,
    prev_rz,
    density_index,
    stiffness_table,
    coarse_inverse,
):
    if residual.shape != (COMPS, X, Y, Z):
        raise ValueError(residual.shape)
    block = shape(COMPS, X, Y, Z)
    n_z = 1 if lax.axis_size("gz") == 2 else 2
    n_all = lax.axis_size(ALL)

    res, young, px, qx = call(
        pack_x_body,
        [block, shape(X, Y, Z), shape(X_PACK, Y, Z), shape(X_PACK, Y, Z)],
        scratch=[
            pltpu.SMEM(stiffness_table.shape, F32),
            pltpu.VMEM((X, Y, Z), jnp.int32),
            pltpu.SemaphoreType.DMA((3,)),
        ],
        n_in=3,
        hbm=(0, 1, 2),
    )(*[in_hbm(a) for a in (stiffness_table, density_index, residual)])
    got_x = swap("gx", px, qx)
    py, qy = call(pack_y_body, [shape(Y_PACK, Y, Z)] * 2, n_in=4)(res, young, *got_x)
    got_y = swap("gy", py, qy, closed=False)
    packs = call(pack_z_body, [shape(Z_PACK, 128)] * n_z, n_in=6)(res, young, *got_x, *got_y)
    got_z = swap("gz", packs[0], packs[-1])

    r, s1, e, c1, w, em, em_side, c1m, wm, pack = smooth_call(n_z)(res, young, *got_x, *got_y, *got_z)

    got_z = swap("gz", pack, pack)
    gathered = []
    if n_z > 1:
        gathered = [lax.all_gather(pack[8 * LOW_TILE, :24], "gz", axis=0, tiled=True)[None]]
    size = coarse_inverse.shape[-1]
    mid_planes, column, px, qx = call(
        functools.partial(coarse_body, n_z),
        [
            shape(LOW_TILE, 8, MID_LANES),
            shape(16, MID_LANES),
            shape(MX_PACK, 128),
            shape(MX_PACK, 128),
        ],
        scratch=[pltpu.VMEM((size + 64, 128), F32)],
        n_in=2 + n_z + len(gathered),
    )(pack, *got_z, coarse_inverse, *gathered)
    got_x = swap("gx", px, qx)
    mid_planes, columns, py, qy = call(
        mid_y_body,
        [
            shape(COMPS * 8, 8, MID_LANES),
            shape(40, MID_LANES),
            shape(MY_PACK, 128),
            shape(MY_PACK, 128),
        ],
        n_in=4,
    )(mid_planes, column, *got_x)
    got_y = swap("gy", py, qy, closed=False)
    precond, operated, sums = finish_call(n_all)(
        mid_planes, columns, *got_y, r, s1, e, c1, w, em, em_side, c1m, wm, prev_direction, prev_image
    )
    precond, operated = in_vmem(precond), in_vmem(operated)
    sums = lax.all_to_all(sums, ALL, 0, 0, tiled=True)
    return tuple(
        call(
            last_body,
            [block] * 4,
            scratch=[
                pltpu.VMEM((4, COMPS, X, Y, Z), F32),
                pltpu.SemaphoreType.DMA((4, X // STEP)),
            ],
            n_in=8,
            smem=(0,),
            hbm_out=(0, 1, 2, 3),
        )(
            prev_rz.reshape(1), sums, precond, operated, prev_direction, prev_image, solution, residual
        )
    )


def solution(mesh):
    field = P(None, "gx", "gy", "gz")
    return jax.shard_map(
        on_device,
        mesh=mesh,
        in_specs=(
            field,
            field,
            field,
            field,
            P(),
            P("gx", "gy", "gz"),
            P(),
            P("gx", "gy", None, None),
        ),
        out_specs=(field, field, field, field),
        check_vma=False,
    )
```

```python
import functools
import math

import jax
import jax.numpy as jnp
from jax import lax
from jax.experimental import pallas as pl
from jax.experimental.pallas import tpu as pltpu
from jax.sharding import PartitionSpec as P

X, Y, Z = 8, 8, 256
COMPS = 3
RIM = 4
WIDE = 6
ROWS = Y + 2 * RIM
LANES = Z + 128
MID_LANES = Z // 2 + 128
DAMPING = 0.6
COUPLING = (1.6, 0.7, 0.7)
ALL = ("gx", "gy", "gz")
F32 = jnp.float32
VMEM = pl.BlockSpec(memory_space=pltpu.VMEM)
SMEM = pl.BlockSpec(memory_space=pltpu.SMEM)
HBM = pl.BlockSpec(memory_space=pltpu.HBM)


def shape(*dims):
    return jax.ShapeDtypeStruct(dims, F32)


def call(body, outs, scratch=(), n_in=0, smem=(), hbm=(), hbm_out=(), vmem=16 << 20):
    return pl.pallas_call(
        body,
        out_shape=outs,
        in_specs=[SMEM if i in smem else HBM if i in hbm else VMEM for i in range(n_in)],
        out_specs=[HBM if i in hbm_out else VMEM for i in range(len(outs))],
        scratch_shapes=list(scratch),
        compiler_params=pltpu.CompilerParams(vmem_limit_bytes=vmem),
    )


def in_hbm(a):
    return pltpu.with_memory_space_constraint(a, pltpu.HBM)


def in_vmem(a):
    return pltpu.with_memory_space_constraint(a, pltpu.VMEM)


def pairs(count, odd, closed):
    if not odd:
        return [(i, i ^ 1) for i in range(count)]
    made = [(i, (i + 1) % count if i % 2 else (i - 1) % count) for i in range(count)]
    return made if closed else made[1:-1]


def swap(axis, even_pack, odd_pack, closed=True):
    count = lax.axis_size(axis)
    got_even = lax.ppermute(even_pack, axis, pairs(count, False, closed))
    if count == 2:
        return [got_even]
    return [got_even, lax.ppermute(odd_pack, axis, pairs(count, True, closed))]


def is_even(axis):
    return lax.rem(lax.axis_index(axis), 2) == 0


def inner(axis):
    index = lax.axis_index(axis)
    return jnp.logical_and(index > 0, index < lax.axis_size(axis) - 1)


def from_sides(got, axis):
    even = is_even(axis)
    if len(got) == 1:

        def lower(key):
            value = got[0][key]
            return jnp.where(even, 0.0, value)

        def upper(key):
            value = got[0][key]
            return jnp.where(even, value, 0.0)

        return lower, upper
    ok = inner(axis)

    def lower(key):
        return jnp.where(even, jnp.where(ok, got[1][key], 0.0), got[0][key])

    def upper(key):
        return jnp.where(even, got[0][key], jnp.where(ok, got[1][key], 0.0))

    return lower, upper


def tri_y(a):
    a = a + pltpu.roll(a, 1, 0)
    return a + pltpu.roll(a, a.shape[0] - 1, 0)


def tri_y_with(a, below, above, last):
    rows = a.shape[0]
    row = row_of(a.shape)
    former = jnp.where(row == last + 1, below, pltpu.roll(a, 1, 0))
    after = jnp.where(row == last, above, pltpu.roll(a, rows - 1, 0))
    return former + after + (a + a)


def mixed_z(e, e_next, e_last, v, ev):
    both = e * v + ev
    moved = pltpu.roll(e_next * v + ev, 1, 1) + pltpu.roll(e_last * v + ev, v.shape[1] - 1, 1)
    return moved + (both + both)


def tri_x(before, centre, after):
    return before + after + (centre + centre)


def tri_x_pair(a, b, c, d):
    near = b + c
    return (a + b) + near, near + (c + d)


def tri_rows(a, below=None, above=None):
    even, odd = a[:8], a[8:]
    former, after = pltpu.roll(odd, 1, 0), pltpu.roll(even, 7, 0)
    if below is not None:
        row = row_of(even.shape)
        former = jnp.where(row == 6, below, former)
        after = jnp.where(row == 5, above, after)
    both = even + odd
    return jnp.concatenate([both + (even + former), both + (odd + after)], axis=0)


def tree_sum(terms):
    while len(terms) > 1:
        terms = [sum(terms[k : k + 2]) for k in range(0, len(terms), 2)]
    return terms[0]


def to_modes(v0, v1, v2):
    total = v0 + v1 + v2
    third = total * (1.0 / 3.0)
    return total, v0 - third, v1 - third


def from_modes(total, a, b):
    third = total * (1.0 / 3.0)
    return a + third, b + third, third - a - b


def row_of(shape):
    return lax.broadcasted_iota(jnp.int32, shape, 0)


def lane_of(shape):
    return lax.broadcasted_iota(jnp.int32, shape, 1)


def up(a, shift):
    shift %= a.shape[0]
    return pltpu.roll(a, shift, 0) if shift else a


def pool_matrix(value):
    lane = row_of((LANES, MID_LANES))
    mid = jnp.where(lane < Z + 64, lane // 2, lane // 2 + 64)
    return jnp.where(mid == lane_of((LANES, MID_LANES)), value, 0.0).astype(F32)


def spread_matrix():
    lane = lane_of((MID_LANES, LANES))
    mid = jnp.where(lane < Z + 64, lane // 2, lane // 2 + 64)
    return jnp.where(mid == row_of((MID_LANES, LANES)), 1.0, 0.0).astype(F32)


def dot_exact_weights(a, b):
    b = b.astype(jnp.bfloat16)
    total = None
    for k in range(3):
        part = a.astype(jnp.bfloat16)
        found = jnp.dot(part, b, preferred_element_type=F32)
        total = found if total is None else total + found
        if k < 2:
            a = a - part.astype(F32)
    return total


X_PACK = COMPS * RIM + WIDE
R_TILES = COMPS * X
E_PLANES = X + 2 * WIDE
E4_TILES = E_PLANES // 2
E2_TILES = E_PLANES // 4
Y_PACK = R_TILES + E4_TILES + E2_TILES
Z_TILES = COMPS * (X + 2 * RIM) * (ROWS // 8) + E_PLANES * 3
Z_PACK = -(-Z_TILES // 16) * 8


def pack_x_body(
    table_in, index_in, res_in, res, young, pack_even, pack_odd, table, index, res_n, young_n, sems
):
    copies = [
        pltpu.make_async_copy(table_in, table, sems.at[0]),
        pltpu.make_async_copy(index_in, index, sems.at[1]),
    ]
    for k in range(2):
        source = res_in.at[:, :, :, pl.ds(128 * k, 128)]
        copies.append(pltpu.make_async_copy(source, res_n.at[k], sems.at[2 + k]))
    for copy in copies:
        copy.start()
    copies[0].wait()
    copies[1].wait()
    levels = index[...]
    value = jnp.zeros(levels.shape, F32)
    for level in range(table.shape[0]):
        value = jnp.where(levels == level, table[level], value)

    def own_tile(ref, *at):
        rows = [ref[(*at, pl.ds(start, 4, stride=2), slice(None))] for start in (0, 1)]
        return jnp.concatenate(rows, axis=0)

    for k in range(2):
        young_n[k] = value[:, :, 128 * k : 128 * k + 128]
    for k in range(2):
        for x in range(X):
            young[x, :, 128 * k : 128 * k + 128] = own_tile(young_n, k, x)
    for k in range(2):
        copies[2 + k].wait()
        for x in range(X):
            modes = to_modes(*[own_tile(res_n, k, c, x) for c in range(COMPS)])
            for c in range(COMPS):
                res[c, x, :, 128 * k : 128 * k + 128] = modes[c]
    high_first = jnp.where(is_even("gx"), 1, 0)
    for pack, high in ((pack_even, high_first), (pack_odd, 1 - high_first)):
        for c in range(COMPS):
            pack[c * RIM : (c + 1) * RIM] = res[c, pl.ds(high * (X - RIM), RIM)]
        pack[COMPS * RIM :] = young[pl.ds(high * (X - WIDE), WIDE)]


def x_planes(res, young, got_x, lanes=slice(None)):
    lower, upper = from_sides(got_x, "gx")
    whole = slice(None)

    def res_plane(c, i):
        if i < RIM:
            return lower((c * RIM + i, whole, lanes))
        if i < RIM + X:
            return res[c, i - RIM, :, lanes]
        return upper((c * RIM + i - RIM - X, whole, lanes))

    def young_plane(i):
        if i < WIDE:
            return lower((COMPS * RIM + i, whole, lanes))
        if i < WIDE + X:
            return young[i - WIDE, :, lanes]
        return upper((COMPS * RIM + i - WIDE - X, whole, lanes))

    return res_plane, young_plane


def pack_y_body(res, young, got_a, got_b, pack_even, pack_odd):
    res_plane, young_plane = x_planes(res, young, (got_a, got_b))
    row = row_of((Y, Z))
    even = is_even("gy")

    def put(tile, low, high):
        pack_even[tile] = jnp.where(even, high, low)
        pack_odd[tile] = jnp.where(even, low, high)

    def halves(tile, a, b):
        put(
            tile,
            jnp.where(row % 4 < 2, a, up(b, 2)),
            jnp.where(row % 4 < 2, up(a, -2), b),
        )

    for c in range(COMPS):
        for i in range(X):
            halves(c * X + i, res_plane(c, i), res_plane(c, i + X))
    planes = [young_plane(i) for i in range(E_PLANES)]
    for i in range(E4_TILES):
        halves(R_TILES + i, planes[i], planes[i + E4_TILES])
    for j in range(E2_TILES):
        low = high = None
        for k in range(4):
            plane = planes[4 * j + k]
            a, b = up(plane, k - 2), up(plane, k - 1)
            low = a if k == 0 else jnp.where(row % 4 == k, a, low)
            high = b if k == 0 else jnp.where(row % 4 == k, b, high)
        put(R_TILES + E4_TILES + j, low, high)


def xy_planes(res, young, got_x, got_y, lanes, width):
    res_plane, young_plane = x_planes(res, young, got_x, lanes)
    lower, upper = from_sides(got_y, "gy")
    row = row_of((Y, width))
    whole = slice(None)

    def with_rims(own, tile, second):
        key = (tile, whole, lanes)
        low, high = lower(key), upper(key)
        at = 2 if second else 0
        even = jnp.where(row < 6, up(high, 4 - at), up(low, 6 - at))
        odd = jnp.where(row < 6, up(high, -at), up(low, 2 - at))
        return [jnp.where(row < 4, own, even), jnp.where(row < 4, up(own, 4), odd)]

    def res_tiles(c, i):
        return with_rims(res_plane(c, i), c * X + i % X, i >= X)

    def young_tiles(i):
        two = (R_TILES + E4_TILES + i // 4, whole, lanes)
        k = i % 4
        low2, high2 = up(lower(two), -k), up(upper(two), 1 - k)
        side = jnp.where(row % 4 == 0, low2, jnp.where(row % 4 == 1, high2, 0.0))
        return with_rims(young_plane(i), R_TILES + i % E4_TILES, i >= E4_TILES) + [side]

    return res_tiles, young_tiles


def pack_z_body(res, young, xa, xb, ya, yb, *packs):
    high_first = jnp.where(is_even("gz"), 1, 0)
    lane = lane_of((8, 128))
    for pack, high in zip(packs, (high_first, 1 - high_first)):
        lanes = pl.ds(pl.multiple_of(high * (Z - 128), 128), 128)
        res_tiles, young_tiles = xy_planes(res, young, (xa, xb), (ya, yb), lanes, 128)
        tiles = [t for c in range(COMPS) for i in range(X + 2 * RIM) for t in res_tiles(c, i)]
        tiles += [t for i in range(E_PLANES) for t in young_tiles(i)]
        for first in range(0, len(tiles), 16):
            packed = None
            for j, tile in enumerate(tiles[first : first + 16]):
                moved = pltpu.roll(tile, lax.rem(8 * j + 8 * high, 128), 1)
                packed = moved if j == 0 else jnp.where(lane < 8 * j, packed, moved)
            pack[first // 2 : first // 2 + 8] = packed


def z_rims(got_z):
    lane = lane_of((8, 128))
    even = is_even("gz")

    def piece(got, t, right):
        start = jnp.where(right, 0, 120)
        tile = got[8 * (t // 16) : 8 * (t // 16) + 8, :]
        moved = pltpu.roll(tile, lax.rem(start + 128 - 8 * (t % 16), 128), 1)
        inside = jnp.logical_and(lane >= start, lane < start + 8)
        return jnp.where(inside, moved, 0.0)

    def rim(t):
        first = piece(got_z[0], t, even)
        if len(got_z) == 1:
            return first
        second = piece(got_z[1], t, jnp.logical_not(even))
        return first + jnp.where(inner("gz"), second, 0.0)

    return rim


M_PLANES = X // 2 + 4
EM_PLANES = X // 2 + 6
LOW_TILE = COMPS * (X // 2)
MZ_PACK = (LOW_TILE + 1) * 8


def fine_parts(s, es, c1, e, i):
    found = []
    for c in range(COMPS):
        v = tri_x_pair(*[s[c, i + k] for k in range(-1, 3)])
        ev = tri_x_pair(*[es[c, i + k] for k in range(-1, 3)])
        found.append(
            [
                c1[i + k] * s[c, i + k]
                - mixed_z(e[0, i + k], e[1, i + k], e[2, i + k], tri_rows(v[k]), tri_rows(ev[k]))
                for k in range(2)
            ]
        )
    return found


def sweep(source, e_source, target, e_target, s0, c1, e, w, first, last):
    def body(n, carry):
        i = first + 2 * n
        parts = fine_parts(source, e_source, c1, e, i)
        for k in range(2):
            for c in range(COMPS):
                factor = w[0 if c == 0 else 1, i + k]
                value = (source[c, i + k] + s0[c, i + k]) - factor * parts[c][k]
                target[c, i + k] = value
                e_target[c, i + k] = e[0, i + k] * value
        return carry

    lax.fori_loop(0, (last - first) // 2, body, 0)


def smooth_body(n_z, *refs):
    res, young, xa, xb, ya, yb = refs[:6]
    got_z = refs[6 : 6 + n_z]
    s0, s1, e, c1, w, em, em_side, c1m, wm, pack = refs[6 + n_z : 16 + n_z]
    wide, wide_z, r, es0, es1, to_pool = refs[16 + n_z :]

    res_tiles, young_tiles = xy_planes(res, young, (xa, xb), (ya, yb), slice(None), Z)
    rim = z_rims(got_z)
    at = 0
    for c in range(COMPS):
        for i in range(PLANES):
            for t, tile in enumerate(res_tiles(c, i)):
                r[c, i, 8 * t : 8 * t + 8, :Z] = tile
                r[c, i, 8 * t : 8 * t + 8, Z:] = rim(at)
                at += 1
    for i in range(E_PLANES):
        for t, tile in enumerate(young_tiles(i)):
            wide[i, 8 * t : 8 * t + 8, :Z] = tile * 0.0125
            wide[i, 8 * t : 8 * t + 8, Z:] = rim(at) * 0.0125
            at += 1

    def shift(k, carry):
        for i in (2 * k, 2 * k + 1):
            centre = wide[i]
            after, before = pltpu.roll(centre, LANES - 1, 1), pltpu.roll(centre, 1, 1)
            wide_z[i] = after + before + (centre + centre)
            e[0, i] = centre[:ROWS]
            e[1, i] = after[:ROWS]
            e[2, i] = before[:ROWS]
        total = wide[2 * k] + wide[2 * k + 1]
        side = total[ROWS:]
        start = pl.multiple_of(COMPS * 6 * 8 + 16 * k, 16)
        to_pool[pl.ds(start, 8)] = total[:8] + total[8:ROWS]
        to_pool[pl.ds(start + 8, 8)] = side + up(side, 4)
        return carry

    lax.fori_loop(0, E_PLANES // 2, shift, 0, unroll=5)

    def prepare(k, carry):
        for i in (2 * k, 2 * k + 1):
            total = tri_x(wide_z[i + 1], wide_z[i + 2], wide_z[i + 3])
            side = total[ROWS:]
            total = tri_rows(total[:ROWS], up(side, 2), up(side, 4))
            centre = e[0, i + 2]
            c1[i] = 72.0 * centre + total
            inverse = jnp.where(centre > 0.0, DAMPING / (56.0 * centre + total), 0.0)
            for n in range(2):
                w[n, i] = COUPLING[n] * inverse
            for c in range(COMPS):
                value = inverse * r[c, i]
                s0[c, i] = value
                es0[c, i] = centre * value
        return carry

    lax.fori_loop(0, PLANES // 2, prepare, 0)
    e = e.at[:, 2 : 2 + PLANES]
    sweep(s0, es0, s1, es1, s0, c1, e, w, 1, PLANES - 1)

    def residue(m, carry):
        i = 2 * m + 2
        parts = fine_parts(s1, es1, c1, e, i)
        for c in range(COMPS):
            total = (r[c, i] + r[c, i + 1]) - COUPLING[c] * (parts[c][0] + parts[c][1])
            start = pl.multiple_of((c * 6 + m) * 8, 8)
            to_pool[pl.ds(start, 8)] = total[:8] + total[8:]
        return carry

    lax.fori_loop(0, 6, residue, 0)

    pooled = dot_exact_weights(to_pool[...], pool_matrix(0.5))
    pooled = [pooled[8 * t : 8 * t + 8] for t in range(COMPS * 6 + 2 * EM_PLANES)]
    for m in range(EM_PLANES):
        centre = 0.25 * pooled[COMPS * 6 + 2 * m]
        em[0, m] = centre
        em[1, m] = pltpu.roll(centre, MID_LANES - 1, 1)
        em[2, m] = pltpu.roll(centre, 1, 1)
        em_side[m] = 0.25 * pooled[COMPS * 6 + 2 * m + 1]
    for m in range(M_PLANES):
        total = tri_x(*[em[0, m + k] for k in range(3)])
        side = tri_x(*[em_side[m + k] for k in range(3)])
        total = tri_y_with(total, up(side, 6), up(side, 4), 5)
        total = total + total + pltpu.roll(total, 1, 1) + pltpu.roll(total, MID_LANES - 1, 1)
        centre = em[0, m + 1]
        c1m[m] = 72.0 * centre + total
        wm[m] = jnp.where(centre > 0.0, DAMPING / (56.0 * centre + total), 0.0)

    rhs, mid, e_mid = {}, {}, {}
    for m in range(6):
        for c in range(COMPS):
            rhs[c, m] = pooled[c * 6 + m]
            mid[c, m] = wm[m + 1] * rhs[c, m]
            e_mid[c, m] = em[0, m + 2] * mid[c, m]
    kept = {}
    for m in range(1, 5):
        for c in range(COMPS):
            v = tri_y(tri_x(mid[c, m - 1], mid[c, m], mid[c, m + 1]))
            ev = tri_y(tri_x(e_mid[c, m - 1], e_mid[c, m], e_mid[c, m + 1]))
            mixed = mixed_z(em[0, m + 2], em[1, m + 2], em[2, m + 2], v, ev)
            left_over = rhs[c, m] - COUPLING[c] * (c1m[m + 1] * mid[c, m] - mixed)
            kept[c, m - 1] = left_over
            value = mid[c, m] + wm[m + 1] * left_over
            tile = c * 4 + m - 1
            pack[8 * tile : 8 * tile + 8] = value[:, :128]
    rows = {}
    for b in range(2):
        found = from_modes(*[kept[c, 2 * b] + kept[c, 2 * b + 1] for c in range(COMPS)])
        for c in range(COMPS):
            rows[c, b] = found[c]
    stacked = jnp.concatenate([rows[c, b] for c in range(COMPS) for b in range(2)], axis=0)
    lane_box = row_of((MID_LANES, 128))
    column = lane_of((MID_LANES, 128))
    boxes = jnp.where(
        jnp.logical_and(lane_box < Z // 2, lane_box // 64 == column % 2), 1.0, 0.0
    ).astype(F32)
    sums = dot_exact_weights(stacked, boxes)
    line = row_of((48, 128))
    entry = lane_of((48, 128))
    inside = line % 8
    match = jnp.logical_and((line // 8) * 2 + inside // 2 == entry // 2, inside < 4)
    scale = 1.0 / math.sqrt((X // 4) * (Y // 4) * (Z // 4))
    low = jnp.sum(jnp.where(match, sums, 0.0), axis=0, keepdims=True) * scale
    pack[8 * LOW_TILE :] = jnp.broadcast_to(low, (8, 128))


def pack_mid(pack, tiles):
    lane = lane_of((8, 128))
    rims = None
    for n, tile in enumerate(tiles):
        pack[8 * n : 8 * n + 8] = tile[:, :128]
        moved = pltpu.roll(tile[:, 128:], 4 + 8 * n, 1)
        rims = moved if n == 0 else jnp.where(lane < 8 * n, rims, moved)
    pack[8 * len(tiles) :] = rims


def unpack_mid(side, count):
    lane = lane_of((8, 128))
    near = jnp.logical_or(lane < 4, lane >= 124)
    rims = side((slice(8 * count, 8 * count + 8), slice(None)))
    tiles = []
    for n in range(count):
        main = side((slice(8 * n, 8 * n + 8), slice(None)))
        rim = jnp.where(near, pltpu.roll(rims, 124 - 8 * n, 1), 0.0)
        tiles.append(jnp.concatenate([main, rim], axis=1))
    return tiles


def coarse_body(n_z, *refs):
    pack = refs[0]
    got_z = refs[1 : 1 + n_z]
    matrix = refs[1 + n_z]
    gathered = refs[2 + n_z : -5]
    planes, column, pack_even, pack_odd, scratch = refs[-5:]
    place = lax.axis_index("gz")
    left, right = from_sides(got_z, "gz")
    lane = lane_of((8, 128))
    for t in range(LOW_TILE):
        key = (slice(8 * t, 8 * t + 8), slice(None))
        planes[t, :, :128] = pack[key]
        planes[t, :, 128:] = jnp.where(lane < 64, right(key), left(key))

    size = 24
    if gathered:
        rhs = gathered[0][...]
    else:
        mine = pack[8 * LOW_TILE : 8 * LOW_TILE + 8]
        other = got_z[0][8 * LOW_TILE : 8 * LOW_TILE + 8]
        first = jnp.where(place == 0, mine, other)
        second = jnp.where(place == 0, other, mine)
        rhs = jnp.where(lane < size, first, pltpu.roll(second, size, 1))[:1, : 2 * size]
    solved = jnp.sum(matrix[0, 0] * rhs, axis=1, keepdims=True)
    scratch[...] = jnp.zeros(scratch.shape, F32)
    scratch[size : size + solved.shape[0]] = jnp.broadcast_to(solved, (solved.shape[0], 128))
    base = pl.multiple_of(place * size, 8)
    wide = lane_of((16, MID_LANES))
    before, own_a, own_b, after = [
        jnp.concatenate([scratch[pl.ds(base + at, 16, stride=2)]] * 2, axis=1)
        for at in (1, size, size + 1, 2 * size)
    ]
    value = jnp.where(wide < 64, own_a, own_b)
    value = jnp.where(wide < 128, value, jnp.where(wide < 192, after, before))
    row = row_of((8, MID_LANES))
    first, second, third = value[:8], up(value[:8], 4), value[8:]
    total, a, b = to_modes(first, second, third)
    rest = [jnp.where(row < 4, total, up(a, 4)), jnp.where(row < 4, b, 0.0)]
    column[:8] = rest[0]
    column[8:] = rest[1]

    even = is_even("gx")
    low, high = [
        [jnp.where(row < 4, planes[c * 4 + p], up(planes[c * 4 + p + 1], 4)) for c in range(COMPS)]
        for p in (0, 2)
    ]
    pack_mid(pack_even, [jnp.where(even, b, a) for a, b in zip(low, high)] + rest)
    pack_mid(pack_odd, [jnp.where(even, a, b) for a, b in zip(low, high)] + rest)


MX_TILES = COMPS + 2
MY_TILES = 2 * COMPS + 5
MX_PACK = (MX_TILES + 1) * 8
MY_PACK = (MY_TILES + 1) * 8


def mid_y_body(planes, column, got_a, got_b, wide_planes, columns, pack_even, pack_odd):
    lower, upper = from_sides((got_a, got_b), "gx")
    low_tiles, high_tiles = unpack_mid(lower, MX_TILES), unpack_mid(upper, MX_TILES)
    row = row_of((8, MID_LANES))
    even = is_even("gy")
    below_packs, above_packs = [], []
    for c in range(COMPS):
        tiles = [low_tiles[c], up(low_tiles[c], 4)]
        tiles += [planes[c * 4 + p] for p in range(4)]
        tiles += [high_tiles[c], up(high_tiles[c], 4)]
        for t in range(8):
            wide_planes[c * 8 + t] = tiles[t]
        for h in range(2):
            below = above = None
            for k in range(4):
                tile = tiles[4 * h + k]
                a, b = up(tile, 2 * k), up(tile, 2 * k - 2)
                below = a if k == 0 else jnp.where(row < 2 * k, below, a)
                above = b if k == 0 else jnp.where(row < 2 * k, above, b)
            below_packs.append(below)
            above_packs.append(above)
    columns[:8] = low_tiles[COMPS]
    columns[8:12] = low_tiles[COMPS + 1][:4]
    columns[12:24] = column[:12]
    columns[24:32] = high_tiles[COMPS]
    columns[32:36] = high_tiles[COMPS + 1][:4]
    columns[36:] = jnp.zeros((4, MID_LANES), F32)
    rest = [columns[8 * t : 8 * t + 8] for t in range(5)]
    pairs_of = list(zip(below_packs, above_packs))
    pack_mid(pack_even, [jnp.where(even, a, b) for b, a in pairs_of] + rest)
    pack_mid(pack_odd, [jnp.where(even, b, a) for b, a in pairs_of] + rest)


def finish_body(
    wide_planes, columns, got_a, got_b, s0, s1, e_all, c1, w, em, em_side, c1m, wm, prev_d, prev_i,
    res, precond, operated, sums, cor, cor_side, mid, fine, s2, es2, s3, es3, p, ep,
):
    e = e_all.at[:, 2 : 2 + PLANES]
    lower, upper = from_sides((got_a, got_b), "gy")
    row = row_of((8, MID_LANES))

    low_tiles, high_tiles = unpack_mid(lower, MY_TILES), unpack_mid(upper, MY_TILES)
    below = jnp.concatenate(low_tiles[2 * COMPS :], axis=0)
    above = jnp.concatenate(high_tiles[2 * COMPS :], axis=0)
    middle = columns[...]
    for c in range(COMPS):
        for b in range(6):
            at = (b // 2) * 12 + c * 4 + (b % 2) * 2

            def band(source, by):
                return jnp.broadcast_to(source[at + by : at + by + 1], (8, MID_LANES))

            field = jnp.where(row < 6, band(above, 0), band(below, 1))
            field = jnp.where(row < 4, band(middle, 1), field)
            cor[c, b] = jnp.where(row < 2, band(middle, 0), field)
            cor_side[c, b] = jnp.where(row == 0, band(below, 0), band(above, 1))

    def box(m):
        return (m + 1) // 2

    for m in range(M_PLANES):
        for c in range(COMPS):
            near = [cor[c, box(m + k)] for k in range(3)]
            near_side = [cor_side[c, box(m + k)] for k in range(3)]
            e_near = [em[0, m + k] * near[k] for k in range(3)]
            e_side = [em_side[m + k] * near_side[k] for k in range(3)]
            side = tri_x(*near_side)
            v = tri_y_with(tri_x(*near), up(side, 6), up(side, 4), 5)
            side = tri_x(*e_side)
            ev = tri_y_with(tri_x(*e_near), up(side, 6), up(side, 4), 5)
            mixed = mixed_z(em[0, m + 1], em[1, m + 1], em[2, m + 1], v, ev)
            applied = COUPLING[c] * (c1m[m] * near[1] - mixed)
            tile = wide_planes[c * 8 + m]
            n, k = c * 2 + m // 4, m % 4
            outer = jnp.where(row < 6, up(high_tiles[n], 4 - 2 * k), up(low_tiles[n], 6 - 2 * k))
            tile = jnp.where(row < 4, tile, outer)
            at = (c * 8 + m) * 8
            mid[at : at + 8] = tile + cor[c, box(m + 1)] - wm[m] * applied
    fine[...] = dot_exact_weights(mid[...], spread_matrix())

    def add_up(i, carry):
        for c in range(COMPS):
            at = pl.multiple_of((c * 8 + i // 2) * 8, 8)
            more = fine[pl.ds(at, 8)]
            value = s1[c, i] + jnp.concatenate([more, more], axis=0)
            s2[c, i] = value
            es2[c, i] = e[0, i] * value
        return carry

    lax.fori_loop(1, PLANES - 1, add_up, 0)
    sweep(s2, es2, s3, es3, s0, c1, e, w, 2, PLANES - 2)
    sweep(s3, es3, p, ep, s0, c1, e, w, 3, PLANES - 3)

    def put_rows(target, x, modes):
        for half in range(2):
            for c, value in enumerate(from_modes(*[m[8 * half : 8 * half + 8, :Z] for m in modes])):
                for k in range(Z // 128):
                    part = value[:4, 128 * k : 128 * k + 128]
                    target[x, c, k, pl.ds(half, 4, stride=2), :] = part

    def image(n, carry):
        i = 2 * n + RIM
        parts = fine_parts(p, ep, c1, e, i)
        for k in range(2):
            put_rows(precond, 2 * n + k, [p[c, i + k] for c in range(COMPS)])
            put_rows(operated, 2 * n + k, [COUPLING[c] * parts[c][k] for c in range(COMPS)])
        return carry

    lax.fori_loop(0, X // 2, image, 0)
    found = [[], [], [], []]
    for x in range(X):
        for c in range(COMPS):
            for k in range(Z // 128):
                lanes = slice(128 * k, 128 * k + 128)
                own_p, own_a = precond[x, c, k], operated[x, c, k]
                d, q = prev_d[c, x, :, lanes], prev_i[c, x, :, lanes]
                own_r = res[c, x, :, lanes]
                terms = (own_r * own_p, own_p * own_a, own_p * q + d * own_a, d * q)
                for kept, term in zip(found, terms):
                    kept.append(term)
    found = [tree_sum(kept) for kept in found]
    row = row_of((8, 128))
    total = jnp.zeros((8, 128), F32)
    for k, value in enumerate(found):
        line = jnp.sum(value, axis=0, keepdims=True)
        total = jnp.where(row == k, jnp.broadcast_to(line, (8, 128)), total)
    total = total + pltpu.roll(total, 64, 1)
    total = total + pltpu.roll(total, 32, 1)
    total = jnp.where(row == lane_of((8, 128)) // 32, total, 0.0)
    sums[...] = jnp.broadcast_to(jnp.sum(total, axis=0, keepdims=True), sums.shape)


STEP = 2


def last_body(
    prev_rz, sums, precond, operated, prev_d, prev_i, sol, res,
    new_s_out, new_r_out, new_d_out, new_i_out, news, out_sems,
):
    total = jnp.sum(sums[...], axis=0, keepdims=True)
    lane = lane_of((1, 128))

    def entry(k):
        return jnp.sum(jnp.where(lane // 32 == k, total, 0.0), axis=1, keepdims=True)

    rz = entry(0)
    beta = rz / prev_rz[0]
    alpha = rz / (entry(1) + beta * (entry(2) + beta * entry(3)))
    beta = jnp.broadcast_to(beta, (Y, 128))
    alpha = jnp.broadcast_to(alpha, (Y, 128))
    leaving = []
    for step in range(X // STEP):
        for x in range(step * STEP, step * STEP + STEP):
            for c in range(COMPS):
                for k in range(Z // 128):
                    at = (c, x, slice(None), slice(128 * k, 128 * k + 128))
                    d = precond[x, c, k] + beta * prev_d[at]
                    q = operated[x, c, k] + beta * prev_i[at]
                    news[(2, *at)] = d
                    news[(3, *at)] = q
                    news[(0, *at)] = sol[at] + alpha * d
                    news[(1, *at)] = res[at] - alpha * q
        part = pl.ds(step * STEP, STEP)
        for k, target in enumerate((new_s_out, new_r_out, new_d_out, new_i_out)):
            copy = pltpu.make_async_copy(
                news.at[k, :, part], target.at[:, part], out_sems.at[k, step]
            )
            copy.start()
            leaving.append(copy)
    for copy in leaving:
        copy.wait()


PLANES = X + 2 * RIM
FIELD = (COMPS, PLANES, ROWS, LANES)
COLS_SHAPE = (40, MID_LANES)


def smooth_outs():
    return [
        shape(*FIELD),
        shape(*FIELD),
        shape(3, E_PLANES, ROWS, LANES),
        shape(PLANES, ROWS, LANES),
        shape(2, PLANES, ROWS, LANES),
        shape(3, EM_PLANES, 8, MID_LANES),
        shape(EM_PLANES, 8, MID_LANES),
        shape(M_PLANES, 8, MID_LANES),
        shape(M_PLANES, 8, MID_LANES),
        shape(MZ_PACK, 128),
    ]


def smooth_call(n_z):
    return call(
        functools.partial(smooth_body, n_z),
        smooth_outs(),
        scratch=[
            pltpu.VMEM((E_PLANES, 24, LANES), F32),
            pltpu.VMEM((E_PLANES, 24, LANES), F32),
            pltpu.VMEM(FIELD, F32),
            pltpu.VMEM(FIELD, F32),
            pltpu.VMEM(FIELD, F32),
            pltpu.VMEM((COMPS * 6 * 8 + 16 * EM_PLANES, LANES), F32),
        ],
        n_in=6 + n_z,
        vmem=30 << 20,
    )


def finish_call(n_all):
    return call(
        finish_body,
        [pltpu.VMEM((X, COMPS, Z // 128, Y, 128), F32)] * 2 + [shape(n_all, 128)],
        scratch=[
            pltpu.VMEM((COMPS, 6, 8, MID_LANES), F32),
            pltpu.VMEM((COMPS, 6, 8, MID_LANES), F32),
            pltpu.VMEM((COMPS * 64, MID_LANES), F32),
            pltpu.VMEM((COMPS * 64, LANES), F32),
        ]
        + [pltpu.VMEM(FIELD, F32)] * 6,
        n_in=16,
        vmem=30 << 20,
    )


def on_device(
    solution,
    residual,
    prev_direction,
    prev_image,
    prev_rz,
    density_index,
    stiffness_table,
    coarse_inverse,
):
    if residual.shape != (COMPS, X, Y, Z):
        raise ValueError(residual.shape)
    block = shape(COMPS, X, Y, Z)
    n_z = 1 if lax.axis_size("gz") == 2 else 2
    n_all = lax.axis_size(ALL)

    res, young, px, qx = call(
        pack_x_body,
        [block, shape(X, Y, Z), shape(X_PACK, Y, Z), shape(X_PACK, Y, Z)],
        scratch=[
            pltpu.SMEM(stiffness_table.shape, F32),
            pltpu.VMEM((X, Y, Z), jnp.int32),
            pltpu.VMEM((2, COMPS, X, Y, 128), F32),
            pltpu.VMEM((2, X, Y, 128), F32),
            pltpu.SemaphoreType.DMA((4,)),
        ],
        n_in=3,
        hbm=(0, 1, 2),
    )(*[in_hbm(a) for a in (stiffness_table, density_index, residual)])
    got_x = swap("gx", px, qx)
    py, qy = call(pack_y_body, [shape(Y_PACK, Y, Z)] * 2, n_in=4)(res, young, *got_x)
    got_y = swap("gy", py, qy, closed=False)
    packs = call(pack_z_body, [shape(Z_PACK, 128)] * n_z, n_in=6)(res, young, *got_x, *got_y)
    got_z = swap("gz", packs[0], packs[-1])

    s0, s1, e, c1, w, em, em_side, c1m, wm, pack = smooth_call(n_z)(res, young, *got_x, *got_y, *got_z)

    got_z = swap("gz", pack, pack)
    gathered = []
    if n_z > 1:
        gathered = [lax.all_gather(pack[8 * LOW_TILE, :24], "gz", axis=0, tiled=True)[None]]
    size = coarse_inverse.shape[-1]
    mid_planes, column, px, qx = call(
        functools.partial(coarse_body, n_z),
        [
            shape(LOW_TILE, 8, MID_LANES),
            shape(16, MID_LANES),
            shape(MX_PACK, 128),
            shape(MX_PACK, 128),
        ],
        scratch=[pltpu.VMEM((size + 64, 128), F32)],
        n_in=2 + n_z + len(gathered),
    )(pack, *got_z, coarse_inverse, *gathered)
    got_x = swap("gx", px, qx)
    mid_planes, columns, py, qy = call(
        mid_y_body,
        [
            shape(COMPS * 8, 8, MID_LANES),
            shape(40, MID_LANES),
            shape(MY_PACK, 128),
            shape(MY_PACK, 128),
        ],
        n_in=4,
    )(mid_planes, column, *got_x)
    got_y = swap("gy", py, qy, closed=False)
    precond, operated, sums = finish_call(n_all)(
        mid_planes, columns, *got_y, s0, s1, e, c1, w, em, em_side, c1m, wm,
        prev_direction, prev_image, residual,
    )
    precond, operated = in_vmem(precond), in_vmem(operated)
    sums = lax.all_to_all(sums, ALL, 0, 0, tiled=True)
    return tuple(
        call(
            last_body,
            [block] * 4,
            scratch=[
                pltpu.VMEM((4, COMPS, X, Y, Z), F32),
                pltpu.SemaphoreType.DMA((4, X // STEP)),
            ],
            n_in=8,
            smem=(0,),
            hbm_out=(0, 1, 2, 3),
        )(
            prev_rz.reshape(1), sums, precond, operated, prev_direction, prev_image, solution, residual
        )
    )


def solution(mesh):
    field = P(None, "gx", "gy", "gz")
    return jax.shard_map(
        on_device,
        mesh=mesh,
        in_specs=(
            field,
            field,
            field,
            field,
            P(),
            P("gx", "gy", "gz"),
            P(),
            P("gx", "gy", None, None),
        ),
        out_specs=(field, field, field, field),
        check_vma=False,
    )
```

```python
import functools
import math

import jax
import jax.numpy as jnp
from jax import lax
from jax.experimental import pallas as pl
from jax.experimental.pallas import tpu as pltpu
from jax.sharding import PartitionSpec as P

X, Y, Z = 8, 8, 256
COMPS = 3
RIM = 4
WIDE = 6
ROWS = Y + 2 * RIM
LANES = Z + 128
MID_LANES = Z // 2 + 128
DAMPING = 0.6
COUPLING = (1.6, 0.7, 0.7)
ALL = ("gx", "gy", "gz")
F32 = jnp.float32
VMEM = pl.BlockSpec(memory_space=pltpu.VMEM)
SMEM = pl.BlockSpec(memory_space=pltpu.SMEM)
HBM = pl.BlockSpec(memory_space=pltpu.HBM)


def shape(*dims):
    return jax.ShapeDtypeStruct(dims, F32)


def call(body, outs, scratch=(), n_in=0, smem=(), hbm=(), hbm_out=(), vmem=16 << 20):
    return pl.pallas_call(
        body,
        out_shape=outs,
        in_specs=[SMEM if i in smem else HBM if i in hbm else VMEM for i in range(n_in)],
        out_specs=[HBM if i in hbm_out else VMEM for i in range(len(outs))],
        scratch_shapes=list(scratch),
        compiler_params=pltpu.CompilerParams(vmem_limit_bytes=vmem),
    )


def in_hbm(a):
    return pltpu.with_memory_space_constraint(a, pltpu.HBM)


def in_vmem(a):
    return pltpu.with_memory_space_constraint(a, pltpu.VMEM)


def pairs(count, odd, closed):
    if not odd:
        return [(i, i ^ 1) for i in range(count)]
    made = [(i, (i + 1) % count if i % 2 else (i - 1) % count) for i in range(count)]
    return made if closed else made[1:-1]


def swap(axis, even_pack, odd_pack, closed=True):
    count = lax.axis_size(axis)
    got_even = lax.ppermute(even_pack, axis, pairs(count, False, closed))
    if count == 2:
        return [got_even]
    return [got_even, lax.ppermute(odd_pack, axis, pairs(count, True, closed))]


def swap_yz(even_packs, odd_packs):
    count_y, count_z = lax.axis_size("gy"), lax.axis_size("gz")
    got = []
    for odd_z in range(len(even_packs)):
        found = []
        for odd_y, packs in enumerate((even_packs, odd_packs)):
            pairs_z = pairs(count_z, odd_z, True)
            made = [
                (a * count_z + c, b * count_z + d)
                for a, b in pairs(count_y, odd_y, False)
                for c, d in pairs_z
            ]
            found.append(lax.ppermute(packs[odd_z], ("gy", "gz"), made))
        got.append(found)
    return got


def is_even(axis):
    return lax.rem(lax.axis_index(axis), 2) == 0


def inner(axis):
    index = lax.axis_index(axis)
    return jnp.logical_and(index > 0, index < lax.axis_size(axis) - 1)


def from_sides(got, axis):
    even = is_even(axis)
    if len(got) == 1:

        def lower(key):
            value = got[0][key]
            return jnp.where(even, 0.0, value)

        def upper(key):
            value = got[0][key]
            return jnp.where(even, value, 0.0)

        return lower, upper
    ok = inner(axis)

    def lower(key):
        return jnp.where(even, jnp.where(ok, got[1][key], 0.0), got[0][key])

    def upper(key):
        return jnp.where(even, got[0][key], jnp.where(ok, got[1][key], 0.0))

    return lower, upper


def tri_y(a):
    a = a + pltpu.roll(a, 1, 0)
    return a + pltpu.roll(a, a.shape[0] - 1, 0)


def tri_y_with(a, below, above, last):
    rows = a.shape[0]
    row = row_of(a.shape)
    former = jnp.where(row == last + 1, below, pltpu.roll(a, 1, 0))
    after = jnp.where(row == last, above, pltpu.roll(a, rows - 1, 0))
    return former + after + (a + a)


def mixed_z(e, e_next, e_last, v, ev):
    both = e * v + ev
    moved = pltpu.roll(e_next * v + ev, 1, 1) + pltpu.roll(e_last * v + ev, v.shape[1] - 1, 1)
    return moved + (both + both)


def tri_x(before, centre, after):
    return before + after + (centre + centre)


def tri_x_pair(a, b, c, d):
    near = b + c
    return (a + b) + near, near + (c + d)


def tri_rows(a, below=None, above=None):
    even, odd = a[:8], a[8:]
    former, after = pltpu.roll(odd, 1, 0), pltpu.roll(even, 7, 0)
    if below is not None:
        row = row_of(even.shape)
        former = jnp.where(row == 6, below, former)
        after = jnp.where(row == 5, above, after)
    both = even + odd
    return jnp.concatenate([both + (even + former), both + (odd + after)], axis=0)


def tree_sum(terms):
    while len(terms) > 1:
        terms = [sum(terms[k : k + 2]) for k in range(0, len(terms), 2)]
    return terms[0]


def to_modes(v0, v1, v2):
    total = v0 + v1 + v2
    third = total * (1.0 / 3.0)
    return total, v0 - third, v1 - third


def from_modes(total, a, b):
    third = total * (1.0 / 3.0)
    return a + third, b + third, third - a - b


def row_of(shape):
    return lax.broadcasted_iota(jnp.int32, shape, 0)


def lane_of(shape):
    return lax.broadcasted_iota(jnp.int32, shape, 1)


def up(a, shift):
    shift %= a.shape[0]
    return pltpu.roll(a, shift, 0) if shift else a


def pool_matrix(value):
    lane = row_of((LANES, MID_LANES))
    mid = jnp.where(lane < Z + 64, lane // 2, lane // 2 + 64)
    return jnp.where(mid == lane_of((LANES, MID_LANES)), value, 0.0).astype(F32)


def spread_matrix():
    lane = lane_of((MID_LANES, LANES))
    mid = jnp.where(lane < Z + 64, lane // 2, lane // 2 + 64)
    return jnp.where(mid == row_of((MID_LANES, LANES)), 1.0, 0.0).astype(F32)


def dot_exact_weights(a, b):
    b = b.astype(jnp.bfloat16)
    total = None
    for k in range(3):
        part = a.astype(jnp.bfloat16)
        found = jnp.dot(part, b, preferred_element_type=F32)
        total = found if total is None else total + found
        if k < 2:
            a = a - part.astype(F32)
    return total


X_PACK = COMPS * RIM + WIDE
R_TILES = COMPS * X
E_PLANES = X + 2 * WIDE
E4_TILES = E_PLANES // 2
E2_TILES = E_PLANES // 4
Y_PACK = R_TILES + E4_TILES + E2_TILES
Z_TILES = COMPS * (X + 2 * RIM) + E_PLANES
Z_PACK = -(-Z_TILES // 16) * 8
YZ_PACK = -(-Y_PACK // 16) * 8


def pack_x_body(
    table_in, index_in, res_in, res, young, pack_even, pack_odd, table, index, res_n, young_n, sems
):
    copies = [
        pltpu.make_async_copy(table_in, table, sems.at[0]),
        pltpu.make_async_copy(index_in, index, sems.at[1]),
    ]
    for k in range(2):
        source = res_in.at[:, :, :, pl.ds(128 * k, 128)]
        copies.append(pltpu.make_async_copy(source, res_n.at[k], sems.at[2 + k]))
    for copy in copies:
        copy.start()
    copies[0].wait()
    copies[1].wait()
    levels = index[...]
    value = jnp.zeros(levels.shape, F32)
    for level in range(table.shape[0]):
        value = jnp.where(levels == level, table[level], value)

    def own_tile(ref, *at):
        rows = [ref[(*at, pl.ds(start, 4, stride=2), slice(None))] for start in (0, 1)]
        return jnp.concatenate(rows, axis=0)

    for k in range(2):
        young_n[k] = value[:, :, 128 * k : 128 * k + 128]
    for k in range(2):
        for x in range(X):
            young[x, :, 128 * k : 128 * k + 128] = own_tile(young_n, k, x)
    for k in range(2):
        copies[2 + k].wait()
        for x in range(X):
            modes = to_modes(*[own_tile(res_n, k, c, x) for c in range(COMPS)])
            for c in range(COMPS):
                res[c, x, :, 128 * k : 128 * k + 128] = modes[c]
    high_first = jnp.where(is_even("gx"), 1, 0)
    for pack, high in ((pack_even, high_first), (pack_odd, 1 - high_first)):
        for c in range(COMPS):
            pack[c * RIM : (c + 1) * RIM] = res[c, pl.ds(high * (X - RIM), RIM)]
        pack[COMPS * RIM :] = young[pl.ds(high * (X - WIDE), WIDE)]


def x_planes(res, young, got_x):
    lower, upper = from_sides(got_x, "gx")
    whole = lanes = slice(None)

    def res_plane(c, i):
        if i < RIM:
            return lower((c * RIM + i, whole, lanes))
        if i < RIM + X:
            return res[c, i - RIM, :, lanes]
        return upper((c * RIM + i - RIM - X, whole, lanes))

    def young_plane(i):
        if i < WIDE:
            return lower((COMPS * RIM + i, whole, lanes))
        if i < WIDE + X:
            return young[i - WIDE, :, lanes]
        return upper((COMPS * RIM + i - WIDE - X, whole, lanes))

    return res_plane, young_plane


def pack_lanes(pack, tiles, high):
    lane = lane_of((8, 128))
    for first in range(0, len(tiles), 16):
        packed = None
        for j, tile in enumerate(tiles[first : first + 16]):
            edge = jnp.where(high == 1, tile[:, Z - 128 :], tile[:, :128])
            moved = pltpu.roll(edge, lax.rem(8 * j + 8 * high, 128), 1)
            packed = moved if j == 0 else jnp.where(lane < 8 * j, packed, moved)
        pack[first // 2 : first // 2 + 8] = packed


def pack_y_body(res, young, got_a, got_b, pack_even, pack_odd):
    res_plane, young_plane = x_planes(res, young, (got_a, got_b))
    row = row_of((Y, Z))
    even = is_even("gy")


    def put(tile, low, high):
        pack_even[tile] = jnp.where(even, high, low)
        pack_odd[tile] = jnp.where(even, low, high)

    def halves(tile, a, b):
        put(
            tile,
            jnp.where(row % 4 < 2, a, up(b, 2)),
            jnp.where(row % 4 < 2, up(a, -2), b),
        )

    for c in range(COMPS):
        for i in range(X):
            halves(c * X + i, res_plane(c, i), res_plane(c, i + X))
    planes = [young_plane(i) for i in range(E_PLANES)]
    for i in range(E4_TILES):
        halves(R_TILES + i, planes[i], planes[i + E4_TILES])
    for j in range(E2_TILES):
        low = high = None
        for k in range(4):
            plane = planes[4 * j + k]
            a, b = up(plane, k - 2), up(plane, k - 1)
            low = a if k == 0 else jnp.where(row % 4 == k, a, low)
            high = b if k == 0 else jnp.where(row % 4 == k, b, high)
        put(R_TILES + E4_TILES + j, low, high)


def pack_z_body(n_z, res, young, got_a, got_b, sent_even, sent_odd, *packs):
    res_plane, young_plane = x_planes(res, young, (got_a, got_b))
    own = [res_plane(c, i) for c in range(COMPS) for i in range(X + 2 * RIM)]
    own += [young_plane(i) for i in range(E_PLANES)]
    high_first = jnp.where(is_even("gz"), 1, 0)
    for k, high in enumerate((high_first, 1 - high_first)[:n_z]):
        pack_lanes(packs[k], own, high)
        for y, sent in enumerate((sent_even, sent_odd)):
            pack_lanes(packs[n_z * (1 + y) + k], [sent[t] for t in range(Y_PACK)], high)


def y_tiles(res_plane, young_plane, lower, upper, width):
    row = row_of((Y, width))

    def with_rims(own, tile, second):
        low, high = lower(tile), upper(tile)
        at = 2 if second else 0
        even = jnp.where(row < 6, up(high, 4 - at), up(low, 6 - at))
        odd = jnp.where(row < 6, up(high, -at), up(low, 2 - at))
        return [jnp.where(row < 4, own, even), jnp.where(row < 4, up(own, 4), odd)]

    def res_tiles(c, i):
        return with_rims(res_plane(c, i), c * X + i % X, i >= X)

    def young_tiles(i):
        two = R_TILES + E4_TILES + i // 4
        k = i % 4
        low2, high2 = up(lower(two), -k), up(upper(two), 1 - k)
        side = jnp.where(row % 4 == 0, low2, jnp.where(row % 4 == 1, high2, 0.0))
        return with_rims(young_plane(i), R_TILES + i % E4_TILES, i >= E4_TILES) + [side]

    return res_tiles, young_tiles


def z_rims(sources):
    lane = lane_of((8, 128))
    even = is_even("gz")

    def piece(source, t, right):
        start = jnp.where(right, 0, 120)
        tile = source((slice(8 * (t // 16), 8 * (t // 16) + 8), slice(None)))
        moved = pltpu.roll(tile, lax.rem(start + 128 - 8 * (t % 16), 128), 1)
        inside = jnp.logical_and(lane >= start, lane < start + 8)
        return jnp.where(inside, moved, 0.0)

    def rim(t):
        first = piece(sources[0], t, even)
        if len(sources) == 1:
            return first
        second = piece(sources[1], t, jnp.logical_not(even))
        return first + jnp.where(inner("gz"), second, 0.0)

    return rim


M_PLANES = X // 2 + 4
EM_PLANES = X // 2 + 6
LOW_TILE = COMPS * (X // 2)
MZ_PACK = (LOW_TILE + 1) * 8


def fine_parts(s, es, c1, e, i):
    found = []
    for c in range(COMPS):
        v = tri_x_pair(*[s[c, i + k] for k in range(-1, 3)])
        ev = tri_x_pair(*[es[c, i + k] for k in range(-1, 3)])
        found.append(
            [
                c1[i + k] * s[c, i + k]
                - mixed_z(e[0, i + k], e[1, i + k], e[2, i + k], tri_rows(v[k]), tri_rows(ev[k]))
                for k in range(2)
            ]
        )
    return found


def sweep(source, e_source, target, e_target, s0, c1, e, w, first, last):
    def body(n, carry):
        i = first + 2 * n
        parts = fine_parts(source, e_source, c1, e, i)
        for k in range(2):
            for c in range(COMPS):
                factor = w[0 if c == 0 else 1, i + k]
                value = (source[c, i + k] + s0[c, i + k]) - factor * parts[c][k]
                target[c, i + k] = value
                e_target[c, i + k] = e[0, i + k] * value
        return carry

    lax.fori_loop(0, (last - first) // 2, body, 0, unroll=True)


def smooth_body(n_z, *refs):
    n_in = 6 + 3 * n_z
    res, young, xa, xb, ya, yb = refs[:6]
    got_z = refs[6 : 6 + n_z]
    got_yz = [refs[6 + n_z + 2 * k : 8 + n_z + 2 * k] for k in range(n_z)]
    s0, s1, e, c1, w, em, em_side, c1m, wm, pack = refs[n_in : n_in + 10]
    wide, wide_z, r, es0, es1, to_pool = refs[n_in + 10 :]

    whole = slice(None)
    lower, upper = from_sides((ya, yb), "gy")
    res_tiles, young_tiles = y_tiles(
        *x_planes(res, young, (xa, xb)),
        lambda t: lower((t, whole, whole)),
        lambda t: upper((t, whole, whole)),
        Z,
    )
    own_rim = z_rims([functools.partial(lambda ref, key: ref[key], ref) for ref in got_z])
    corners = [from_sides(got, "gy") for got in got_yz]
    res_rims, young_rims = y_tiles(
        lambda c, i: own_rim(c * PLANES + i),
        lambda i: own_rim(COMPS * PLANES + i),
        z_rims([low for low, _ in corners]),
        z_rims([high for _, high in corners]),
        128,
    )
    for c in range(COMPS):
        for i in range(PLANES):
            for t, (tile, rim) in enumerate(zip(res_tiles(c, i), res_rims(c, i))):
                r[c, i, 8 * t : 8 * t + 8, :Z] = tile
                r[c, i, 8 * t : 8 * t + 8, Z:] = rim
    for i in range(E_PLANES):
        for t, (tile, rim) in enumerate(zip(young_tiles(i), young_rims(i))):
            wide[i, 8 * t : 8 * t + 8, :Z] = tile * 0.0125
            wide[i, 8 * t : 8 * t + 8, Z:] = rim * 0.0125

    def shift(k, carry):
        for i in (2 * k, 2 * k + 1):
            centre = wide[i]
            after, before = pltpu.roll(centre, LANES - 1, 1), pltpu.roll(centre, 1, 1)
            wide_z[i] = after + before + (centre + centre)
            e[0, i] = centre[:ROWS]
            e[1, i] = after[:ROWS]
            e[2, i] = before[:ROWS]
        total = wide[2 * k] + wide[2 * k + 1]
        side = total[ROWS:]
        start = pl.multiple_of(COMPS * 6 * 8 + 16 * k, 16)
        to_pool[pl.ds(start, 8)] = total[:8] + total[8:ROWS]
        to_pool[pl.ds(start + 8, 8)] = side + up(side, 4)
        return carry

    lax.fori_loop(0, E_PLANES // 2, shift, 0, unroll=5)

    def prepare(k, carry):
        for i in (2 * k, 2 * k + 1):
            total = tri_x(wide_z[i + 1], wide_z[i + 2], wide_z[i + 3])
            side = total[ROWS:]
            total = tri_rows(total[:ROWS], up(side, 2), up(side, 4))
            centre = e[0, i + 2]
            c1[i] = 72.0 * centre + total
            inverse = jnp.where(centre > 0.0, DAMPING / (56.0 * centre + total), 0.0)
            for n in range(2):
                w[n, i] = COUPLING[n] * inverse
            for c in range(COMPS):
                value = inverse * r[c, i]
                s0[c, i] = value
                es0[c, i] = centre * value
        return carry

    lax.fori_loop(0, PLANES // 2, prepare, 0, unroll=True)
    e = e.at[:, 2 : 2 + PLANES]
    sweep(s0, es0, s1, es1, s0, c1, e, w, 1, PLANES - 1)

    def residue(m, carry):
        i = 2 * m + 2
        parts = fine_parts(s1, es1, c1, e, i)
        for c in range(COMPS):
            total = (r[c, i] + r[c, i + 1]) - COUPLING[c] * (parts[c][0] + parts[c][1])
            start = pl.multiple_of((c * 6 + m) * 8, 8)
            to_pool[pl.ds(start, 8)] = total[:8] + total[8:]
        return carry

    lax.fori_loop(0, 6, residue, 0, unroll=True)

    pooled = dot_exact_weights(to_pool[...], pool_matrix(0.5))
    pooled = [pooled[8 * t : 8 * t + 8] for t in range(COMPS * 6 + 2 * EM_PLANES)]
    for m in range(EM_PLANES):
        centre = 0.25 * pooled[COMPS * 6 + 2 * m]
        em[0, m] = centre
        em[1, m] = pltpu.roll(centre, MID_LANES - 1, 1)
        em[2, m] = pltpu.roll(centre, 1, 1)
        em_side[m] = 0.25 * pooled[COMPS * 6 + 2 * m + 1]
    for m in range(M_PLANES):
        total = tri_x(*[em[0, m + k] for k in range(3)])
        side = tri_x(*[em_side[m + k] for k in range(3)])
        total = tri_y_with(total, up(side, 6), up(side, 4), 5)
        total = total + total + pltpu.roll(total, 1, 1) + pltpu.roll(total, MID_LANES - 1, 1)
        centre = em[0, m + 1]
        c1m[m] = 72.0 * centre + total
        wm[m] = jnp.where(centre > 0.0, DAMPING / (56.0 * centre + total), 0.0)

    rhs, mid, e_mid = {}, {}, {}
    for m in range(6):
        for c in range(COMPS):
            rhs[c, m] = pooled[c * 6 + m]
            mid[c, m] = wm[m + 1] * rhs[c, m]
            e_mid[c, m] = em[0, m + 2] * mid[c, m]
    kept = {}
    for m in range(1, 5):
        for c in range(COMPS):
            v = tri_y(tri_x(mid[c, m - 1], mid[c, m], mid[c, m + 1]))
            ev = tri_y(tri_x(e_mid[c, m - 1], e_mid[c, m], e_mid[c, m + 1]))
            mixed = mixed_z(em[0, m + 2], em[1, m + 2], em[2, m + 2], v, ev)
            left_over = rhs[c, m] - COUPLING[c] * (c1m[m + 1] * mid[c, m] - mixed)
            kept[c, m - 1] = left_over
            value = mid[c, m] + wm[m + 1] * left_over
            tile = c * 4 + m - 1
            pack[8 * tile : 8 * tile + 8] = value[:, :128]
    rows = {}
    for b in range(2):
        found = from_modes(*[kept[c, 2 * b] + kept[c, 2 * b + 1] for c in range(COMPS)])
        for c in range(COMPS):
            rows[c, b] = found[c]
    stacked = jnp.concatenate([rows[c, b] for c in range(COMPS) for b in range(2)], axis=0)
    lane_box = row_of((MID_LANES, 128))
    column = lane_of((MID_LANES, 128))
    boxes = jnp.where(
        jnp.logical_and(lane_box < Z // 2, lane_box // 64 == column % 2), 1.0, 0.0
    ).astype(F32)
    sums = dot_exact_weights(stacked, boxes)
    line = row_of((48, 128))
    entry = lane_of((48, 128))
    inside = line % 8
    match = jnp.logical_and((line // 8) * 2 + inside // 2 == entry // 2, inside < 4)
    scale = 1.0 / math.sqrt((X // 4) * (Y // 4) * (Z // 4))
    low = jnp.sum(jnp.where(match, sums, 0.0), axis=0, keepdims=True) * scale
    pack[8 * LOW_TILE :] = jnp.broadcast_to(low, (8, 128))


def pack_mid(pack, tiles):
    lane = lane_of((8, 128))
    rims = None
    for n, tile in enumerate(tiles):
        pack[8 * n : 8 * n + 8] = tile[:, :128]
        moved = pltpu.roll(tile[:, 128:], 4 + 8 * n, 1)
        rims = moved if n == 0 else jnp.where(lane < 8 * n, rims, moved)
    pack[8 * len(tiles) :] = rims


def unpack_mid(side, count):
    lane = lane_of((8, 128))
    near = jnp.logical_or(lane < 4, lane >= 124)
    rims = side((slice(8 * count, 8 * count + 8), slice(None)))
    tiles = []
    for n in range(count):
        main = side((slice(8 * n, 8 * n + 8), slice(None)))
        rim = jnp.where(near, pltpu.roll(rims, 124 - 8 * n, 1), 0.0)
        tiles.append(jnp.concatenate([main, rim], axis=1))
    return tiles


def coarse_body(n_z, *refs):
    pack = refs[0]
    got_z = refs[1 : 1 + n_z]
    matrix = refs[1 + n_z]
    gathered = refs[2 + n_z : -5]
    planes, column, pack_even, pack_odd, scratch = refs[-5:]
    place = lax.axis_index("gz")
    left, right = from_sides(got_z, "gz")
    lane = lane_of((8, 128))
    for t in range(LOW_TILE):
        key = (slice(8 * t, 8 * t + 8), slice(None))
        planes[t, :, :128] = pack[key]
        planes[t, :, 128:] = jnp.where(lane < 64, right(key), left(key))

    size = 24
    if gathered:
        rhs = gathered[0][...]
    else:
        mine = pack[8 * LOW_TILE : 8 * LOW_TILE + 8]
        other = got_z[0][8 * LOW_TILE : 8 * LOW_TILE + 8]
        first = jnp.where(place == 0, mine, other)
        second = jnp.where(place == 0, other, mine)
        rhs = jnp.where(lane < size, first, pltpu.roll(second, size, 1))[:1, : 2 * size]
    solved = jnp.sum(matrix[0, 0] * rhs, axis=1, keepdims=True)
    scratch[...] = jnp.zeros(scratch.shape, F32)
    scratch[size : size + solved.shape[0]] = jnp.broadcast_to(solved, (solved.shape[0], 128))
    base = pl.multiple_of(place * size, 8)
    wide = lane_of((16, MID_LANES))
    before, own_a, own_b, after = [
        jnp.concatenate([scratch[pl.ds(base + at, 16, stride=2)]] * 2, axis=1)
        for at in (1, size, size + 1, 2 * size)
    ]
    value = jnp.where(wide < 64, own_a, own_b)
    value = jnp.where(wide < 128, value, jnp.where(wide < 192, after, before))
    row = row_of((8, MID_LANES))
    first, second, third = value[:8], up(value[:8], 4), value[8:]
    total, a, b = to_modes(first, second, third)
    rest = [jnp.where(row < 4, total, up(a, 4)), jnp.where(row < 4, b, 0.0)]
    column[:8] = rest[0]
    column[8:] = rest[1]

    even = is_even("gx")
    low, high = [
        [jnp.where(row < 4, planes[c * 4 + p], up(planes[c * 4 + p + 1], 4)) for c in range(COMPS)]
        for p in (0, 2)
    ]
    pack_mid(pack_even, [jnp.where(even, b, a) for a, b in zip(low, high)] + rest)
    pack_mid(pack_odd, [jnp.where(even, a, b) for a, b in zip(low, high)] + rest)


MX_TILES = COMPS + 2
MY_TILES = 2 * COMPS + 5
MX_PACK = (MX_TILES + 1) * 8
MY_PACK = (MY_TILES + 1) * 8


def mid_y_body(planes, column, got_a, got_b, wide_planes, columns, pack_even, pack_odd):
    lower, upper = from_sides((got_a, got_b), "gx")
    low_tiles, high_tiles = unpack_mid(lower, MX_TILES), unpack_mid(upper, MX_TILES)
    row = row_of((8, MID_LANES))
    even = is_even("gy")
    below_packs, above_packs = [], []
    for c in range(COMPS):
        tiles = [low_tiles[c], up(low_tiles[c], 4)]
        tiles += [planes[c * 4 + p] for p in range(4)]
        tiles += [high_tiles[c], up(high_tiles[c], 4)]
        for t in range(8):
            wide_planes[c * 8 + t] = tiles[t]
        for h in range(2):
            below = above = None
            for k in range(4):
                tile = tiles[4 * h + k]
                a, b = up(tile, 2 * k), up(tile, 2 * k - 2)
                below = a if k == 0 else jnp.where(row < 2 * k, below, a)
                above = b if k == 0 else jnp.where(row < 2 * k, above, b)
            below_packs.append(below)
            above_packs.append(above)
    columns[:8] = low_tiles[COMPS]
    columns[8:12] = low_tiles[COMPS + 1][:4]
    columns[12:24] = column[:12]
    columns[24:32] = high_tiles[COMPS]
    columns[32:36] = high_tiles[COMPS + 1][:4]
    columns[36:] = jnp.zeros((4, MID_LANES), F32)
    rest = [columns[8 * t : 8 * t + 8] for t in range(5)]
    pairs_of = list(zip(below_packs, above_packs))
    pack_mid(pack_even, [jnp.where(even, a, b) for b, a in pairs_of] + rest)
    pack_mid(pack_odd, [jnp.where(even, b, a) for b, a in pairs_of] + rest)


def finish_body(
    wide_planes, columns, got_a, got_b, s0, s1, e_all, c1, w, em, em_side, c1m, wm, prev_d, prev_i,
    res, precond, operated, sums, cor, cor_side, mid, fine, s2, es2, s3, es3, p, ep,
):
    e = e_all.at[:, 2 : 2 + PLANES]
    lower, upper = from_sides((got_a, got_b), "gy")
    row = row_of((8, MID_LANES))

    low_tiles, high_tiles = unpack_mid(lower, MY_TILES), unpack_mid(upper, MY_TILES)
    below = jnp.concatenate(low_tiles[2 * COMPS :], axis=0)
    above = jnp.concatenate(high_tiles[2 * COMPS :], axis=0)
    middle = columns[...]
    for c in range(COMPS):
        for b in range(6):
            at = (b // 2) * 12 + c * 4 + (b % 2) * 2

            def band(source, by):
                return jnp.broadcast_to(source[at + by : at + by + 1], (8, MID_LANES))

            field = jnp.where(row < 6, band(above, 0), band(below, 1))
            field = jnp.where(row < 4, band(middle, 1), field)
            cor[c, b] = jnp.where(row < 2, band(middle, 0), field)
            cor_side[c, b] = jnp.where(row == 0, band(below, 0), band(above, 1))

    def box(m):
        return (m + 1) // 2

    for m in range(M_PLANES):
        for c in range(COMPS):
            near = [cor[c, box(m + k)] for k in range(3)]
            near_side = [cor_side[c, box(m + k)] for k in range(3)]
            e_near = [em[0, m + k] * near[k] for k in range(3)]
            e_side = [em_side[m + k] * near_side[k] for k in range(3)]
            side = tri_x(*near_side)
            v = tri_y_with(tri_x(*near), up(side, 6), up(side, 4), 5)
            side = tri_x(*e_side)
            ev = tri_y_with(tri_x(*e_near), up(side, 6), up(side, 4), 5)
            mixed = mixed_z(em[0, m + 1], em[1, m + 1], em[2, m + 1], v, ev)
            applied = COUPLING[c] * (c1m[m] * near[1] - mixed)
            tile = wide_planes[c * 8 + m]
            n, k = c * 2 + m // 4, m % 4
            outer = jnp.where(row < 6, up(high_tiles[n], 4 - 2 * k), up(low_tiles[n], 6 - 2 * k))
            tile = jnp.where(row < 4, tile, outer)
            at = (c * 8 + m) * 8
            mid[at : at + 8] = tile + cor[c, box(m + 1)] - wm[m] * applied
    fine[...] = dot_exact_weights(mid[...], spread_matrix())

    def add_up(i, carry):
        for c in range(COMPS):
            at = pl.multiple_of((c * 8 + i // 2) * 8, 8)
            more = fine[pl.ds(at, 8)]
            value = s1[c, i] + jnp.concatenate([more, more], axis=0)
            s2[c, i] = value
            es2[c, i] = e[0, i] * value
        return carry

    lax.fori_loop(1, PLANES - 1, add_up, 0, unroll=2)
    sweep(s2, es2, s3, es3, s0, c1, e, w, 2, PLANES - 2)
    sweep(s3, es3, p, ep, s0, c1, e, w, 3, PLANES - 3)

    def put_rows(target, x, modes):
        for half in range(2):
            for c, value in enumerate(from_modes(*[m[8 * half : 8 * half + 8, :Z] for m in modes])):
                for k in range(Z // 128):
                    part = value[:4, 128 * k : 128 * k + 128]
                    target[x, c, k, pl.ds(half, 4, stride=2), :] = part

    def image(n, carry):
        i = 2 * n + RIM
        parts = fine_parts(p, ep, c1, e, i)
        for k in range(2):
            put_rows(precond, 2 * n + k, [p[c, i + k] for c in range(COMPS)])
            put_rows(operated, 2 * n + k, [COUPLING[c] * parts[c][k] for c in range(COMPS)])
        return carry

    lax.fori_loop(0, X // 2, image, 0, unroll=True)
    found = [[], [], [], []]
    for x in range(X):
        for c in range(COMPS):
            for k in range(Z // 128):
                lanes = slice(128 * k, 128 * k + 128)
                own_p, own_a = precond[x, c, k], operated[x, c, k]
                d, q = prev_d[c, x, :, lanes], prev_i[c, x, :, lanes]
                own_r = res[c, x, :, lanes]
                terms = (own_r * own_p, own_p * own_a, own_p * q + d * own_a, d * q)
                for kept, term in zip(found, terms):
                    kept.append(term)
    found = [tree_sum(kept) for kept in found]
    row = row_of((8, 128))
    total = jnp.zeros((8, 128), F32)
    for k, value in enumerate(found):
        line = jnp.sum(value, axis=0, keepdims=True)
        total = jnp.where(row == k, jnp.broadcast_to(line, (8, 128)), total)
    total = total + pltpu.roll(total, 64, 1)
    total = total + pltpu.roll(total, 32, 1)
    total = jnp.where(row == lane_of((8, 128)) // 32, total, 0.0)
    sums[...] = jnp.broadcast_to(jnp.sum(total, axis=0, keepdims=True), sums.shape)


STEP = 2


def last_body(
    prev_rz, sums, precond, operated, prev_d, prev_i, sol, res,
    new_s_out, new_r_out, new_d_out, new_i_out, news, out_sems,
):
    total = jnp.sum(sums[...], axis=0, keepdims=True)
    lane = lane_of((1, 128))

    def entry(k):
        return jnp.sum(jnp.where(lane // 32 == k, total, 0.0), axis=1, keepdims=True)

    rz = entry(0)
    beta = rz / prev_rz[0]
    alpha = rz / (entry(1) + beta * (entry(2) + beta * entry(3)))
    beta = jnp.broadcast_to(beta, (Y, 128))
    alpha = jnp.broadcast_to(alpha, (Y, 128))
    leaving = []
    for step in range(X // STEP):
        for x in range(step * STEP, step * STEP + STEP):
            for c in range(COMPS):
                for k in range(Z // 128):
                    at = (c, x, slice(None), slice(128 * k, 128 * k + 128))
                    d = precond[x, c, k] + beta * prev_d[at]
                    q = operated[x, c, k] + beta * prev_i[at]
                    news[(2, *at)] = d
                    news[(3, *at)] = q
                    news[(0, *at)] = sol[at] + alpha * d
                    news[(1, *at)] = res[at] - alpha * q
        part = pl.ds(step * STEP, STEP)
        for k, target in enumerate((new_s_out, new_r_out, new_d_out, new_i_out)):
            copy = pltpu.make_async_copy(
                news.at[k, :, part], target.at[:, part], out_sems.at[k, step]
            )
            copy.start()
            leaving.append(copy)
    for copy in leaving:
        copy.wait()


PLANES = X + 2 * RIM
FIELD = (COMPS, PLANES, ROWS, LANES)
COLS_SHAPE = (40, MID_LANES)


def smooth_outs():
    return [
        shape(*FIELD),
        shape(*FIELD),
        shape(3, E_PLANES, ROWS, LANES),
        shape(PLANES, ROWS, LANES),
        shape(2, PLANES, ROWS, LANES),
        shape(3, EM_PLANES, 8, MID_LANES),
        shape(EM_PLANES, 8, MID_LANES),
        shape(M_PLANES, 8, MID_LANES),
        shape(M_PLANES, 8, MID_LANES),
        shape(MZ_PACK, 128),
    ]


def smooth_call(n_z):
    return call(
        functools.partial(smooth_body, n_z),
        smooth_outs(),
        scratch=[
            pltpu.VMEM((E_PLANES, 24, LANES), F32),
            pltpu.VMEM((E_PLANES, 24, LANES), F32),
            pltpu.VMEM(FIELD, F32),
            pltpu.VMEM(FIELD, F32),
            pltpu.VMEM(FIELD, F32),
            pltpu.VMEM((COMPS * 6 * 8 + 16 * EM_PLANES, LANES), F32),
        ],
        n_in=6 + 3 * n_z,
        vmem=30 << 20,
    )


def finish_call(n_all):
    return call(
        finish_body,
        [pltpu.VMEM((X, COMPS, Z // 128, Y, 128), F32)] * 2 + [shape(n_all, 128)],
        scratch=[
            pltpu.VMEM((COMPS, 6, 8, MID_LANES), F32),
            pltpu.VMEM((COMPS, 6, 8, MID_LANES), F32),
            pltpu.VMEM((COMPS * 64, MID_LANES), F32),
            pltpu.VMEM((COMPS * 64, LANES), F32),
        ]
        + [pltpu.VMEM(FIELD, F32)] * 6,
        n_in=16,
        vmem=30 << 20,
    )


def on_device(
    solution,
    residual,
    prev_direction,
    prev_image,
    prev_rz,
    density_index,
    stiffness_table,
    coarse_inverse,
):
    if residual.shape != (COMPS, X, Y, Z):
        raise ValueError(residual.shape)
    block = shape(COMPS, X, Y, Z)
    n_z = 1 if lax.axis_size("gz") == 2 else 2
    n_all = lax.axis_size(ALL)

    res, young, px, qx = call(
        pack_x_body,
        [block, shape(X, Y, Z), shape(X_PACK, Y, Z), shape(X_PACK, Y, Z)],
        scratch=[
            pltpu.SMEM(stiffness_table.shape, F32),
            pltpu.VMEM((X, Y, Z), jnp.int32),
            pltpu.VMEM((2, COMPS, X, Y, 128), F32),
            pltpu.VMEM((2, X, Y, 128), F32),
            pltpu.SemaphoreType.DMA((4,)),
        ],
        n_in=3,
        hbm=(0, 1, 2),
    )(*[in_hbm(a) for a in (stiffness_table, density_index, residual)])
    got_x = swap("gx", px, qx)
    py, qy = call(pack_y_body, [shape(Y_PACK, Y, Z)] * 2, n_in=4)(res, young, *got_x)
    packs = call(
        functools.partial(pack_z_body, n_z),
        [shape(Z_PACK, 128)] * n_z + [shape(YZ_PACK, 128)] * (2 * n_z),
        n_in=6,
    )(res, young, *got_x, py, qy)
    got_y = swap("gy", py, qy, closed=False)
    got_z = swap("gz", packs[0], packs[n_z - 1])
    got_yz = swap_yz(packs[n_z : 2 * n_z], packs[2 * n_z :])
    corners = [got for both in got_yz for got in both]

    s0, s1, e, c1, w, em, em_side, c1m, wm, pack = smooth_call(n_z)(
        res, young, *got_x, *got_y, *got_z, *corners
    )

    got_z = swap("gz", pack, pack)
    gathered = []
    if n_z > 1:
        gathered = [lax.all_gather(pack[8 * LOW_TILE, :24], "gz", axis=0, tiled=True)[None]]
    size = coarse_inverse.shape[-1]
    mid_planes, column, px, qx = call(
        functools.partial(coarse_body, n_z),
        [
            shape(LOW_TILE, 8, MID_LANES),
            shape(16, MID_LANES),
            shape(MX_PACK, 128),
            shape(MX_PACK, 128),
        ],
        scratch=[pltpu.VMEM((size + 64, 128), F32)],
        n_in=2 + n_z + len(gathered),
    )(pack, *got_z, coarse_inverse, *gathered)
    got_x = swap("gx", px, qx)
    mid_planes, columns, py, qy = call(
        mid_y_body,
        [
            shape(COMPS * 8, 8, MID_LANES),
            shape(40, MID_LANES),
            shape(MY_PACK, 128),
            shape(MY_PACK, 128),
        ],
        n_in=4,
    )(mid_planes, column, *got_x)
    got_y = swap("gy", py, qy, closed=False)
    precond, operated, sums = finish_call(n_all)(
        mid_planes, columns, *got_y, s0, s1, e, c1, w, em, em_side, c1m, wm,
        prev_direction, prev_image, residual,
    )
    precond, operated = in_vmem(precond), in_vmem(operated)
    sums = lax.all_to_all(sums, ALL, 0, 0, tiled=True)
    return tuple(
        call(
            last_body,
            [block] * 4,
            scratch=[
                pltpu.VMEM((4, COMPS, X, Y, Z), F32),
                pltpu.SemaphoreType.DMA((4, X // STEP)),
            ],
            n_in=8,
            smem=(0,),
            hbm_out=(0, 1, 2, 3),
        )(
            prev_rz.reshape(1), sums, precond, operated, prev_direction, prev_image, solution, residual
        )
    )


def solution(mesh):
    field = P(None, "gx", "gy", "gz")
    return jax.shard_map(
        on_device,
        mesh=mesh,
        in_specs=(
            field,
            field,
            field,
            field,
            P(),
            P("gx", "gy", "gz"),
            P(),
            P("gx", "gy", None, None),
        ),
        out_specs=(field, field, field, field),
        check_vma=False,
    )
```

```python
import functools
import math

import jax
import jax.numpy as jnp
from jax import lax
from jax.experimental import pallas as pl
from jax.experimental.pallas import tpu as pltpu
from jax.sharding import PartitionSpec as P

X, Y, Z = 8, 8, 256
COMPS = 3
RIM = 4
WIDE = 6
ROWS = Y + 2 * RIM
LANES = Z + 128
MID_LANES = Z // 2 + 128
DAMPING = 0.6
COUPLING = (1.6, 0.7, 0.7)
ALL = ("gx", "gy", "gz")
F32 = jnp.float32
VMEM = pl.BlockSpec(memory_space=pltpu.VMEM)
SMEM = pl.BlockSpec(memory_space=pltpu.SMEM)
HBM = pl.BlockSpec(memory_space=pltpu.HBM)


def shape(*dims):
    return jax.ShapeDtypeStruct(dims, F32)


def call(body, outs, scratch=(), n_in=0, smem=(), hbm=(), hbm_out=(), vmem=16 << 20):
    return pl.pallas_call(
        body,
        out_shape=outs,
        in_specs=[SMEM if i in smem else HBM if i in hbm else VMEM for i in range(n_in)],
        out_specs=[HBM if i in hbm_out else VMEM for i in range(len(outs))],
        scratch_shapes=list(scratch),
        compiler_params=pltpu.CompilerParams(vmem_limit_bytes=vmem),
    )


def in_hbm(a):
    return pltpu.with_memory_space_constraint(a, pltpu.HBM)


def in_vmem(a):
    return pltpu.with_memory_space_constraint(a, pltpu.VMEM)


def pairs(count, odd, closed):
    if not odd:
        return [(i, i ^ 1) for i in range(count)]
    made = [(i, (i + 1) % count if i % 2 else (i - 1) % count) for i in range(count)]
    return made if closed else made[1:-1]


def swap(axis, even_pack, odd_pack, closed=True):
    count = lax.axis_size(axis)
    got_even = lax.ppermute(even_pack, axis, pairs(count, False, closed))
    if count == 2:
        return [got_even]
    return [got_even, lax.ppermute(odd_pack, axis, pairs(count, True, closed))]


def swap_yz(even_packs, odd_packs):
    count_y, count_z = lax.axis_size("gy"), lax.axis_size("gz")
    got = []
    for odd_z in range(len(even_packs)):
        found = []
        for odd_y, packs in enumerate((even_packs, odd_packs)):
            pairs_z = pairs(count_z, odd_z, True)
            made = [
                (a * count_z + c, b * count_z + d)
                for a, b in pairs(count_y, odd_y, False)
                for c, d in pairs_z
            ]
            found.append(lax.ppermute(packs[odd_z], ("gy", "gz"), made))
        got.append(found)
    return got


def is_even(axis):
    return lax.rem(lax.axis_index(axis), 2) == 0


def inner(axis):
    index = lax.axis_index(axis)
    return jnp.logical_and(index > 0, index < lax.axis_size(axis) - 1)


def from_sides(got, axis):
    even = is_even(axis)
    if len(got) == 1:

        def lower(key):
            value = got[0][key]
            return jnp.where(even, 0.0, value)

        def upper(key):
            value = got[0][key]
            return jnp.where(even, value, 0.0)

        return lower, upper
    ok = inner(axis)

    def lower(key):
        return jnp.where(even, jnp.where(ok, got[1][key], 0.0), got[0][key])

    def upper(key):
        return jnp.where(even, got[0][key], jnp.where(ok, got[1][key], 0.0))

    return lower, upper


def tri_y(a):
    a = a + pltpu.roll(a, 1, 0)
    return a + pltpu.roll(a, a.shape[0] - 1, 0)


def tri_y_with(a, below, above, last):
    rows = a.shape[0]
    row = row_of(a.shape)
    former = jnp.where(row == last + 1, below, pltpu.roll(a, 1, 0))
    after = jnp.where(row == last, above, pltpu.roll(a, rows - 1, 0))
    return former + after + (a + a)


def mixed_z(e, e_next, e_last, v, ev):
    both = e * v + ev
    moved = pltpu.roll(e_next * v + ev, 1, 1) + pltpu.roll(e_last * v + ev, v.shape[1] - 1, 1)
    return moved + (both + both)


def tri_x(before, centre, after):
    return before + after + (centre + centre)


def tri_x_pair(a, b, c, d):
    near = b + c
    return (a + b) + near, near + (c + d)


def tri_rows(a, below=None, above=None):
    even, odd = a[:8], a[8:]
    former, after = pltpu.roll(odd, 1, 0), pltpu.roll(even, 7, 0)
    if below is not None:
        row = row_of(even.shape)
        former = jnp.where(row == 6, below, former)
        after = jnp.where(row == 5, above, after)
    both = even + odd
    return jnp.concatenate([both + (even + former), both + (odd + after)], axis=0)


def tree_sum(terms):
    while len(terms) > 1:
        terms = [sum(terms[k : k + 2]) for k in range(0, len(terms), 2)]
    return terms[0]


def to_modes(v0, v1, v2):
    total = v0 + v1 + v2
    third = total * (1.0 / 3.0)
    return total, v0 - third, v1 - third


def from_modes(total, a, b):
    third = total * (1.0 / 3.0)
    return a + third, b + third, third - a - b


def row_of(shape):
    return lax.broadcasted_iota(jnp.int32, shape, 0)


def lane_of(shape):
    return lax.broadcasted_iota(jnp.int32, shape, 1)


def up(a, shift):
    shift %= a.shape[0]
    return pltpu.roll(a, shift, 0) if shift else a


def pool_matrix(value):
    lane = row_of((LANES, MID_LANES))
    mid = jnp.where(lane < Z + 64, lane // 2, lane // 2 + 64)
    return jnp.where(mid == lane_of((LANES, MID_LANES)), value, 0.0).astype(F32)


def spread_matrix():
    lane = lane_of((MID_LANES, LANES))
    mid = jnp.where(lane < Z + 64, lane // 2, lane // 2 + 64)
    return jnp.where(mid == row_of((MID_LANES, LANES)), 1.0, 0.0).astype(F32)


def dot_exact_weights(a, b):
    high = a.astype(jnp.bfloat16)
    low = (a - high.astype(F32)).astype(jnp.bfloat16)
    both = jnp.concatenate([high, low], axis=0)
    found = jnp.dot(both, b.astype(jnp.bfloat16), preferred_element_type=F32)
    return found[: a.shape[0]] + found[a.shape[0] :]


X_PACK = COMPS * RIM + WIDE
R_TILES = COMPS * X
E_PLANES = X + 2 * WIDE
E4_TILES = E_PLANES // 2
E2_TILES = E_PLANES // 4
Y_PACK = R_TILES + E4_TILES + E2_TILES
Z_TILES = COMPS * (X + 2 * RIM) + E_PLANES
Z_PACK = -(-Z_TILES // 16) * 8
YZ_PACK = -(-Y_PACK // 16) * 8


def pack_x_body(
    table_in, index_in, res_in, res, young, pack_even, pack_odd, table, index, res_n, young_n, sems
):
    copies = [
        pltpu.make_async_copy(table_in, table, sems.at[0]),
        pltpu.make_async_copy(index_in, index, sems.at[1]),
    ]
    for k in range(2):
        source = res_in.at[:, :, :, pl.ds(128 * k, 128)]
        copies.append(pltpu.make_async_copy(source, res_n.at[k], sems.at[2 + k]))
    for copy in copies:
        copy.start()
    copies[0].wait()
    copies[1].wait()
    levels = index[...]
    value = jnp.zeros(levels.shape, F32)
    for level in range(table.shape[0]):
        value = jnp.where(levels == level, table[level], value)

    def own_tile(ref, *at):
        rows = [ref[(*at, pl.ds(start, 4, stride=2), slice(None))] for start in (0, 1)]
        return jnp.concatenate(rows, axis=0)

    for k in range(2):
        young_n[k] = value[:, :, 128 * k : 128 * k + 128]
    for k in range(2):
        for x in range(X):
            young[x, :, 128 * k : 128 * k + 128] = own_tile(young_n, k, x)
    for k in range(2):
        copies[2 + k].wait()
        for x in range(X):
            modes = to_modes(*[own_tile(res_n, k, c, x) for c in range(COMPS)])
            for c in range(COMPS):
                res[c, x, :, 128 * k : 128 * k + 128] = modes[c]
    high_first = jnp.where(is_even("gx"), 1, 0)
    for pack, high in ((pack_even, high_first), (pack_odd, 1 - high_first)):
        for c in range(COMPS):
            pack[c * RIM : (c + 1) * RIM] = res[c, pl.ds(high * (X - RIM), RIM)]
        pack[COMPS * RIM :] = young[pl.ds(high * (X - WIDE), WIDE)]


def x_planes(res, young, got_x):
    lower, upper = from_sides(got_x, "gx")
    whole = lanes = slice(None)

    def res_plane(c, i):
        if i < RIM:
            return lower((c * RIM + i, whole, lanes))
        if i < RIM + X:
            return res[c, i - RIM, :, lanes]
        return upper((c * RIM + i - RIM - X, whole, lanes))

    def young_plane(i):
        if i < WIDE:
            return lower((COMPS * RIM + i, whole, lanes))
        if i < WIDE + X:
            return young[i - WIDE, :, lanes]
        return upper((COMPS * RIM + i - WIDE - X, whole, lanes))

    return res_plane, young_plane


def pack_lanes(pack, tiles, high):
    lane = lane_of((8, 128))
    for first in range(0, len(tiles), 16):
        packed = None
        for j, tile in enumerate(tiles[first : first + 16]):
            edge = jnp.where(high == 1, tile[:, Z - 128 :], tile[:, :128])
            moved = pltpu.roll(edge, lax.rem(8 * j + 8 * high, 128), 1)
            packed = moved if j == 0 else jnp.where(lane < 8 * j, packed, moved)
        pack[first // 2 : first // 2 + 8] = packed


def pack_y_body(res, young, got_a, got_b, pack_even, pack_odd):
    res_plane, young_plane = x_planes(res, young, (got_a, got_b))
    row = row_of((Y, Z))
    even = is_even("gy")


    def put(tile, low, high):
        pack_even[tile] = jnp.where(even, high, low)
        pack_odd[tile] = jnp.where(even, low, high)

    def halves(tile, a, b):
        put(
            tile,
            jnp.where(row % 4 < 2, a, up(b, 2)),
            jnp.where(row % 4 < 2, up(a, -2), b),
        )

    for c in range(COMPS):
        for i in range(X):
            halves(c * X + i, res_plane(c, i), res_plane(c, i + X))
    planes = [young_plane(i) for i in range(E_PLANES)]
    for i in range(E4_TILES):
        halves(R_TILES + i, planes[i], planes[i + E4_TILES])
    for j in range(E2_TILES):
        low = high = None
        for k in range(4):
            plane = planes[4 * j + k]
            a, b = up(plane, k - 2), up(plane, k - 1)
            low = a if k == 0 else jnp.where(row % 4 == k, a, low)
            high = b if k == 0 else jnp.where(row % 4 == k, b, high)
        put(R_TILES + E4_TILES + j, low, high)


def pack_z_body(n_z, res, young, got_a, got_b, sent_even, sent_odd, *packs):
    res_plane, young_plane = x_planes(res, young, (got_a, got_b))
    own = [res_plane(c, i) for c in range(COMPS) for i in range(X + 2 * RIM)]
    own += [young_plane(i) for i in range(E_PLANES)]
    high_first = jnp.where(is_even("gz"), 1, 0)
    for k, high in enumerate((high_first, 1 - high_first)[:n_z]):
        pack_lanes(packs[k], own, high)
        for y, sent in enumerate((sent_even, sent_odd)):
            pack_lanes(packs[n_z * (1 + y) + k], [sent[t] for t in range(Y_PACK)], high)


def y_tiles(res_plane, young_plane, lower, upper, width):
    row = row_of((Y, width))

    def with_rims(own, tile, second):
        low, high = lower(tile), upper(tile)
        at = 2 if second else 0
        even = jnp.where(row < 6, up(high, 4 - at), up(low, 6 - at))
        odd = jnp.where(row < 6, up(high, -at), up(low, 2 - at))
        return [jnp.where(row < 4, own, even), jnp.where(row < 4, up(own, 4), odd)]

    def res_tiles(c, i):
        return with_rims(res_plane(c, i), c * X + i % X, i >= X)

    def young_tiles(i):
        two = R_TILES + E4_TILES + i // 4
        k = i % 4
        low2, high2 = up(lower(two), -k), up(upper(two), 1 - k)
        side = jnp.where(row % 4 == 0, low2, jnp.where(row % 4 == 1, high2, 0.0))
        return with_rims(young_plane(i), R_TILES + i % E4_TILES, i >= E4_TILES) + [side]

    return res_tiles, young_tiles


def z_rims(sources):
    lane = lane_of((8, 128))
    even = is_even("gz")

    def piece(source, t, right):
        start = jnp.where(right, 0, 120)
        tile = source((slice(8 * (t // 16), 8 * (t // 16) + 8), slice(None)))
        moved = pltpu.roll(tile, lax.rem(start + 128 - 8 * (t % 16), 128), 1)
        inside = jnp.logical_and(lane >= start, lane < start + 8)
        return jnp.where(inside, moved, 0.0)

    def rim(t):
        first = piece(sources[0], t, even)
        if len(sources) == 1:
            return first
        second = piece(sources[1], t, jnp.logical_not(even))
        return first + jnp.where(inner("gz"), second, 0.0)

    return rim


M_PLANES = X // 2 + 4
EM_PLANES = X // 2 + 6
LOW_TILE = COMPS * (X // 2)
MZ_PACK = (LOW_TILE + 1) * 8


def fine_parts(s, es, c1, e, i):
    found = []
    for c in range(COMPS):
        v = tri_x_pair(*[s[c, i + k] for k in range(-1, 3)])
        ev = tri_x_pair(*[es[c, i + k] for k in range(-1, 3)])
        found.append(
            [
                c1[i + k] * s[c, i + k]
                - mixed_z(e[0, i + k], e[1, i + k], e[2, i + k], tri_rows(v[k]), tri_rows(ev[k]))
                for k in range(2)
            ]
        )
    return found


def sweep(source, e_source, target, e_target, s0, c1, e, w, first, last):
    def body(n, carry):
        i = first + 2 * n
        parts = fine_parts(source, e_source, c1, e, i)
        for k in range(2):
            for c in range(COMPS):
                factor = w[0 if c == 0 else 1, i + k]
                value = (source[c, i + k] + s0[c, i + k]) - factor * parts[c][k]
                target[c, i + k] = value
                e_target[c, i + k] = e[0, i + k] * value
        return carry

    lax.fori_loop(0, (last - first) // 2, body, 0, unroll=True)


def smooth_body(n_z, *refs):
    n_in = 6 + 3 * n_z
    res, young, xa, xb, ya, yb = refs[:6]
    got_z = refs[6 : 6 + n_z]
    got_yz = [refs[6 + n_z + 2 * k : 8 + n_z + 2 * k] for k in range(n_z)]
    s0, s1, e, c1, w, em, em_side, c1m, wm, pack = refs[n_in : n_in + 10]
    wide, wide_z, r, es0, es1, to_pool = refs[n_in + 10 :]

    whole = slice(None)
    lower, upper = from_sides((ya, yb), "gy")
    res_tiles, young_tiles = y_tiles(
        *x_planes(res, young, (xa, xb)),
        lambda t: lower((t, whole, whole)),
        lambda t: upper((t, whole, whole)),
        Z,
    )
    own_rim = z_rims([functools.partial(lambda ref, key: ref[key], ref) for ref in got_z])
    corners = [from_sides(got, "gy") for got in got_yz]
    res_rims, young_rims = y_tiles(
        lambda c, i: own_rim(c * PLANES + i),
        lambda i: own_rim(COMPS * PLANES + i),
        z_rims([low for low, _ in corners]),
        z_rims([high for _, high in corners]),
        128,
    )
    for c in range(COMPS):
        for i in range(PLANES):
            for t, (tile, rim) in enumerate(zip(res_tiles(c, i), res_rims(c, i))):
                r[c, i, 8 * t : 8 * t + 8, :Z] = tile
                r[c, i, 8 * t : 8 * t + 8, Z:] = rim
    for i in range(E_PLANES):
        for t, (tile, rim) in enumerate(zip(young_tiles(i), young_rims(i))):
            wide[i, 8 * t : 8 * t + 8, :Z] = tile * 0.0125
            wide[i, 8 * t : 8 * t + 8, Z:] = rim * 0.0125

    def shift(k, carry):
        for i in (2 * k, 2 * k + 1):
            centre = wide[i]
            after, before = pltpu.roll(centre, LANES - 1, 1), pltpu.roll(centre, 1, 1)
            wide_z[i] = after + before + (centre + centre)
            e[0, i] = centre[:ROWS]
            e[1, i] = after[:ROWS]
            e[2, i] = before[:ROWS]
        total = wide[2 * k] + wide[2 * k + 1]
        side = total[ROWS:]
        start = pl.multiple_of(COMPS * 6 * 8 + 16 * k, 16)
        to_pool[pl.ds(start, 8)] = total[:8] + total[8:ROWS]
        to_pool[pl.ds(start + 8, 8)] = side + up(side, 4)
        return carry

    lax.fori_loop(0, E_PLANES // 2, shift, 0, unroll=True)

    def prepare(k, carry):
        for i in (2 * k, 2 * k + 1):
            total = tri_x(wide_z[i + 1], wide_z[i + 2], wide_z[i + 3])
            side = total[ROWS:]
            total = tri_rows(total[:ROWS], up(side, 2), up(side, 4))
            centre = e[0, i + 2]
            c1[i] = 72.0 * centre + total
            inverse = jnp.where(centre > 0.0, DAMPING / (56.0 * centre + total), 0.0)
            for n in range(2):
                w[n, i] = COUPLING[n] * inverse
            for c in range(COMPS):
                value = inverse * r[c, i]
                s0[c, i] = value
                es0[c, i] = centre * value
        return carry

    lax.fori_loop(0, PLANES // 2, prepare, 0, unroll=True)
    e = e.at[:, 2 : 2 + PLANES]
    sweep(s0, es0, s1, es1, s0, c1, e, w, 1, PLANES - 1)

    def residue(m, carry):
        i = 2 * m + 2
        parts = fine_parts(s1, es1, c1, e, i)
        for c in range(COMPS):
            total = (r[c, i] + r[c, i + 1]) - COUPLING[c] * (parts[c][0] + parts[c][1])
            start = pl.multiple_of((c * 6 + m) * 8, 8)
            to_pool[pl.ds(start, 8)] = total[:8] + total[8:]
        return carry

    lax.fori_loop(0, 6, residue, 0, unroll=True)

    pooled = dot_exact_weights(to_pool[...], pool_matrix(0.5))
    pooled = [pooled[8 * t : 8 * t + 8] for t in range(COMPS * 6 + 2 * EM_PLANES)]
    for m in range(EM_PLANES):
        centre = 0.25 * pooled[COMPS * 6 + 2 * m]
        em[0, m] = centre
        em[1, m] = pltpu.roll(centre, MID_LANES - 1, 1)
        em[2, m] = pltpu.roll(centre, 1, 1)
        em_side[m] = 0.25 * pooled[COMPS * 6 + 2 * m + 1]
    for m in range(M_PLANES):
        total = tri_x(*[em[0, m + k] for k in range(3)])
        side = tri_x(*[em_side[m + k] for k in range(3)])
        total = tri_y_with(total, up(side, 6), up(side, 4), 5)
        total = total + total + pltpu.roll(total, 1, 1) + pltpu.roll(total, MID_LANES - 1, 1)
        centre = em[0, m + 1]
        c1m[m] = 72.0 * centre + total
        wm[m] = jnp.where(centre > 0.0, DAMPING / (56.0 * centre + total), 0.0)

    rhs, mid, e_mid = {}, {}, {}
    for m in range(6):
        for c in range(COMPS):
            rhs[c, m] = pooled[c * 6 + m]
            mid[c, m] = wm[m + 1] * rhs[c, m]
            e_mid[c, m] = em[0, m + 2] * mid[c, m]
    kept = {}
    for m in range(1, 5):
        for c in range(COMPS):
            v = tri_y(tri_x(mid[c, m - 1], mid[c, m], mid[c, m + 1]))
            ev = tri_y(tri_x(e_mid[c, m - 1], e_mid[c, m], e_mid[c, m + 1]))
            mixed = mixed_z(em[0, m + 2], em[1, m + 2], em[2, m + 2], v, ev)
            left_over = rhs[c, m] - COUPLING[c] * (c1m[m + 1] * mid[c, m] - mixed)
            kept[c, m - 1] = left_over
            value = mid[c, m] + wm[m + 1] * left_over
            tile = c * 4 + m - 1
            pack[8 * tile : 8 * tile + 8] = value[:, :128]
    rows = {}
    for b in range(2):
        found = from_modes(*[kept[c, 2 * b] + kept[c, 2 * b + 1] for c in range(COMPS)])
        for c in range(COMPS):
            rows[c, b] = found[c]
    stacked = jnp.concatenate([rows[c, b] for c in range(COMPS) for b in range(2)], axis=0)
    lane_box = row_of((MID_LANES, 128))
    column = lane_of((MID_LANES, 128))
    boxes = jnp.where(
        jnp.logical_and(lane_box < Z // 2, lane_box // 64 == column % 2), 1.0, 0.0
    ).astype(F32)
    sums = dot_exact_weights(stacked, boxes)
    line = row_of((48, 128))
    entry = lane_of((48, 128))
    inside = line % 8
    match = jnp.logical_and((line // 8) * 2 + inside // 2 == entry // 2, inside < 4)
    scale = 1.0 / math.sqrt((X // 4) * (Y // 4) * (Z // 4))
    low = jnp.sum(jnp.where(match, sums, 0.0), axis=0, keepdims=True) * scale
    pack[8 * LOW_TILE :] = jnp.broadcast_to(low, (8, 128))


def pack_mid(pack, tiles):
    lane = lane_of((8, 128))
    rims = None
    for n, tile in enumerate(tiles):
        pack[8 * n : 8 * n + 8] = tile[:, :128]
        moved = pltpu.roll(tile[:, 128:], 4 + 8 * n, 1)
        rims = moved if n == 0 else jnp.where(lane < 8 * n, rims, moved)
    pack[8 * len(tiles) :] = rims


def unpack_mid(side, count):
    lane = lane_of((8, 128))
    near = jnp.logical_or(lane < 4, lane >= 124)
    rims = side((slice(8 * count, 8 * count + 8), slice(None)))
    tiles = []
    for n in range(count):
        main = side((slice(8 * n, 8 * n + 8), slice(None)))
        rim = jnp.where(near, pltpu.roll(rims, 124 - 8 * n, 1), 0.0)
        tiles.append(jnp.concatenate([main, rim], axis=1))
    return tiles


def coarse_body(n_z, *refs):
    pack = refs[0]
    got_z = refs[1 : 1 + n_z]
    matrix = refs[1 + n_z]
    gathered = refs[2 + n_z : -5]
    planes, column, pack_even, pack_odd, scratch = refs[-5:]
    place = lax.axis_index("gz")
    left, right = from_sides(got_z, "gz")
    lane = lane_of((8, 128))
    for t in range(LOW_TILE):
        key = (slice(8 * t, 8 * t + 8), slice(None))
        planes[t, :, :128] = pack[key]
        planes[t, :, 128:] = jnp.where(lane < 64, right(key), left(key))

    size = 24
    if gathered:
        rhs = gathered[0][...]
    else:
        mine = pack[8 * LOW_TILE : 8 * LOW_TILE + 8]
        other = got_z[0][8 * LOW_TILE : 8 * LOW_TILE + 8]
        first = jnp.where(place == 0, mine, other)
        second = jnp.where(place == 0, other, mine)
        rhs = jnp.where(lane < size, first, pltpu.roll(second, size, 1))[:1, : 2 * size]
    solved = jnp.sum(matrix[0, 0] * rhs, axis=1, keepdims=True)
    scratch[...] = jnp.zeros(scratch.shape, F32)
    scratch[size : size + solved.shape[0]] = jnp.broadcast_to(solved, (solved.shape[0], 128))
    base = pl.multiple_of(place * size, 8)
    wide = lane_of((16, MID_LANES))
    before, own_a, own_b, after = [
        jnp.concatenate([scratch[pl.ds(base + at, 16, stride=2)]] * 2, axis=1)
        for at in (1, size, size + 1, 2 * size)
    ]
    value = jnp.where(wide < 64, own_a, own_b)
    value = jnp.where(wide < 128, value, jnp.where(wide < 192, after, before))
    row = row_of((8, MID_LANES))
    first, second, third = value[:8], up(value[:8], 4), value[8:]
    total, a, b = to_modes(first, second, third)
    rest = [jnp.where(row < 4, total, up(a, 4)), jnp.where(row < 4, b, 0.0)]
    column[:8] = rest[0]
    column[8:] = rest[1]

    even = is_even("gx")
    low, high = [
        [jnp.where(row < 4, planes[c * 4 + p], up(planes[c * 4 + p + 1], 4)) for c in range(COMPS)]
        for p in (0, 2)
    ]
    pack_mid(pack_even, [jnp.where(even, b, a) for a, b in zip(low, high)] + rest)
    pack_mid(pack_odd, [jnp.where(even, a, b) for a, b in zip(low, high)] + rest)


MX_TILES = COMPS + 2
MY_TILES = 2 * COMPS + 5
MX_PACK = (MX_TILES + 1) * 8
MY_PACK = (MY_TILES + 1) * 8


def mid_y_body(planes, column, got_a, got_b, wide_planes, columns, pack_even, pack_odd):
    lower, upper = from_sides((got_a, got_b), "gx")
    low_tiles, high_tiles = unpack_mid(lower, MX_TILES), unpack_mid(upper, MX_TILES)
    row = row_of((8, MID_LANES))
    even = is_even("gy")
    below_packs, above_packs = [], []
    for c in range(COMPS):
        tiles = [low_tiles[c], up(low_tiles[c], 4)]
        tiles += [planes[c * 4 + p] for p in range(4)]
        tiles += [high_tiles[c], up(high_tiles[c], 4)]
        for t in range(8):
            wide_planes[c * 8 + t] = tiles[t]
        for h in range(2):
            below = above = None
            for k in range(4):
                tile = tiles[4 * h + k]
                a, b = up(tile, 2 * k), up(tile, 2 * k - 2)
                below = a if k == 0 else jnp.where(row < 2 * k, below, a)
                above = b if k == 0 else jnp.where(row < 2 * k, above, b)
            below_packs.append(below)
            above_packs.append(above)
    columns[:8] = low_tiles[COMPS]
    columns[8:12] = low_tiles[COMPS + 1][:4]
    columns[12:24] = column[:12]
    columns[24:32] = high_tiles[COMPS]
    columns[32:36] = high_tiles[COMPS + 1][:4]
    columns[36:] = jnp.zeros((4, MID_LANES), F32)
    rest = [columns[8 * t : 8 * t + 8] for t in range(5)]
    pairs_of = list(zip(below_packs, above_packs))
    pack_mid(pack_even, [jnp.where(even, a, b) for b, a in pairs_of] + rest)
    pack_mid(pack_odd, [jnp.where(even, b, a) for b, a in pairs_of] + rest)


def finish_body(
    wide_planes, columns, got_a, got_b, s0, s1, e_all, c1, w, em, em_side, c1m, wm, prev_d, prev_i,
    res, precond, operated, sums, cor, cor_side, mid, fine, s2, es2, s3, es3, p, ep,
):
    e = e_all.at[:, 2 : 2 + PLANES]
    lower, upper = from_sides((got_a, got_b), "gy")
    row = row_of((8, MID_LANES))

    low_tiles, high_tiles = unpack_mid(lower, MY_TILES), unpack_mid(upper, MY_TILES)
    below = jnp.concatenate(low_tiles[2 * COMPS :], axis=0)
    above = jnp.concatenate(high_tiles[2 * COMPS :], axis=0)
    middle = columns[...]
    for c in range(COMPS):
        for b in range(6):
            at = (b // 2) * 12 + c * 4 + (b % 2) * 2

            def band(source, by):
                return jnp.broadcast_to(source[at + by : at + by + 1], (8, MID_LANES))

            field = jnp.where(row < 6, band(above, 0), band(below, 1))
            field = jnp.where(row < 4, band(middle, 1), field)
            cor[c, b] = jnp.where(row < 2, band(middle, 0), field)
            cor_side[c, b] = jnp.where(row == 0, band(below, 0), band(above, 1))

    def box(m):
        return (m + 1) // 2

    for m in range(M_PLANES):
        for c in range(COMPS):
            near = [cor[c, box(m + k)] for k in range(3)]
            near_side = [cor_side[c, box(m + k)] for k in range(3)]
            e_near = [em[0, m + k] * near[k] for k in range(3)]
            e_side = [em_side[m + k] * near_side[k] for k in range(3)]
            side = tri_x(*near_side)
            v = tri_y_with(tri_x(*near), up(side, 6), up(side, 4), 5)
            side = tri_x(*e_side)
            ev = tri_y_with(tri_x(*e_near), up(side, 6), up(side, 4), 5)
            mixed = mixed_z(em[0, m + 1], em[1, m + 1], em[2, m + 1], v, ev)
            applied = COUPLING[c] * (c1m[m] * near[1] - mixed)
            tile = wide_planes[c * 8 + m]
            n, k = c * 2 + m // 4, m % 4
            outer = jnp.where(row < 6, up(high_tiles[n], 4 - 2 * k), up(low_tiles[n], 6 - 2 * k))
            tile = jnp.where(row < 4, tile, outer)
            at = (c * 8 + m) * 8
            mid[at : at + 8] = tile + cor[c, box(m + 1)] - wm[m] * applied
    fine[...] = dot_exact_weights(mid[...], spread_matrix())

    def add_up(i, carry):
        for c in range(COMPS):
            at = pl.multiple_of((c * 8 + i // 2) * 8, 8)
            more = fine[pl.ds(at, 8)]
            value = s1[c, i] + jnp.concatenate([more, more], axis=0)
            s2[c, i] = value
            es2[c, i] = e[0, i] * value
        return carry

    lax.fori_loop(1, PLANES - 1, add_up, 0, unroll=True)
    sweep(s2, es2, s3, es3, s0, c1, e, w, 2, PLANES - 2)
    sweep(s3, es3, p, ep, s0, c1, e, w, 3, PLANES - 3)

    def put_rows(target, x, modes):
        for half in range(2):
            for c, value in enumerate(from_modes(*[m[8 * half : 8 * half + 8, :Z] for m in modes])):
                for k in range(Z // 128):
                    part = value[:4, 128 * k : 128 * k + 128]
                    target[x, c, k, pl.ds(half, 4, stride=2), :] = part

    def image(n, carry):
        i = 2 * n + RIM
        parts = fine_parts(p, ep, c1, e, i)
        for k in range(2):
            put_rows(precond, 2 * n + k, [p[c, i + k] for c in range(COMPS)])
            put_rows(operated, 2 * n + k, [COUPLING[c] * parts[c][k] for c in range(COMPS)])
        return carry

    lax.fori_loop(0, X // 2, image, 0, unroll=True)
    found = [[], [], [], []]
    for x in range(X):
        for c in range(COMPS):
            for k in range(Z // 128):
                lanes = slice(128 * k, 128 * k + 128)
                own_p, own_a = precond[x, c, k], operated[x, c, k]
                d, q = prev_d[c, x, :, lanes], prev_i[c, x, :, lanes]
                own_r = res[c, x, :, lanes]
                terms = (own_r * own_p, own_p * own_a, own_p * q + d * own_a, d * q)
                for kept, term in zip(found, terms):
                    kept.append(term)
    found = [tree_sum(kept) for kept in found]
    row = row_of((8, 128))
    total = jnp.zeros((8, 128), F32)
    for k, value in enumerate(found):
        line = jnp.sum(value, axis=0, keepdims=True)
        total = jnp.where(row == k, jnp.broadcast_to(line, (8, 128)), total)
    total = total + pltpu.roll(total, 64, 1)
    total = total + pltpu.roll(total, 32, 1)
    total = jnp.where(row == lane_of((8, 128)) // 32, total, 0.0)
    sums[...] = jnp.broadcast_to(jnp.sum(total, axis=0, keepdims=True), sums.shape)


STEP = 4


def last_body(
    prev_rz, sums, precond, operated, prev_d, prev_i, sol, res,
    new_s_out, new_r_out, new_d_out, new_i_out, news, out_sems,
):
    total = jnp.sum(sums[...], axis=0, keepdims=True)
    lane = lane_of((1, 128))

    def entry(k):
        return jnp.sum(jnp.where(lane // 32 == k, total, 0.0), axis=1, keepdims=True)

    rz = entry(0)
    beta = rz / prev_rz[0]
    alpha = rz / (entry(1) + beta * (entry(2) + beta * entry(3)))
    beta = jnp.broadcast_to(beta, (Y, 128))
    alpha = jnp.broadcast_to(alpha, (Y, 128))
    leaving = []
    for step in range(X // STEP):
        for x in range(step * STEP, step * STEP + STEP):
            for c in range(COMPS):
                for k in range(Z // 128):
                    at = (c, x, slice(None), slice(128 * k, 128 * k + 128))
                    d = precond[x, c, k] + beta * prev_d[at]
                    q = operated[x, c, k] + beta * prev_i[at]
                    news[(2, *at)] = d
                    news[(3, *at)] = q
                    news[(0, *at)] = sol[at] + alpha * d
                    news[(1, *at)] = res[at] - alpha * q
        part = pl.ds(step * STEP, STEP)
        for k, target in enumerate((new_s_out, new_r_out, new_d_out, new_i_out)):
            copy = pltpu.make_async_copy(
                news.at[k, :, part], target.at[:, part], out_sems.at[k, step]
            )
            copy.start()
            leaving.append(copy)
    for copy in leaving:
        copy.wait()


PLANES = X + 2 * RIM
FIELD = (COMPS, PLANES, ROWS, LANES)
COLS_SHAPE = (40, MID_LANES)


def smooth_outs():
    return [
        shape(*FIELD),
        shape(*FIELD),
        shape(3, E_PLANES, ROWS, LANES),
        shape(PLANES, ROWS, LANES),
        shape(2, PLANES, ROWS, LANES),
        shape(3, EM_PLANES, 8, MID_LANES),
        shape(EM_PLANES, 8, MID_LANES),
        shape(M_PLANES, 8, MID_LANES),
        shape(M_PLANES, 8, MID_LANES),
        shape(MZ_PACK, 128),
    ]


def smooth_call(n_z):
    return call(
        functools.partial(smooth_body, n_z),
        smooth_outs(),
        scratch=[
            pltpu.VMEM((E_PLANES, 24, LANES), F32),
            pltpu.VMEM((E_PLANES, 24, LANES), F32),
            pltpu.VMEM(FIELD, F32),
            pltpu.VMEM(FIELD, F32),
            pltpu.VMEM(FIELD, F32),
            pltpu.VMEM((COMPS * 6 * 8 + 16 * EM_PLANES, LANES), F32),
        ],
        n_in=6 + 3 * n_z,
        vmem=30 << 20,
    )


def finish_call(n_all):
    return call(
        finish_body,
        [pltpu.VMEM((X, COMPS, Z // 128, Y, 128), F32)] * 2 + [shape(n_all, 128)],
        scratch=[
            pltpu.VMEM((COMPS, 6, 8, MID_LANES), F32),
            pltpu.VMEM((COMPS, 6, 8, MID_LANES), F32),
            pltpu.VMEM((COMPS * 64, MID_LANES), F32),
            pltpu.VMEM((COMPS * 64, LANES), F32),
        ]
        + [pltpu.VMEM(FIELD, F32)] * 6,
        n_in=16,
        vmem=30 << 20,
    )


def on_device(
    solution,
    residual,
    prev_direction,
    prev_image,
    prev_rz,
    density_index,
    stiffness_table,
    coarse_inverse,
):
    if residual.shape != (COMPS, X, Y, Z):
        raise ValueError(residual.shape)
    block = shape(COMPS, X, Y, Z)
    n_z = 1 if lax.axis_size("gz") == 2 else 2
    n_all = lax.axis_size(ALL)

    res, young, px, qx = call(
        pack_x_body,
        [block, shape(X, Y, Z), shape(X_PACK, Y, Z), shape(X_PACK, Y, Z)],
        scratch=[
            pltpu.SMEM(stiffness_table.shape, F32),
            pltpu.VMEM((X, Y, Z), jnp.int32),
            pltpu.VMEM((2, COMPS, X, Y, 128), F32),
            pltpu.VMEM((2, X, Y, 128), F32),
            pltpu.SemaphoreType.DMA((4,)),
        ],
        n_in=3,
        hbm=(0, 1, 2),
    )(*[in_hbm(a) for a in (stiffness_table, density_index, residual)])
    got_x = swap("gx", px, qx)
    py, qy = call(pack_y_body, [shape(Y_PACK, Y, Z)] * 2, n_in=4)(res, young, *got_x)
    packs = call(
        functools.partial(pack_z_body, n_z),
        [shape(Z_PACK, 128)] * n_z + [shape(YZ_PACK, 128)] * (2 * n_z),
        n_in=6,
    )(res, young, *got_x, py, qy)
    got_y = swap("gy", py, qy, closed=False)
    got_z = swap("gz", packs[0], packs[n_z - 1])
    got_yz = swap_yz(packs[n_z : 2 * n_z], packs[2 * n_z :])
    corners = [got for both in got_yz for got in both]

    s0, s1, e, c1, w, em, em_side, c1m, wm, pack = smooth_call(n_z)(
        res, young, *got_x, *got_y, *got_z, *corners
    )

    got_z = swap("gz", pack, pack)
    gathered = []
    if n_z > 1:
        gathered = [lax.all_gather(pack[8 * LOW_TILE, :24], "gz", axis=0, tiled=True)[None]]
    size = coarse_inverse.shape[-1]
    mid_planes, column, px, qx = call(
        functools.partial(coarse_body, n_z),
        [
            shape(LOW_TILE, 8, MID_LANES),
            shape(16, MID_LANES),
            shape(MX_PACK, 128),
            shape(MX_PACK, 128),
        ],
        scratch=[pltpu.VMEM((size + 64, 128), F32)],
        n_in=2 + n_z + len(gathered),
    )(pack, *got_z, coarse_inverse, *gathered)
    got_x = swap("gx", px, qx)
    mid_planes, columns, py, qy = call(
        mid_y_body,
        [
            shape(COMPS * 8, 8, MID_LANES),
            shape(40, MID_LANES),
            shape(MY_PACK, 128),
            shape(MY_PACK, 128),
        ],
        n_in=4,
    )(mid_planes, column, *got_x)
    got_y = swap("gy", py, qy, closed=False)
    precond, operated, sums = finish_call(n_all)(
        mid_planes, columns, *got_y, s0, s1, e, c1, w, em, em_side, c1m, wm,
        prev_direction, prev_image, residual,
    )
    precond, operated = in_vmem(precond), in_vmem(operated)
    sums = lax.all_to_all(sums, ALL, 0, 0, tiled=True)
    return tuple(
        call(
            last_body,
            [block] * 4,
            scratch=[
                pltpu.VMEM((4, COMPS, X, Y, Z), F32),
                pltpu.SemaphoreType.DMA((4, X // STEP)),
            ],
            n_in=8,
            smem=(0,),
            hbm_out=(0, 1, 2, 3),
        )(
            prev_rz.reshape(1), sums, precond, operated, prev_direction, prev_image, solution, residual
        )
    )


def solution(mesh):
    field = P(None, "gx", "gy", "gz")
    return jax.shard_map(
        on_device,
        mesh=mesh,
        in_specs=(
            field,
            field,
            field,
            field,
            P(),
            P("gx", "gy", "gz"),
            P(),
            P("gx", "gy", None, None),
        ),
        out_specs=(field, field, field, field),
        check_vma=False,
    )
```
